128 devices in a mesh: ty: 16 (over x, y), tx: 8 (over z, core).
Axes of the slice: x: 4, y: 4, z: 4, core: 2. Of those that a mesh axis runs over, the one named last changes fastest.
Arguments:
- raw_bricks: bfloat16 [128, 3, 4, 4096], P(('ty', 'tx')), may hold values from -6 to 6
- stretch_reader: int32 [128], replicated, may hold values from 0 to 127, as said below
- fine_open: bfloat16 [3, 3, 3, 32, 1], replicated, may hold values from -1.75 to 1.75
- fine_second: bfloat16 [3, 3, 3, 32, 32], replicated, may hold values from -0.3125 to 0.3125
- middle_open: bfloat16 [3, 3, 3, 64, 32], replicated, may hold values from -0.3125 to 0.3125
- middle_second: bfloat16 [3, 3, 3, 64, 64], replicated, may hold values from -0.21875 to 0.21875
- coarse_open: bfloat16 [3, 3, 3, 64, 64], replicated, may hold values from -0.21875 to 0.21875
- coarse_second: bfloat16 [3, 3, 3, 64, 64], replicated, may hold values from -0.21875 to 0.21875
- middle_merge: bfloat16 [3, 3, 3, 64, 128], replicated, may hold values from -0.15625 to 0.15625
- middle_final: bfloat16 [3, 3, 3, 64, 64], replicated, may hold values from -0.21875 to 0.21875
- fine_merge: bfloat16 [3, 3, 3, 32, 96], replicated, may hold values from -0.15625 to 0.15625
- fine_final: bfloat16 [3, 3, 3, 32, 32], replicated, may hold values from -0.3125 to 0.3125
- affinity_head: bfloat16 [3, 32], replicated, may hold values from -1 to 1
Outputs:
- affinity_logits: float32 [3, 32, 256, 256], P(None, None, 'ty', 'tx')
The draws below stay inside these ranges and needn't reach their ends.
Inputs may be any that keep to these rules, and one draw needn't show every extreme that they name: `stretch_reader`: stretch cy * 8 + cx is read by a device cy * 8 + j of the same row of tiles. In every row of tiles one or more devices read exactly 3 stretches, and every other device of the row reads one stretch or none.
All inputs are finite; a program needn't handle non-finite values.
Results may differ from the reference program's by a relative error of at most 0.04.
Values may be sent and summed in bfloat16 or wider, within the bound.
A program may use at most 128 MiB of HBM per device.

```python
import jax
import jax.numpy as jnp
from jax import lax

DEPTH = 32
HELD = 3
FINE_CH = 32
COARSE_CH = 64
BRICK_Y = 8
BRICK_X = 16
BRICK_VOX = 4096
NCHUNK = 128
VOL_Y = 256
VOL_X = 256
N_TY = 16
N_TX = 8


def reader_row(row_key, row_number):
    key_order, key_readers, key_groups = jax.random.split(row_key, 3)
    order = jax.random.permutation(key_order, N_TX).astype(jnp.int32)
    readers = jax.random.permutation(key_readers, N_TX).astype(jnp.int32)
    groups = jax.random.randint(key_groups, (), 1, N_TX // 4 + 1)
    position = jnp.arange(N_TX, dtype=jnp.int32)
    single = jnp.clip(groups + position - HELD * groups, 0, N_TX - 1)
    label = jnp.where(position < HELD * groups, readers[position // HELD], readers[single])
    placed = jnp.zeros((N_TX,), jnp.int32).at[order].set(label.astype(jnp.int32))
    return placed + row_number * N_TX


def draw_stretch_reader(key, part):
    key = jax.random.fold_in(key, 11)
    row_keys = jax.random.split(key, N_TY)
    row_numbers = jnp.arange(N_TY, dtype=jnp.int32)
    return jax.vmap(reader_row)(row_keys, row_numbers).reshape(-1).astype(jnp.int32)


def block_scale(stream_key, dims, pieces, least, top_value):
    gain, own = 1.0, jax.random.fold_in(stream_key, 6)
    for dim, blocks in pieces:
        heights = jnp.exp(jax.random.uniform(jax.random.fold_in(own, dim), (blocks,), jnp.float32, least / len(pieces), top_value / len(pieces)))
        gain = gain * jnp.repeat(heights, dims[dim] // blocks).reshape([-1 if axis == dim else 1 for axis in range(len(dims))])
    return gain


def bell_draw(own_key, shape, spread, limit, shards=(), kind=jnp.bfloat16):
    loudness = block_scale(own_key, shape, shards, -0.22, 0.18) if shards else 1.0
    array = jax.random.normal(own_key, shape, jnp.float32) * spread * loudness
    return jnp.minimum(jnp.maximum(array, -limit), limit).astype(kind)


def setup_inputs(seed: int = 0) -> dict:
    streams_of = jax.random.split(jax.random.key(seed), 14)
    return {
        "raw_bricks": bell_draw(streams_of[0], (NCHUNK, HELD, 4, BRICK_VOX), 1.0, 6.0, ((0, 128),)),
        "stretch_reader": draw_stretch_reader(jax.random.fold_in(streams_of[13], 71), 0),
        "fine_open": bell_draw(streams_of[2], (3, 3, 3, FINE_CH, 1), (27 // 2) ** -0.5, 1.75),
        "fine_second": bell_draw(streams_of[3], (3, 3, 3, FINE_CH, FINE_CH), (27 * FINE_CH // 2) ** -0.5, 0.3125),
        "middle_open": bell_draw(streams_of[4], (3, 3, 3, COARSE_CH, FINE_CH), (27 * FINE_CH // 2) ** -0.5, 0.3125),
        "middle_second": bell_draw(streams_of[5], (3, 3, 3, COARSE_CH, COARSE_CH), (27 * COARSE_CH // 2) ** -0.5, 0.21875),
        "coarse_open": bell_draw(streams_of[6], (3, 3, 3, COARSE_CH, COARSE_CH), (27 * COARSE_CH // 2) ** -0.5, 0.21875),
        "coarse_second": bell_draw(streams_of[7], (3, 3, 3, COARSE_CH, COARSE_CH), (27 * COARSE_CH // 2) ** -0.5, 0.21875),
        "middle_merge": bell_draw(streams_of[8], (3, 3, 3, COARSE_CH, 2 * COARSE_CH), (27 * COARSE_CH) ** -0.5, 0.15625),
        "middle_final": bell_draw(streams_of[9], (3, 3, 3, COARSE_CH, COARSE_CH), (27 * COARSE_CH // 2) ** -0.5, 0.21875),
        "fine_merge": bell_draw(streams_of[10], (3, 3, 3, FINE_CH, COARSE_CH + FINE_CH), (27 * (COARSE_CH + FINE_CH) // 2) ** -0.5, 0.15625),
        "fine_final": bell_draw(streams_of[11], (3, 3, 3, FINE_CH, FINE_CH), (27 * FINE_CH // 2) ** -0.5, 0.3125),
        "affinity_head": bell_draw(streams_of[12], (3, FINE_CH), FINE_CH ** -0.5, 1.0),
    }


def conv_layer(source, weight):
    kernel = weight.astype(jnp.float32).transpose(3, 4, 0, 1, 2)
    summed = lax.conv_general_dilated(source.astype(jnp.float32)[None], kernel, (1, 1, 1), "SAME", dimension_numbers=("NCDHW", "OIDHW", "NCDHW"), precision=lax.Precision.HIGHEST)[0]
    return jnp.maximum(summed, 0.0).astype(jnp.bfloat16)


def pooled(source):
    extent = source.shape
    return source.reshape(extent[0], extent[1] // 2, 2, extent[2] // 2, 2, extent[3] // 2, 2).max(axis=(2, 4, 6))


def doubled(source):
    return jnp.repeat(jnp.repeat(jnp.repeat(source, 2, axis=1), 2, axis=2), 2, axis=3)


def reference(raw_bricks, stretch_reader, fine_open, fine_second, middle_open, middle_second, coarse_open, coarse_second, middle_merge, middle_final, fine_merge, fine_final, affinity_head):
    numbers = jnp.arange(NCHUNK, dtype=jnp.int32)
    same_reader = stretch_reader[:, None] == stretch_reader[None, :]
    earlier = numbers[None, :] < numbers[:, None]
    stretch_rank = jnp.sum(same_reader & earlier, axis=1).astype(jnp.int32)
    bricks = raw_bricks[stretch_reader, stretch_rank]
    volume = bricks.reshape(N_TY, N_TX, 2, 2, DEPTH, BRICK_Y, BRICK_X).transpose(4, 0, 2, 5, 1, 3, 6).reshape(DEPTH, VOL_Y, VOL_X)
    volume = jnp.roll(volume, (BRICK_Y, BRICK_X), axis=(1, 2))
    fine_skip = conv_layer(conv_layer(volume[None], fine_open), fine_second)
    middle_skip = conv_layer(conv_layer(pooled(fine_skip), middle_open), middle_second)
    bottom = conv_layer(conv_layer(pooled(middle_skip), coarse_open), coarse_second)
    joined_middle = jnp.concatenate([doubled(bottom), middle_skip], axis=0)
    middle_out = conv_layer(conv_layer(joined_middle, middle_merge), middle_final)
    joined_fine = jnp.concatenate([doubled(middle_out), fine_skip], axis=0)
    fine_out = conv_layer(conv_layer(joined_fine, fine_merge), fine_final)
    return jnp.einsum("oc,czyx->ozyx", affinity_head.astype(jnp.float32), fine_out.astype(jnp.float32), precision=lax.Precision.HIGHEST)
```

```python
import functools

import jax
import jax.numpy as jnp
from jax import lax
from jax.experimental import pallas as pl
from jax.experimental.pallas import tpu as pltpu
from jax.sharding import PartitionSpec as P

TILE_Y = 16
TILE_X = 32
DEPTH = 32
BF16 = jnp.bfloat16
F32 = jnp.float32
MIB = 1 << 20


def iota(shape, dim):
    return lax.broadcasted_iota(jnp.int32, shape, dim)


def lane_block(shape, width):
    return iota(shape, len(shape) - 1) // width


def spread_blocks(w_ref, out_chans):
    rep = 128 // out_chans
    eye = (iota((out_chans, 128), 0) == iota((out_chans, 128), 1) % out_chans).astype(BF16)
    return [
        lax.dot_general(w_ref[t], eye, (((0,), (0,)), ((), ())), preferred_element_type=F32)
        for t in range(27)
    ]


def tap(a, b, e):
    if 0 <= a <= 2 and 0 <= b <= 2 and 0 <= e <= 2:
        return 9 * a + 3 * b + e
    return None


def masked_sum(blocks, taps, width):
    shape = blocks[0].shape
    lanes = lane_block(shape, width)
    tile = jnp.zeros(shape, F32)
    for place, index in enumerate(taps):
        if index is not None:
            tile = jnp.where(lanes == place, blocks[index], tile)
    return tile


def build_fine(blocks, out_ref):
    for y in range(4):
        for j in range(2):
            for half in range(2):
                for px_in in range(2):
                    for slot in range(2):
                        z = (1 + slot) if half == 0 else (3, 0)[slot]
                        row = (y * 2 + j) * 256 + half * 128 + px_in * 64 + slot * 32
                        for py in range(2):
                            taps = [
                                tap(z - pz, y - py, 2 * j + px_in - px)
                                for px in range(2)
                                for pz in range(2)
                            ]
                            out_ref[row : row + 32, py * 128 : (py + 1) * 128] = masked_sum(
                                blocks, taps, 32
                            ).astype(BF16)


def build_middle(blocks, out_ref):
    for y in range(4):
        for j in range(2):
            for slot, dz in enumerate((1, 0, 2)):
                for px_in in range(2):
                    row = (y * 2 + j) * 384 + slot * 128 + px_in * 64
                    for py in range(2):
                        taps = [tap(dz, y - py, 2 * j + px_in - px) for px in range(2)]
                        out_ref[row : row + 64, py * 128 : (py + 1) * 128] = masked_sum(
                            blocks, taps, 64
                        ).astype(BF16)


def build_middle_open(blocks, out_ref):
    for y in range(4):
        for j in range(2):
            for px_in in range(2):
                for slot, dz in enumerate((1, 0, 2, 9)):
                    row = (y * 2 + j) * 256 + px_in * 128 + slot * 32
                    for py in range(2):
                        taps = [tap(dz, y - py, 2 * j + px_in - px) for px in range(2)]
                        out_ref[row : row + 32, py * 128 : (py + 1) * 128] = masked_sum(
                            blocks, taps, 64
                        ).astype(BF16)


def build_up(zcombined, out_ref, row0):
    shape = (64, 128)
    odd = lane_block(shape, 64) == 1
    for slot in range(4):
        for xc in range(2):
            rows = None
            if slot < 3:
                rows = []
                for dy in range(3):
                    t = zcombined[slot][dy]
                    if xc == 0:
                        rows.append(jnp.where(odd, t[0], t[0] + t[1]))
                    else:
                        rows.append(jnp.where(odd, t[1] + t[2], t[2]))
            for yc in range(2):
                row = row0 + (yc * 2 + xc) * 256 + slot * 64
                for py in range(2):
                    if rows is None:
                        tile = jnp.zeros(shape, F32)
                    elif (py, yc) == (0, 0):
                        tile = rows[0] + rows[1]
                    elif (py, yc) == (0, 1):
                        tile = rows[2]
                    elif (py, yc) == (1, 0):
                        tile = rows[0]
                    else:
                        tile = rows[1] + rows[2]
                    out_ref[row : row + 64, py * 128 : (py + 1) * 128] = tile.astype(BF16)


def build_open(w4_ref, out_ref):
    shape = (32, 128)
    z_row = iota(shape, 0)
    lane = iota(shape, 1)
    px = lane // 64
    part = (lane // 32) % 2
    for dy in range(3):
        for x in range(4):
            vectors = []
            for dz in range(3):
                vec = jnp.zeros((1, 128), F32)
                for p in range(2):
                    index = tap(dz, dy, x - p)
                    if index is not None:
                        vec = jnp.where(px[:1] == p, w4_ref[index : index + 1, :], vec)
                vectors.append(vec)
            row = (dy * 4 + x) * 32
            for half in range(2):
                offset = part if half == 0 else jnp.where(part == 0, 2, -1)

                def step(k, _, half=half, offset=offset, vectors=vectors, row=row):
                    z_out = 2 * k + offset
                    d = z_row - z_out + 1
                    tile = jnp.where(d == 0, vectors[0], 0.0)
                    tile = jnp.where(d == 1, vectors[1], tile)
                    tile = jnp.where(d == 2, vectors[2], tile)
                    inside = (z_out >= 0) & (z_out < DEPTH)
                    tile = jnp.where(inside, tile, 0.0)
                    out_ref[k, row : row + 32, half * 128 : (half + 1) * 128] = tile.astype(BF16)
                    return 0

                lax.fori_loop(0, 16, step, 0)


def prep_kernel(
    fo, fs, mo, ms, co, cs, mm, mf, fm, ff, o_fo, o_fs, o_mo, o_ms, o_co, o_cs, o_mm, o_mf, o_fm, o_ff
):
    build_open(fo, o_fo)
    build_fine(spread_blocks(fs, 32), o_fs)
    build_middle_open(spread_blocks(mo, 64), o_mo)
    build_middle(spread_blocks(ms, 64), o_ms)
    build_middle(spread_blocks(co, 64), o_co)
    build_middle(spread_blocks(cs, 64), o_cs)
    build_middle(spread_blocks(mf, 64), o_mf)
    build_fine(spread_blocks(ff, 32), o_ff)
    both = spread_blocks(mm, 64)
    build_middle([block[64:128] for block in both], o_mm)
    up = [block[:64] for block in both]
    grid = [[[up[9 * dz + 3 * dy + dx] for dx in range(3)] for dy in range(3)] for dz in (1, 0, 2)]
    build_up(grid, o_mm, 3072)
    both = spread_blocks(fm, 32)
    build_fine([block[64:96] for block in both], o_fm)
    up = [block[:64] for block in both]
    odd_z = lane_block((64, 128), 32) % 2 == 1

    def zmix(slot, dy, dx):
        w0, w1, w2 = (up[9 * a + 3 * dy + dx] for a in range(3))
        if slot == 0:
            return jnp.where(odd_z, w0 + w1, w1 + w2)
        if slot == 1:
            return jnp.where(odd_z, 0.0, w0)
        return jnp.where(odd_z, w2, 0.0)

    grid = [[[zmix(slot, dy, dx) for dx in range(3)] for dy in range(3)] for slot in range(3)]
    build_up(grid, o_fm, 2048)


def prep(fo, fs, mo, ms, co, cs, mm, mf, fm, ff):
    def flat(w):
        return w.reshape(27, w.shape[3], w.shape[4])

    w4 = jnp.tile(fo.reshape(27, 32), (1, 4)).astype(F32)
    sizes = [2048, 2048, 3072, 3072, 3072, 4096, 3072, 3072, 2048]
    shapes = [jax.ShapeDtypeStruct((16, 384, 256), BF16)]
    shapes += [jax.ShapeDtypeStruct((size, 256), BF16) for size in sizes]
    vmem = pl.BlockSpec(memory_space=pltpu.VMEM)
    return pl.pallas_call(
        prep_kernel,
        out_shape=shapes,
        in_specs=[vmem] * 10,
        out_specs=[vmem] * 10,
        name="prep_weights",
        compiler_params=pltpu.CompilerParams(vmem_limit_bytes=40 * MIB),
        cost_estimate=pl.CostEstimate(flops=10**8, bytes_accessed=20 * MIB, transcendentals=0),
    )(w4, flat(fs), flat(mo), flat(ms), flat(co), flat(cs), flat(mm), flat(mf), flat(fm), flat(ff))


def from_below(x):
    return jnp.where(iota(x.shape, 0) % 16 == 0, 0.0, pltpu.roll(x, 1, 0))


def from_above(x):
    return jnp.where(iota(x.shape, 0) % 16 == 15, 0.0, pltpu.roll(x, x.shape[0] - 1, 0))


def as_rows(x):
    return x.reshape(x.shape[0] * 16, x.shape[2])


def as_blocks(x):
    return x.reshape(x.shape[0] // 16, 16, x.shape[1])


def conv(src, w_ref, yg, groups, extra=()):
    pieces = [as_rows(src[2 * yg + y, j : j + groups]) for y in range(4) for j in range(2)]
    pieces += extra
    return jnp.dot(jnp.concatenate(pieces, axis=1), w_ref[...], preferred_element_type=F32)


def up_pieces(src, yg, shift, groups):
    return [
        as_rows(src[yg + shift + yc, shift + xc : shift + xc + groups])
        for yc in range(2)
        for xc in range(2)
    ]


def column_mask(rows, start, width, tiles):
    shape = (rows, 128)
    column = start + 2 * (iota(shape, 0) // 16) + iota(shape, 1) // 64
    return (column >= 0) & (column < width * tiles)


def row_inside(row, limit):
    return (row >= 0) & (row < limit)


def kept(value, mask, inside):
    return jnp.where(mask & inside, jnp.maximum(value, 0.0), 0.0)


def ends_of(tile):
    odd = lane_block(tile.shape, 32) % 2 == 1
    return jnp.where(odd, from_below(tile), from_above(tile))


def store_fine(ref, y, tile):
    ref[y, :, :, 0:128] = as_blocks(tile.astype(BF16))
    ref[y, :, :, 128:256] = as_blocks(ends_of(tile).astype(BF16))


def store_middle(ref, y, tile):
    ref[y, :, :, 0:128] = as_blocks(tile.astype(BF16))
    ref[y, :, :, 128:256] = as_blocks(from_below(tile).astype(BF16))
    ref[y, :, :, 256:384] = as_blocks(from_above(tile).astype(BF16))


def store_single(ref, y, tile):
    below, above = from_below(tile), from_above(tile)
    low = lane_block(tile.shape, 64) == 0
    near = [
        jnp.where(low, tile, pltpu.roll(below, 64, 1)),
        jnp.where(low, pltpu.roll(tile, 64, 1), below),
    ]
    far = [above, pltpu.roll(above, 64, 1)]
    for px in range(2):
        a, b = as_blocks(near[px].astype(BF16)), as_blocks(far[px].astype(BF16))
        for xg in range(tile.shape[0] // 16):
            ref[y, 2 * xg + px, :, 0:128] = a[xg]
            ref[y, 2 * xg + px, :, 128:256] = b[xg]


def loop(count, body):
    def step(i, carry):
        body(i)
        return carry

    lax.fori_loop(0, count, step, 0)


def fine_kernel(bricks, w_open, w_second, skip, quads, t_ref, low_ref, high_ref, a_ref):
    ty, tx = lax.axis_index("ty"), lax.axis_index("tx")
    for br in range(4):
        for bc in range(4):
            brick = bricks[br, bc].astype(F32)
            ok = True
            if br == 0:
                ok = ty > 0
            if br == 3:
                ok = ty < 15
            if bc == 0:
                ok = (tx > 0) & ok
            if bc == 3:
                ok = (tx < 7) & ok
            if ok is not True:
                brick = jnp.where(ok, brick, 0.0)
            turned = jnp.concatenate([brick] * 4, axis=0).T
            t_ref[8 * br : 8 * br + 8, 16 * bc : 16 * bc + 16, :] = turned.reshape(8, 16, 128)
    lanes = lane_block((24, 128), 32)
    mixed = []
    for y in range(20):
        rows = [t_ref[6 + y, pl.ds(14 + x, 24, stride=2), :] for x in range(4)]
        row = rows[0]
        for x in range(1, 4):
            row = jnp.where(lanes == x, rows[x], row)
        mixed.append(row.astype(BF16))
    lhs = jnp.concatenate(
        [
            jnp.concatenate([mixed[y].astype(F32) for y in range(dy, dy + 18)], axis=0)
            for dy in range(3)
        ],
        axis=1,
    ).astype(BF16)
    shape = (432, 128)
    column = tx * 32 - 1 + 2 * (iota(shape, 0) % 24) + iota(shape, 1) // 64
    line = ty * 16 - 1 + iota(shape, 0) // 24
    mask = (column >= 0) & (column < 256) & (line >= 0) & (line < 256)

    def opened(k):
        out = jnp.dot(lhs, w_open[k], preferred_element_type=F32)
        low_ref[pl.ds(k, 432, stride=16), :] = jnp.where(mask, jnp.maximum(out[:, :128], 0.0), 0.0)
        high_ref[pl.ds(k, 432, stride=16), :] = jnp.where(mask, jnp.maximum(out[:, 128:], 0.0), 0.0)

    loop(16, opened)

    def packed(y):
        start = pl.multiple_of(y * 384, 384)
        a_ref[y, :, :, 0:128] = as_blocks(low_ref[pl.ds(start, 272), :].astype(BF16))
        a_ref[y, :, :, 128:256] = as_blocks(high_ref[pl.ds(start, 272), :].astype(BF16))

    loop(18, packed)
    quad_lane = lane_block((4, 16, 128), 32)

    def second(yg):
        acc = jnp.maximum(conv(a_ref, w_second, yg, 16), 0.0)
        skip[2 * yg] = as_blocks(acc[:, :128].astype(BF16))
        skip[2 * yg + 1] = as_blocks(acc[:, 128:].astype(BF16))
        top = jnp.maximum(acc[:, :128], acc[:, 128:])
        top = jnp.maximum(top, pltpu.roll(top, 64, 1))
        top = jnp.maximum(top, pltpu.roll(top, 32, 1)).reshape(4, 4, 16, 128)
        quad = top[:, 0]
        for q in range(1, 4):
            quad = jnp.where(quad_lane == q, top[:, q], quad)
        quads[yg] = quad.astype(BF16)

    loop(8, second)


def fine_encoder(bricks, w_open, w_second):
    vmem = pl.BlockSpec(memory_space=pltpu.VMEM)
    return pl.pallas_call(
        fine_kernel,
        out_shape=[
            jax.ShapeDtypeStruct((16, 16, 16, 128), BF16),
            jax.ShapeDtypeStruct((8, 4, 16, 128), BF16),
        ],
        in_specs=[vmem] * 3,
        out_specs=[vmem] * 2,
        scratch_shapes=[
            pltpu.VMEM((32, 64, 128), F32),
            pltpu.VMEM((432 * 16, 128), F32),
            pltpu.VMEM((432 * 16, 128), F32),
            pltpu.VMEM((18, 17, 16, 256), BF16),
        ],
        name="fine_encoder",
        compiler_params=pltpu.CompilerParams(vmem_limit_bytes=40 * MIB),
    )(bricks, w_open, w_second)


def middle_kernel(quads, w_open, w_second, skip, pairs, in_ref, b_ref, s_ref):
    ty, tx = lax.axis_index("ty"), lax.axis_index("tx")

    def spread(y):
        c = as_rows(quads[y]).astype(F32)
        below, above = from_below(c), from_above(c)
        lanes = lane_block(c.shape, 32)
        for q in range(4):
            tile = jnp.where(lanes == 0, pltpu.roll(c, (-32 * q) % 128, 1), 0.0)
            tile = jnp.where(lanes == 1, pltpu.roll(below, (32 - 32 * q) % 128, 1), tile)
            tile = jnp.where(lanes == 2, pltpu.roll(above, (64 - 32 * q) % 128, 1), tile)
            blocks = as_blocks(tile.astype(BF16))
            lane = 128 * (q % 2)
            for quad in range(6):
                place = 2 * quad - 1 + q // 2
                if 0 <= place < 10:
                    in_ref[y, place, :, lane : lane + 128] = blocks[quad]

    loop(12, spread)
    mask = column_mask(144, tx * 16 - 1, 16, 8)

    def opened(yg):
        acc = conv(in_ref, w_open, yg, 9)
        for py in range(2):
            inside = row_inside(ty * 8 - 1 + 2 * yg + py, 128)
            store_middle(b_ref, 2 * yg + py, kept(acc[:, 128 * py : 128 * py + 128], mask, inside))

    loop(5, opened)
    low = lane_block((4, 8, 128), 64) == 0

    def second(yg):
        acc = jnp.maximum(conv(b_ref, w_second, yg, 8), 0.0)
        skip[2 * yg] = as_blocks(acc[:, :128].astype(BF16))
        skip[2 * yg + 1] = as_blocks(acc[:, 128:].astype(BF16))
        top = jnp.maximum(acc[:, :128], acc[:, 128:])
        top = jnp.maximum(top, pltpu.roll(top, 64, 1))
        s_ref[...] = jnp.maximum(top, from_above(top))
        some = s_ref[pl.ds(0, 64, stride=2), :].reshape(4, 2, 8, 128)
        pair = jnp.where(low, some[:, 0], some[:, 1])
        pairs[yg] = jnp.concatenate([pair, jnp.zeros_like(pair)], axis=1).astype(BF16)

    loop(4, second)


def middle_encoder(quads, w_open, w_second):
    vmem = pl.BlockSpec(memory_space=pltpu.VMEM)
    return pl.pallas_call(
        middle_kernel,
        out_shape=[
            jax.ShapeDtypeStruct((8, 8, 16, 128), BF16),
            jax.ShapeDtypeStruct((4, 4, 16, 128), BF16),
        ],
        in_specs=[vmem] * 3,
        out_specs=[vmem] * 2,
        scratch_shapes=[
            pltpu.VMEM((12, 10, 16, 256), BF16),
            pltpu.VMEM((10, 9, 16, 384), BF16),
            pltpu.VMEM((128, 128), F32),
        ],
        name="middle_encoder",
        compiler_params=pltpu.CompilerParams(vmem_limit_bytes=40 * MIB),
    )(quads, w_open, w_second)


def decoder_kernel(
    coarse, middle, fine, w_co, w_cs, w_mm, w_mf, w_fm, w_ff, head, out,
    ci_ref, co_ref, s_ref, u1_ref, mi_ref, mm_ref, u2_ref, fi_ref, fm_ref,
):
    ty, tx = lax.axis_index("ty"), lax.axis_index("tx")

    def coarse_in(y):
        store_middle(ci_ref, y, as_rows(coarse[y]).astype(F32))

    loop(12, coarse_in)
    mask = column_mask(112, tx * 8 - 3, 8, 8) & (iota((112, 128), 0) % 16 < 8)

    def coarse_open(yg):
        acc = conv(ci_ref, w_co, yg, 7)
        for py in range(2):
            inside = row_inside(ty * 4 - 3 + 2 * yg + py, 64)
            store_middle(co_ref, 2 * yg + py, kept(acc[:, 128 * py : 128 * py + 128], mask, inside))

    loop(5, coarse_open)
    mask2 = column_mask(96, tx * 8 - 2, 8, 8)

    def coarse_second(yg):
        acc = conv(co_ref, w_cs, yg, 6)
        for py in range(2):
            inside = row_inside(ty * 4 - 2 + 2 * yg + py, 64)
            tile = kept(acc[:, 128 * py : 128 * py + 128], mask2, inside)
            half = tile.reshape(6, 16, 128)[:, :8].reshape(48, 128)
            s_ref[pl.ds(0, 48, stride=2), :] = half
            s_ref[pl.ds(1, 48, stride=2), :] = half
            store_single(u1_ref, 2 * yg + py, s_ref[...])

    loop(4, coarse_second)

    def middle_in(y):
        store_middle(mi_ref, y, as_rows(middle[y]).astype(F32))

    loop(16, middle_in)
    mask3 = column_mask(176, tx * 16 - 3, 16, 8)

    def middle_merge(yg):
        acc = conv(mi_ref, w_mm, yg, 11, up_pieces(u1_ref, yg, 0, 11))
        for py in range(2):
            inside = row_inside(ty * 8 - 3 + 2 * yg + py, 128)
            store_middle(mm_ref, 2 * yg + py, kept(acc[:, 128 * py : 128 * py + 128], mask3, inside))

    loop(7, middle_merge)
    mask4 = column_mask(160, tx * 16 - 2, 16, 8)

    def middle_final(yg):
        acc = conv(mm_ref, w_mf, yg, 10)
        for py in range(2):
            inside = row_inside(ty * 8 - 2 + 2 * yg + py, 128)
            store_single(u2_ref, 2 * yg + py, kept(acc[:, 128 * py : 128 * py + 128], mask4, inside))

    loop(6, middle_final)

    def fine_in(y):
        store_fine(fi_ref, y, as_rows(fine[y]).astype(F32))

    loop(20, fine_in)
    mask5 = column_mask(272, tx * 32 - 1, 32, 8)

    def fine_merge(yg):
        acc = conv(fi_ref, w_fm, yg, 17, up_pieces(u2_ref, yg, 1, 17))
        for py in range(2):
            inside = row_inside(ty * 16 - 1 + 2 * yg + py, 256)
            store_fine(fm_ref, 2 * yg + py, kept(acc[:, 128 * py : 128 * py + 128], mask5, inside))

    loop(9, fine_merge)

    def fine_final(yg):
        acc = jnp.maximum(conv(fm_ref, w_ff, yg, 16), 0.0).astype(BF16)
        out[yg] = lax.dot_general(
            head[...], acc, (((1,), (1,)), ((), ())), preferred_element_type=F32
        )

    loop(8, fine_final)


def decoder(coarse, middle, fine, w_co, w_cs, w_mm, w_mf, w_fm, w_ff, head):
    vmem = pl.BlockSpec(memory_space=pltpu.VMEM)
    return pl.pallas_call(
        decoder_kernel,
        out_shape=jax.ShapeDtypeStruct((8, 32, 256), F32),
        in_specs=[vmem] * 10,
        out_specs=vmem,
        scratch_shapes=[
            pltpu.VMEM((12, 8, 16, 384), BF16),
            pltpu.VMEM((10, 7, 16, 384), BF16),
            pltpu.VMEM((96, 128), F32),
            pltpu.VMEM((8, 12, 16, 256), BF16),
            pltpu.VMEM((16, 12, 16, 384), BF16),
            pltpu.VMEM((14, 11, 16, 384), BF16),
            pltpu.VMEM((12, 20, 16, 256), BF16),
            pltpu.VMEM((20, 18, 16, 256), BF16),
            pltpu.VMEM((18, 17, 16, 256), BF16),
        ],
        name="decoder",
        compiler_params=pltpu.CompilerParams(vmem_limit_bytes=48 * MIB),
    )(coarse, middle, fine, w_co, w_cs, w_mm, w_mf, w_fm, w_ff, head)


def extended(block, sides):
    for axis, dim, width in sides:
        count = lax.axis_size(axis)
        forward = [(i, i + 1) for i in range(count - 1)]
        backward = [(target, source) for source, target in forward]
        low = lax.ppermute(
            lax.slice_in_dim(block, block.shape[dim] - width, None, axis=dim), axis, forward
        )
        high = lax.ppermute(lax.slice_in_dim(block, 0, width, axis=dim), axis, backward)
        block = jnp.concatenate([low, block, high], axis=dim)
    return block


def from_behind(block, axis):
    count = lax.axis_size(axis)
    return lax.ppermute(block, axis, [((i - 1) % count, i) for i in range(count)])


def stretch_order(stretch_reader):
    numbers = jnp.arange(stretch_reader.shape[0], dtype=jnp.int32)
    same_reader = stretch_reader[:, None] == stretch_reader[None, :]
    earlier = numbers[None, :] < numbers[:, None]
    return jnp.sum(same_reader & earlier, axis=1)


def deliver(raw_bricks, stretch_reader):
    tile_row = lax.axis_index("ty")
    tile_col = lax.axis_index("tx")
    rank = lax.dynamic_slice(jnp.minimum(stretch_order(stretch_reader), 2), (tile_row * 8,), (8,))
    reader = lax.dynamic_slice(stretch_reader, (tile_row * 8,), (8,)) % 8
    mine = raw_bricks.reshape(3, 4, 32, 128)
    outgoing = mine[rank]
    arrived = lax.all_to_all(outgoing, "tx", split_axis=0, concat_axis=0, tiled=True)
    stretch = lax.dynamic_index_in_dim(arrived, reader[tile_col], 0, keepdims=False)
    across = jnp.stack([from_behind(stretch, "tx"), stretch])
    held = jnp.stack([from_behind(across, "ty"), across])
    return held.reshape(2, 2, 2, 2, 32, 128).transpose(0, 2, 1, 3, 4, 5).reshape(4, 4, 32, 128)


def head_matrix(affinity_head):
    spots = jnp.eye(8, dtype=BF16)
    full = spots[None, :, :, None] * affinity_head[:, None, None, :]
    return jnp.pad(full.reshape(24, 256), ((0, 8), (0, 0)))


def per_device(
    raw_bricks,
    stretch_reader,
    fine_open,
    fine_second,
    middle_open,
    middle_second,
    coarse_open,
    coarse_second,
    middle_merge,
    middle_final,
    fine_merge,
    fine_final,
    affinity_head,
):
    w_fo, w_fs, w_mo, w_ms, w_co, w_cs, w_mm, w_mf, w_fm, w_ff = prep(
        fine_open, fine_second, middle_open, middle_second, coarse_open, coarse_second,
        middle_merge, middle_final, fine_merge, fine_final,
    )
    bricks = deliver(raw_bricks, stretch_reader)
    skip, quads = fine_encoder(bricks, w_fo, w_fs)
    quads = extended(quads, (("ty", 0, 2), ("tx", 1, 1)))
    skip = extended(skip, (("ty", 0, 2), ("tx", 1, 1)))
    middle, pairs = middle_encoder(quads, w_mo, w_ms)
    middle = extended(middle, (("ty", 0, 4), ("tx", 1, 2)))
    pairs = extended(pairs, (("ty", 0, 4), ("tx", 1, 2)))
    logits = decoder(
        pairs, middle, skip, w_co, w_cs, w_mm, w_mf, w_fm, w_ff, head_matrix(affinity_head)
    )
    logits = logits[:, :24].reshape(8, 3, 2, 2, 2, 16, 16)
    return logits.transpose(1, 6, 4, 0, 2, 5, 3).reshape(3, DEPTH, TILE_Y, TILE_X)


def solution(mesh):
    placed = (P(("ty", "tx"), None, None, None),) + (P(),) * 12
    return jax.shard_map(
        per_device, mesh=mesh, in_specs=placed, out_specs=P(None, None, "ty", "tx"), check_vma=False
    )
```

```python
import jax
import jax.numpy as jnp
from jax import lax
from jax.experimental import pallas as pl
from jax.experimental.pallas import tpu as pltpu
from jax.sharding import PartitionSpec as P

TILE_Y = 16
TILE_X = 32
DEPTH = 32
BF16 = jnp.bfloat16
F32 = jnp.float32
MIB = 1 << 20


def iota(shape, dim):
    return lax.broadcasted_iota(jnp.int32, shape, dim)


def lane_block(shape, width):
    return iota(shape, len(shape) - 1) // width


def spread_blocks(w_ref, out_chans, out_dim=0):
    eye = (iota((out_chans, 128), 0) == iota((out_chans, 128), 1) % out_chans).astype(BF16)
    return [
        lax.dot_general(w_ref[t], eye, (((out_dim,), (0,)), ((), ())), preferred_element_type=F32)
        for t in range(27)
    ]


def tap(a, b, e):
    if 0 <= a <= 2 and 0 <= b <= 2 and 0 <= e <= 2:
        return 9 * a + 3 * b + e
    return None


def masked_sum(blocks, taps, width):
    shape = blocks[0].shape
    lanes = lane_block(shape, width)
    tile = jnp.zeros(shape, F32)
    for place, index in enumerate(taps):
        if index is not None:
            tile = jnp.where(lanes == place, blocks[index], tile)
    return tile


def build_fine(blocks, out_ref):
    for y in range(4):
        for j in range(2):
            for half in range(2):
                for px_in in range(2):
                    for slot in range(2):
                        z = (1 + slot) if half == 0 else (3, 0)[slot]
                        row = (y * 2 + j) * 256 + half * 128 + px_in * 64 + slot * 32
                        for py in range(2):
                            taps = [
                                tap(z - pz, y - py, 2 * j + px_in - px)
                                for px in range(2)
                                for pz in range(2)
                            ]
                            out_ref[row : row + 32, py * 128 : (py + 1) * 128] = masked_sum(
                                blocks, taps, 32
                            ).astype(BF16)


def build_middle(blocks, out_ref):
    for y in range(4):
        for j in range(2):
            for slot, dz in enumerate((1, 0, 2)):
                for px_in in range(2):
                    row = (y * 2 + j) * 384 + slot * 128 + px_in * 64
                    for py in range(2):
                        taps = [tap(dz, y - py, 2 * j + px_in - px) for px in range(2)]
                        out_ref[row : row + 64, py * 128 : (py + 1) * 128] = masked_sum(
                            blocks, taps, 64
                        ).astype(BF16)


def build_middle_open(blocks, out_ref):
    for y in range(4):
        for j in range(2):
            for px_in in range(2):
                for slot, dz in enumerate((1, 0, 2, 9)):
                    row = (y * 2 + j) * 256 + px_in * 128 + slot * 32
                    for py in range(2):
                        taps = [tap(dz, y - py, 2 * j + px_in - px) for px in range(2)]
                        out_ref[row : row + 32, py * 128 : (py + 1) * 128] = masked_sum(
                            blocks, taps, 64
                        ).astype(BF16)


def build_up(zcombined, out_ref, row0):
    shape = (64, 128)
    odd = lane_block(shape, 64) == 1
    for slot in range(4):
        for xc in range(2):
            rows = None
            if slot < 3:
                rows = []
                for dy in range(3):
                    t = zcombined[slot][dy]
                    if xc == 0:
                        rows.append(jnp.where(odd, t[0], t[0] + t[1]))
                    else:
                        rows.append(jnp.where(odd, t[1] + t[2], t[2]))
            for yc in range(2):
                row = row0 + (yc * 2 + xc) * 256 + slot * 64
                for py in range(2):
                    if rows is None:
                        tile = jnp.zeros(shape, F32)
                    elif (py, yc) == (0, 0):
                        tile = rows[0] + rows[1]
                    elif (py, yc) == (0, 1):
                        tile = rows[2]
                    elif (py, yc) == (1, 0):
                        tile = rows[0]
                    else:
                        tile = rows[1] + rows[2]
                    out_ref[row : row + 64, py * 128 : (py + 1) * 128] = tile.astype(BF16)


def build_open(w4_ref, out_ref):
    shape = (32, 128)
    z_row = iota(shape, 0)
    lane = iota(shape, 1)
    px = lane // 64
    part = (lane // 32) % 2
    for dy in range(3):
        for x in range(4):
            vectors = []
            for dz in range(3):
                vec = jnp.zeros((1, 128), F32)
                for p in range(2):
                    index = tap(dz, dy, x - p)
                    if index is not None:
                        vec = jnp.where(px[:1] == p, w4_ref[index : index + 1, :], vec)
                vectors.append(vec)
            row = (dy * 4 + x) * 32
            for half in range(2):
                offset = part if half == 0 else jnp.where(part == 0, 2, -1)

                def step(k, _, half=half, offset=offset, vectors=vectors, row=row):
                    z_out = 2 * k + offset
                    d = z_row - z_out + 1
                    tile = jnp.where(d == 0, vectors[0], 0.0)
                    tile = jnp.where(d == 1, vectors[1], tile)
                    tile = jnp.where(d == 2, vectors[2], tile)
                    inside = (z_out >= 0) & (z_out < DEPTH)
                    tile = jnp.where(inside, tile, 0.0)
                    out_ref[k, row : row + 32, half * 128 : (half + 1) * 128] = tile.astype(BF16)
                    return 0

                lax.fori_loop(0, 16, step, 0)


def build_middle_merge(w_ref, out_ref):
    both = spread_blocks(w_ref, 64)
    build_middle([block[64:128] for block in both], out_ref)
    up = [block[:64] for block in both]
    grid = [[[up[9 * dz + 3 * dy + dx] for dx in range(3)] for dy in range(3)] for dz in (1, 0, 2)]
    build_up(grid, out_ref, 3072)


def build_fine_merge(w_ref, out_ref):
    both = spread_blocks(w_ref, 32)
    build_fine([block[64:96] for block in both], out_ref)
    up = [block[:64] for block in both]
    odd_z = lane_block((64, 128), 32) % 2 == 1

    def zmix(slot, dy, dx):
        w0, w1, w2 = (up[9 * a + 3 * dy + dx] for a in range(3))
        if slot == 0:
            return jnp.where(odd_z, w0 + w1, w1 + w2)
        if slot == 1:
            return jnp.where(odd_z, 0.0, w0)
        return jnp.where(odd_z, w2, 0.0)

    grid = [[[zmix(slot, dy, dx) for dx in range(3)] for dy in range(3)] for slot in range(3)]
    build_up(grid, out_ref, 2048)


def build_head(head_ref, out_ref):
    column = iota((256, 32), 0) % 128 // 32
    picked = jnp.zeros((256, 32), F32)
    for c in range(3):
        picked = jnp.where(column == c, head_ref[c : c + 1, :].astype(F32), picked)
    eye = (iota((256, 32), 0) % 32 == iota((256, 32), 1)).astype(BF16)
    full = lax.dot_general(
        eye, picked.astype(BF16), (((1,), (1,)), ((), ())), preferred_element_type=F32
    )
    row, col = iota((256, 256), 0), iota((256, 256), 1)
    fits = (row // 64 % 2 == col // 128) & (row // 32 % 2 == col // 16 % 2)
    fits = fits & (row // 128 == col % 16) & (col % 128 < 96)
    out_ref[...] = jnp.where(fits, full, 0.0).astype(BF16)


def from_below(x):
    return jnp.where(iota(x.shape, 0) % 16 == 0, 0.0, pltpu.roll(x, 1, 0))


def from_above(x):
    return jnp.where(iota(x.shape, 0) % 16 == 15, 0.0, pltpu.roll(x, x.shape[0] - 1, 0))


def as_rows(x):
    return x.reshape(x.shape[0] * 16, x.shape[2])


def as_blocks(x):
    return x.reshape(x.shape[0] // 16, 16, x.shape[1])


def conv(src, w_ref, yg, groups, extra=()):
    pieces = [as_rows(src[2 * yg + y, j : j + groups]) for y in range(4) for j in range(2)]
    pieces += extra
    return jnp.dot(jnp.concatenate(pieces, axis=1), w_ref[...], preferred_element_type=F32)


def up_pieces(src, yg, shift, groups):
    return [
        as_rows(src[yg + shift + yc, shift + xc : shift + xc + groups])
        for yc in range(2)
        for xc in range(2)
    ]


def column_mask(rows, start, width, tiles):
    shape = (rows, 128)
    column = start + 2 * (iota(shape, 0) // 16) + iota(shape, 1) // 64
    return (column >= 0) & (column < width * tiles)


def row_inside(row, limit):
    return (row >= 0) & (row < limit)


def kept(value, mask, inside):
    return jnp.where(mask & inside, jnp.maximum(value, 0.0), 0.0)


def ends_of(tile):
    odd = lane_block(tile.shape, 32) % 2 == 1
    return jnp.where(odd, from_below(tile), from_above(tile))


def store_fine(ref, y, tile):
    ref[y, :, :, 0:128] = as_blocks(tile.astype(BF16))
    ref[y, :, :, 128:256] = as_blocks(ends_of(tile).astype(BF16))


def store_middle(ref, y, tile):
    ref[y, :, :, 0:128] = as_blocks(tile.astype(BF16))
    ref[y, :, :, 128:256] = as_blocks(from_below(tile).astype(BF16))
    ref[y, :, :, 256:384] = as_blocks(from_above(tile).astype(BF16))


def store_single(ref, y, tile):
    below, above = from_below(tile), from_above(tile)
    low = lane_block(tile.shape, 64) == 0
    near = [
        jnp.where(low, tile, pltpu.roll(below, 64, 1)),
        jnp.where(low, pltpu.roll(tile, 64, 1), below),
    ]
    far = [above, pltpu.roll(above, 64, 1)]
    for px in range(2):
        a, b = as_blocks(near[px].astype(BF16)), as_blocks(far[px].astype(BF16))
        for xg in range(tile.shape[0] // 16):
            ref[y, 2 * xg + px, :, 0:128] = a[xg]
            ref[y, 2 * xg + px, :, 128:256] = b[xg]


def loop(count, body):
    def step(i, carry):
        body(i)
        return carry

    lax.fori_loop(0, count, step, 0)


AROUND = [(-1, 0), (1, 0), (0, -1), (0, 1), (-1, -1), (-1, 1), (1, -1), (1, 1)]


def span(step, core, width):
    if step == 0:
        return width, width, core
    if step > 0:
        return core, 0, width
    return width, core + width, width


def exchange(ref, widths, send_sems, recv_sems, ty, tx):
    copies = []
    for i, (dy, dx) in enumerate(AROUND):
        sy, ly, ny = span(dy, ref.shape[0] - 2 * widths[0], widths[0])
        sx, lx, nx = span(dx, ref.shape[1] - 2 * widths[1], widths[1])
        copy = pltpu.make_async_remote_copy(
            src_ref=ref.at[pl.ds(sy, ny), pl.ds(sx, nx)],
            dst_ref=ref.at[pl.ds(ly, ny), pl.ds(lx, nx)],
            send_sem=send_sems.at[i],
            recv_sem=recv_sems.at[i],
            device_id=((ty + dy + 16) % 16, (tx + dx + 8) % 8),
            device_id_type=pl.DeviceIdType.MESH,
        )
        copy.start()
        copies.append(copy)
    return copies


def finish(copies):
    for copy in copies:
        copy.wait()


def inside_tile(x, row, row_limit, first, col_limit):
    column = first + iota(x.shape, 0) // 16
    return jnp.where((column >= 0) & (column < col_limit) & row_inside(row, row_limit), x, 0.0)


def whole_kernel(
    readers, raw, head, w4, fs, mo, ms, co, cs, mm, mf, fm, ff,
    out,
    r_fs, r_mo, r_ms, r_co, r_cs, r_mm, r_mf, r_fm, r_ff,
    w_fo, w_fs, w_mo, w_ms, w_co, w_cs, w_mm, w_mf, w_fm, w_ff, w_head,
    outgoing, arrived, held,
    t_ref, low_ref, high_ref, a_ref,
    quads, skip, in_ref, b_ref, s_ref,
    coarse, middle, ci_ref, co_ref, s2_ref, u1_ref, mi_ref, mm_ref, u2_ref, fi_ref, fm_ref,
    first_ref, second_ref, turn_ref,
    load_sems, row_send, row_recv, near_send, near_recv,
    quad_send, quad_recv, skip_send, skip_recv, coarse_send, coarse_recv, middle_send, middle_recv,
):
    ty, tx = lax.axis_index("ty"), lax.axis_index("tx")
    mesh_id = pl.DeviceIdType.MESH
    loads = [
        pltpu.make_async_copy(source, target, load_sems.at[i])
        for i, (source, target) in enumerate(
            zip((fs, mo, ms, co, cs, mm, mf, fm, ff), (r_fs, r_mo, r_ms, r_co, r_cs, r_mm, r_mf, r_fm, r_ff))
        )
    ]
    for load in loads:
        load.start()

    barrier = pltpu.get_barrier_semaphore()
    greeted = [(ty, (tx + d) % 8) for d in range(1, 8)]
    greeted += [((ty + dy + 16) % 16, (tx + dx + 8) % 8) for dy in (-1, 1) for dx in (-1, 0, 1)]
    for device in greeted:
        pl.semaphore_signal(barrier, inc=1, device_id=device, device_id_type=mesh_id)
    pl.semaphore_wait(barrier, len(greeted))

    reader = [readers[ty * 8 + c] for c in range(8)]
    for c in range(8):
        rank = 0
        for earlier in range(c):
            rank += (reader[earlier] == reader[c]).astype(jnp.int32)
        outgoing[c] = raw[jnp.minimum(rank, 2)]
    copies = []
    for d in range(1, 8):
        peer = (tx + d) % 8
        copy = pltpu.make_async_remote_copy(
            src_ref=outgoing.at[peer],
            dst_ref=arrived.at[tx],
            send_sem=row_send.at[d],
            recv_sem=row_recv.at[d],
            device_id=(ty, peer),
            device_id_type=mesh_id,
        )
        copy.start()
        copies.append(copy)
    arrived[tx] = outgoing[tx]
    build_open(w4, w_fo)
    loads[0].wait()
    build_fine(spread_blocks(r_fs, 32), w_fs)
    finish(copies)
    own = readers[ty * 8 + tx] % 8
    held[1, 1] = arrived[own]
    copies = []
    for i, (dy, dx) in enumerate([(0, 1), (1, 0), (1, 1)]):
        copy = pltpu.make_async_remote_copy(
            src_ref=held.at[1, 1],
            dst_ref=held.at[1 - dy, 1 - dx],
            send_sem=near_send.at[i],
            recv_sem=near_recv.at[i],
            device_id=((ty + dy) % 16, (tx + dx) % 8),
            device_id_type=mesh_id,
        )
        copy.start()
        copies.append(copy)
    loads[1].wait()
    build_middle_open(spread_blocks(r_mo, 64, 1), w_mo)
    build_head(head, w_head)
    finish(copies)

    for br in range(4):
        for bc in range(4):
            brick = held[br // 2, bc // 2, br % 2 * 2 + bc % 2].astype(F32)
            ok = True
            if br == 0:
                ok = ty > 0
            if br == 3:
                ok = ty < 15
            if bc == 0:
                ok = (tx > 0) & ok
            if bc == 3:
                ok = (tx < 7) & ok
            if ok is not True:
                brick = jnp.where(ok, brick, 0.0)
            turned = jnp.concatenate([brick] * 4, axis=0).T
            t_ref[8 * br : 8 * br + 8, 16 * bc : 16 * bc + 16, :] = turned.reshape(8, 16, 128)
    lanes = lane_block((24, 128), 32)
    mixed = []
    for y in range(20):
        rows = [t_ref[6 + y, pl.ds(14 + x, 24, stride=2), :] for x in range(4)]
        row = rows[0]
        for x in range(1, 4):
            row = jnp.where(lanes == x, rows[x], row)
        mixed.append(row)
    lhs = jnp.concatenate(
        [jnp.concatenate(mixed[dy : dy + 18], axis=0) for dy in range(3)], axis=1
    ).astype(BF16)
    shape = (432, 128)
    column = tx * 32 - 1 + 2 * (iota(shape, 0) % 24) + iota(shape, 1) // 64
    line = ty * 16 - 1 + iota(shape, 0) // 24
    mask0 = (column >= 0) & (column < 256) & (line >= 0) & (line < 256)

    def opened(k):
        acc = jnp.dot(lhs, w_fo[k], preferred_element_type=F32)
        low_ref[pl.ds(k, 432, stride=16), :] = jnp.where(mask0, jnp.maximum(acc[:, :128], 0.0), 0.0)
        high_ref[pl.ds(k, 432, stride=16), :] = jnp.where(mask0, jnp.maximum(acc[:, 128:], 0.0), 0.0)

    loop(16, opened)

    def packed(y):
        start = pl.multiple_of(y * 384, 384)
        a_ref[y, :, :, 0:128] = as_blocks(low_ref[pl.ds(start, 272), :].astype(BF16))
        a_ref[y, :, :, 128:256] = as_blocks(high_ref[pl.ds(start, 272), :].astype(BF16))

    loop(18, packed)
    quad_lane = lane_block((4, 16, 128), 32)

    def second(yg):
        acc = jnp.maximum(conv(a_ref, w_fs, yg, 16), 0.0)
        skip[2 + 2 * yg, 1:17] = as_blocks(acc[:, :128].astype(BF16))
        skip[3 + 2 * yg, 1:17] = as_blocks(acc[:, 128:].astype(BF16))
        top = jnp.maximum(acc[:, :128], acc[:, 128:])
        top = jnp.maximum(top, pltpu.roll(top, 64, 1))
        top = jnp.maximum(top, pltpu.roll(top, 32, 1)).reshape(4, 4, 16, 128)
        quad = top[:, 0]
        for q in range(1, 4):
            quad = jnp.where(quad_lane == q, top[:, q], quad)
        quads[2 + yg, 1:5] = quad.astype(BF16)

    loop(8, second)
    copies = exchange(quads, (2, 1), quad_send, quad_recv, ty, tx)
    skip_copies = exchange(skip, (2, 1), skip_send, skip_recv, ty, tx)
    loads[2].wait()
    build_middle(spread_blocks(r_ms, 64), w_ms)
    loads[3].wait()
    build_middle(spread_blocks(r_co, 64), w_co)
    finish(copies)

    def spread(y):
        c = as_rows(quads[y]).astype(F32)
        c = inside_tile(c, ty * 8 - 2 + y, 128, tx * 4 - 1, 32)
        below, above = from_below(c), from_above(c)
        lanes = lane_block(c.shape, 32)
        for q in range(4):
            tile = jnp.where(lanes == 0, pltpu.roll(c, (-32 * q) % 128, 1), 0.0)
            tile = jnp.where(lanes == 1, pltpu.roll(below, (32 - 32 * q) % 128, 1), tile)
            tile = jnp.where(lanes == 2, pltpu.roll(above, (64 - 32 * q) % 128, 1), tile)
            blocks = as_blocks(tile.astype(BF16))
            lane = 128 * (q % 2)
            for quad in range(6):
                place = 2 * quad - 1 + q // 2
                if 0 <= place < 10:
                    in_ref[y, place, :, lane : lane + 128] = blocks[quad]

    loop(12, spread)
    mask1 = column_mask(144, tx * 16 - 1, 16, 8)

    def middle_open(yg):
        acc = conv(in_ref, w_mo, yg, 9)
        for py in range(2):
            inside = row_inside(ty * 8 - 1 + 2 * yg + py, 128)
            store_middle(b_ref, 2 * yg + py, kept(acc[:, 128 * py : 128 * py + 128], mask1, inside))

    loop(5, middle_open)
    low = lane_block((4, 8, 128), 64) == 0

    def middle_second(yg):
        acc = jnp.maximum(conv(b_ref, w_ms, yg, 8), 0.0)
        middle[4 + 2 * yg, 2:10] = as_blocks(acc[:, :128].astype(BF16))
        middle[5 + 2 * yg, 2:10] = as_blocks(acc[:, 128:].astype(BF16))
        top = jnp.maximum(acc[:, :128], acc[:, 128:])
        top = jnp.maximum(top, pltpu.roll(top, 64, 1))
        s_ref[...] = jnp.maximum(top, from_above(top))
        some = s_ref[pl.ds(0, 64, stride=2), :].reshape(4, 2, 8, 128)
        pair = jnp.where(low, some[:, 0], some[:, 1])
        coarse[4 + yg, 2:6] = jnp.concatenate([pair, jnp.zeros_like(pair)], axis=1).astype(BF16)

    loop(4, middle_second)
    copies = exchange(coarse, (4, 2), coarse_send, coarse_recv, ty, tx)
    middle_copies = exchange(middle, (4, 2), middle_send, middle_recv, ty, tx)
    loads[4].wait()
    build_middle(spread_blocks(r_cs, 64), w_cs)
    loads[5].wait()
    build_middle_merge(r_mm, w_mm)
    finish(copies)

    def coarse_in(y):
        x = as_rows(coarse[y]).astype(F32)
        store_middle(ci_ref, y, inside_tile(x, ty * 4 - 4 + y, 64, tx * 4 - 2, 32))

    loop(12, coarse_in)
    mask2 = column_mask(112, tx * 8 - 3, 8, 8) & (iota((112, 128), 0) % 16 < 8)

    def coarse_open(yg):
        acc = conv(ci_ref, w_co, yg, 7)
        for py in range(2):
            inside = row_inside(ty * 4 - 3 + 2 * yg + py, 64)
            store_middle(co_ref, 2 * yg + py, kept(acc[:, 128 * py : 128 * py + 128], mask2, inside))

    loop(5, coarse_open)
    mask3 = column_mask(96, tx * 8 - 2, 8, 8)

    def coarse_second(yg):
        acc = conv(co_ref, w_cs, yg, 6)
        for py in range(2):
            inside = row_inside(ty * 4 - 2 + 2 * yg + py, 64)
            tile = kept(acc[:, 128 * py : 128 * py + 128], mask3, inside)
            half = tile.reshape(6, 16, 128)[:, :8].reshape(48, 128)
            s2_ref[pl.ds(0, 48, stride=2), :] = half
            s2_ref[pl.ds(1, 48, stride=2), :] = half
            store_single(u1_ref, 2 * yg + py, s2_ref[...])

    loop(4, coarse_second)
    loads[6].wait()
    build_middle(spread_blocks(r_mf, 64), w_mf)
    finish(middle_copies)

    def middle_in(y):
        x = as_rows(middle[y]).astype(F32)
        store_middle(mi_ref, y, inside_tile(x, ty * 8 - 4 + y, 128, tx * 8 - 2, 64))

    loop(16, middle_in)
    mask4 = column_mask(176, tx * 16 - 3, 16, 8)

    def middle_merge(yg):
        acc = conv(mi_ref, w_mm, yg, 11, up_pieces(u1_ref, yg, 0, 11))
        for py in range(2):
            inside = row_inside(ty * 8 - 3 + 2 * yg + py, 128)
            store_middle(mm_ref, 2 * yg + py, kept(acc[:, 128 * py : 128 * py + 128], mask4, inside))

    loop(7, middle_merge)
    mask5 = column_mask(160, tx * 16 - 2, 16, 8)

    def middle_final(yg):
        acc = conv(mm_ref, w_mf, yg, 10)
        for py in range(2):
            inside = row_inside(ty * 8 - 2 + 2 * yg + py, 128)
            store_single(u2_ref, 2 * yg + py, kept(acc[:, 128 * py : 128 * py + 128], mask5, inside))

    loop(6, middle_final)
    loads[7].wait()
    build_fine_merge(r_fm, w_fm)
    loads[8].wait()
    build_fine(spread_blocks(r_ff, 32), w_ff)
    finish(skip_copies)

    def fine_in(y):
        x = as_rows(skip[y]).astype(F32)
        store_fine(fi_ref, y, inside_tile(x, ty * 16 - 2 + y, 256, tx * 16 - 1, 128))

    loop(20, fine_in)
    mask6 = column_mask(272, tx * 32 - 1, 32, 8)

    def fine_merge(yg):
        acc = conv(fi_ref, w_fm, yg, 17, up_pieces(u2_ref, yg, 1, 17))
        for py in range(2):
            inside = row_inside(ty * 16 - 1 + 2 * yg + py, 256)
            store_fine(fm_ref, 2 * yg + py, kept(acc[:, 128 * py : 128 * py + 128], mask6, inside))

    loop(9, fine_merge)
    first_ref[...] = jnp.zeros_like(first_ref)
    second_ref[...] = jnp.zeros_like(second_ref)

    def fine_final(yg):
        acc = jnp.maximum(conv(fm_ref, w_ff, yg, 16), 0.0).astype(BF16)
        logits = jnp.dot(acc, w_head[...], preferred_element_type=F32)
        first_ref[...] += pltpu.roll(logits[:, :128], 2 * yg, 1)
        second_ref[...] += pltpu.roll(logits[:, 128:], 2 * yg, 1)

    loop(8, fine_final)

    def finished(k):
        turn_ref[pl.ds(0, 16, stride=2), :] = first_ref[pl.ds(k, 16, stride=16), :]
        turn_ref[pl.ds(1, 16, stride=2), :] = second_ref[pl.ds(k, 16, stride=16), :]
        turned = turn_ref[...].T
        for c in range(3):
            for pz in range(2):
                row = 32 * c + 16 * pz
                out[c, 2 * k + pz] = turned[row : row + 16]

    loop(16, finished)


def per_device(
    raw_bricks,
    stretch_reader,
    fine_open,
    fine_second,
    middle_open,
    middle_second,
    coarse_open,
    coarse_second,
    middle_merge,
    middle_final,
    fine_merge,
    fine_final,
    affinity_head,
):
    def flat(w):
        return w.reshape(27, w.shape[3], w.shape[4])

    weights = [
        flat(fine_second),
        flat(middle_open.transpose(0, 1, 2, 4, 3)),
        flat(middle_second),
        flat(coarse_open),
        flat(coarse_second),
        flat(middle_merge),
        flat(middle_final),
        flat(fine_merge),
        flat(fine_final),
    ]
    w4 = jnp.tile(fine_open.reshape(27, 32), (1, 4)).astype(F32)
    vmem = pl.BlockSpec(memory_space=pltpu.VMEM)
    smem = pl.BlockSpec(memory_space=pltpu.SMEM)
    hbm = pl.BlockSpec(memory_space=pl.ANY)
    dma = pltpu.SemaphoreType.DMA

    def half(*shape):
        return pltpu.VMEM(shape, BF16)

    def full(*shape):
        return pltpu.VMEM(shape, F32)

    return pl.pallas_call(
        whole_kernel,
        out_shape=jax.ShapeDtypeStruct((3, DEPTH, TILE_Y, TILE_X), F32),
        in_specs=[smem] + [vmem] * 3 + [hbm] * 9,
        out_specs=vmem,
        scratch_shapes=[half(*w.shape) for w in weights]
        + [half(16, 384, 256)]
        + [half(size, 256) for size in (2048, 2048, 3072, 3072, 3072, 4096, 3072, 3072, 2048, 256)]
        + [
            half(8, 4, 32, 128),
            half(8, 4, 32, 128),
            half(2, 2, 4, 32, 128),
            full(32, 64, 128),
            full(432 * 16, 128),
            full(432 * 16, 128),
            half(18, 17, 16, 256),
            half(12, 6, 16, 128),
            half(20, 18, 16, 128),
            half(12, 10, 16, 256),
            half(10, 9, 16, 384),
            full(128, 128),
            half(12, 8, 16, 128),
            half(16, 12, 16, 128),
            half(12, 8, 16, 384),
            half(10, 7, 16, 384),
            full(96, 128),
            half(8, 12, 16, 256),
            half(16, 12, 16, 384),
            half(14, 11, 16, 384),
            half(12, 20, 16, 256),
            half(20, 18, 16, 256),
            half(18, 17, 16, 256),
            full(256, 128),
            full(256, 128),
            full(32, 128),
            dma((9,)),
            dma((8,)),
            dma((8,)),
            dma((3,)),
            dma((3,)),
        ]
        + [dma((8,))] * 8,
        name="whole",
        compiler_params=pltpu.CompilerParams(
            vmem_limit_bytes=58 * MIB, collective_id=0, has_side_effects=True
        ),
        cost_estimate=pl.CostEstimate(flops=10**10, bytes_accessed=10**7, transcendentals=0),
    )(stretch_reader, raw_bricks.reshape(3, 4, 32, 128), affinity_head, w4, *weights)


def solution(mesh):
    placed = (P(("ty", "tx"), None, None, None),) + (P(),) * 12
    return jax.shard_map(
        per_device, mesh=mesh, in_specs=placed, out_specs=P(None, None, "ty", "tx"), check_vma=False
    )
```

```python
import jax
import jax.numpy as jnp
from jax import lax
from jax.experimental import pallas as pl
from jax.experimental.pallas import tpu as pltpu
from jax.sharding import PartitionSpec as P

TILE_Y = 16
TILE_X = 32
DEPTH = 32
BF16 = jnp.bfloat16
F32 = jnp.float32
MIB = 1 << 20


def iota(shape, dim):
    return lax.broadcasted_iota(jnp.int32, shape, dim)


def lane_block(shape, width):
    return iota(shape, len(shape) - 1) // width


def spread_blocks(w_ref, out_chans, out_dim=0):
    eye = (iota((out_chans, 128), 0) == iota((out_chans, 128), 1) % out_chans).astype(BF16)
    return [
        lax.dot_general(w_ref[t], eye, (((out_dim,), (0,)), ((), ())), preferred_element_type=F32)
        for t in range(27)
    ]


def tap(a, b, e):
    if 0 <= a <= 2 and 0 <= b <= 2 and 0 <= e <= 2:
        return 9 * a + 3 * b + e
    return None


def masked_sum(blocks, taps, width):
    shape = blocks[0].shape
    lanes = lane_block(shape, width)
    tile = jnp.zeros(shape, F32)
    for place, index in enumerate(taps):
        if index is not None:
            tile = jnp.where(lanes == place, blocks[index], tile)
    return tile


def build_fine(blocks, out_ref):
    for y in range(4):
        for j in range(2):
            for half in range(2):
                for px_in in range(2):
                    for slot in range(2):
                        z = (1 + slot) if half == 0 else (3, 0)[slot]
                        row = (y * 2 + j) * 256 + half * 128 + px_in * 64 + slot * 32
                        for py in range(2):
                            taps = [
                                tap(z - pz, y - py, 2 * j + px_in - px)
                                for px in range(2)
                                for pz in range(2)
                            ]
                            out_ref[row : row + 32, py * 128 : (py + 1) * 128] = masked_sum(
                                blocks, taps, 32
                            ).astype(BF16)


def build_middle(blocks, out_ref):
    for y in range(4):
        for j in range(2):
            for slot, dz in enumerate((1, 0, 2)):
                for px_in in range(2):
                    row = (y * 2 + j) * 384 + slot * 128 + px_in * 64
                    for py in range(2):
                        taps = [tap(dz, y - py, 2 * j + px_in - px) for px in range(2)]
                        out_ref[row : row + 64, py * 128 : (py + 1) * 128] = masked_sum(
                            blocks, taps, 64
                        ).astype(BF16)


def build_middle_open(blocks, out_ref):
    for y in range(4):
        for j in range(2):
            for px_in in range(2):
                for slot, dz in enumerate((1, 0, 2, 9)):
                    row = (y * 2 + j) * 256 + px_in * 128 + slot * 32
                    for py in range(2):
                        taps = [tap(dz, y - py, 2 * j + px_in - px) for px in range(2)]
                        out_ref[row : row + 32, py * 128 : (py + 1) * 128] = masked_sum(
                            blocks, taps, 64
                        ).astype(BF16)


def build_up(zcombined, out_ref, row0):
    shape = (64, 128)
    odd = lane_block(shape, 64) == 1
    for slot in range(4):
        for xc in range(2):
            rows = None
            if slot < 3:
                rows = []
                for dy in range(3):
                    t = zcombined[slot][dy]
                    if xc == 0:
                        rows.append(jnp.where(odd, t[0], t[0] + t[1]))
                    else:
                        rows.append(jnp.where(odd, t[1] + t[2], t[2]))
            for yc in range(2):
                row = row0 + (yc * 2 + xc) * 256 + slot * 64
                for py in range(2):
                    if rows is None:
                        tile = jnp.zeros(shape, F32)
                    elif (py, yc) == (0, 0):
                        tile = rows[0] + rows[1]
                    elif (py, yc) == (0, 1):
                        tile = rows[2]
                    elif (py, yc) == (1, 0):
                        tile = rows[0]
                    else:
                        tile = rows[1] + rows[2]
                    out_ref[row : row + 64, py * 128 : (py + 1) * 128] = tile.astype(BF16)


def build_open(w4_ref, base_ref, out_ref):
    base_ref[...] = jnp.zeros_like(base_ref)
    rows = [w4_ref[t : t + 1, :] for t in range(27)]
    for dy in range(3):
        for z in range(6):
            for x in range(4):
                row = 40 + z // 3 * 128 + z % 3 * 40 + x
                for half in range(2):
                    taps = []
                    for px in range(2):
                        for p in range(2):
                            z_out = p if half == 0 else (2, -1)[p]
                            taps.append(tap(z - 1 - z_out, dy, x - px))
                    base_ref[dy, row : row + 1, 128 * half : 128 * half + 128] = masked_sum(
                        rows, taps, 32
                    )
    for xp in range(17):
        for dy in range(3):
            out_ref[xp, 256 * dy : 256 * dy + 256] = base_ref[
                dy, 40 - 2 * xp : 296 - 2 * xp
            ].astype(BF16)


def build_middle_merge(w_ref, out_ref):
    both = spread_blocks(w_ref, 64)
    build_middle([block[64:128] for block in both], out_ref)
    up = [block[:64] for block in both]
    grid = [[[up[9 * dz + 3 * dy + dx] for dx in range(3)] for dy in range(3)] for dz in (1, 0, 2)]
    build_up(grid, out_ref, 3072)


def build_fine_merge(w_ref, out_ref):
    both = spread_blocks(w_ref, 32)
    build_fine([block[64:96] for block in both], out_ref)
    up = [block[:64] for block in both]
    odd_z = lane_block((64, 128), 32) % 2 == 1

    def zmix(slot, dy, dx):
        w0, w1, w2 = (up[9 * a + 3 * dy + dx] for a in range(3))
        if slot == 0:
            return jnp.where(odd_z, w0 + w1, w1 + w2)
        if slot == 1:
            return jnp.where(odd_z, 0.0, w0)
        return jnp.where(odd_z, w2, 0.0)

    grid = [[[zmix(slot, dy, dx) for dx in range(3)] for dy in range(3)] for slot in range(3)]
    build_up(grid, out_ref, 2048)


def build_head(head_ref, out_ref):
    column = iota((256, 32), 0) % 128 // 32
    picked = jnp.zeros((256, 32), F32)
    for c in range(3):
        picked = jnp.where(column == c, head_ref[c : c + 1, :].astype(F32), picked)
    eye = (iota((256, 32), 0) % 32 == iota((256, 32), 1)).astype(BF16)
    full = lax.dot_general(
        eye, picked.astype(BF16), (((1,), (1,)), ((), ())), preferred_element_type=F32
    )
    row, col = iota((256, 256), 0), iota((256, 256), 1)
    fits = (row // 64 % 2 == col // 128) & (row // 32 % 2 == col // 16 % 2)
    fits = fits & (row // 128 == col % 16) & (col % 128 < 96)
    out_ref[...] = jnp.where(fits, full, 0.0).astype(BF16)


def from_below(x):
    return jnp.where(iota(x.shape, 0) % 16 == 0, 0.0, pltpu.roll(x, 1, 0))


def from_above(x):
    return jnp.where(iota(x.shape, 0) % 16 == 15, 0.0, pltpu.roll(x, x.shape[0] - 1, 0))


def as_rows(x):
    return x.reshape(x.shape[0] * 16, x.shape[2])


def as_blocks(x):
    return x.reshape(x.shape[0] // 16, 16, x.shape[1])


def window(src, yg, groups, up=None, shift=0):
    pieces = [as_rows(src[2 * yg + y, j : j + groups]) for y in range(4) for j in range(2)]
    if up is not None:
        y, x = yg + shift, shift
        pieces += [
            as_rows(up[y + yc, x + xc : x + xc + groups]) for yc in range(2) for xc in range(2)
        ]
    return jnp.concatenate(pieces, axis=1)


def conv(src, w_ref, yg, groups, up=None, shift=0):
    lhs = window(src, yg, groups, up, shift)
    return jnp.dot(lhs, w_ref[...], preferred_element_type=F32)


def conv_all(src, w_ref, lines, groups, up=None):
    lhs = jnp.concatenate([window(src, yg, groups, up) for yg in range(lines)], axis=0)
    acc = jnp.dot(lhs, w_ref[...], preferred_element_type=F32)
    rows = groups * 16
    return [acc[yg * rows : (yg + 1) * rows] for yg in range(lines)]


def column_mask(rows, start, width, tiles):
    shape = (rows, 128)
    column = start + 2 * (iota(shape, 0) // 16) + iota(shape, 1) // 64
    return (column >= 0) & (column < width * tiles)


def row_inside(row, limit):
    return (row >= 0) & (row < limit)


def kept(value, mask, inside):
    return jnp.where(mask & inside, jnp.maximum(value, 0.0), 0.0)


def ends_of(tile):
    odd = lane_block(tile.shape, 32) % 2 == 1
    return jnp.where(odd, from_below(tile), from_above(tile))


def store_fine(ref, y, tile):
    ref[y, :, :, 0:128] = as_blocks(tile.astype(BF16))
    ref[y, :, :, 128:256] = as_blocks(ends_of(tile).astype(BF16))


def store_middle(ref, y, tile):
    ref[y, :, :, 0:128] = as_blocks(tile.astype(BF16))
    ref[y, :, :, 128:256] = as_blocks(from_below(tile).astype(BF16))
    ref[y, :, :, 256:384] = as_blocks(from_above(tile).astype(BF16))


def store_single(ref, y, tile):
    below, above = from_below(tile), from_above(tile)
    low = lane_block(tile.shape, 64) == 0
    near = [
        jnp.where(low, tile, pltpu.roll(below, 64, 1)),
        jnp.where(low, pltpu.roll(tile, 64, 1), below),
    ]
    far = [above, pltpu.roll(above, 64, 1)]
    for px in range(2):
        a, b = as_blocks(near[px].astype(BF16)), as_blocks(far[px].astype(BF16))
        for xg in range(tile.shape[0] // 16):
            ref[y, 2 * xg + px, :, 0:128] = a[xg]
            ref[y, 2 * xg + px, :, 128:256] = b[xg]


def loop(count, body, unroll=1):
    def step(i, carry):
        body(i)
        return carry

    lax.fori_loop(0, count, step, 0, unroll=unroll)


def each(parts, body):
    for i, part in enumerate(parts):
        body(i, part)


AROUND = [(-1, 0), (1, 0), (0, -1), (0, 1), (-1, -1), (-1, 1), (1, -1), (1, 1)]


def span(step, core, width):
    if step == 0:
        return width, width, core
    if step > 0:
        return core, 0, width
    return width, core + width, width


def exchange(ref, widths, send_sems, recv_sems, ty, tx):
    copies = []
    for i, (dy, dx) in enumerate(AROUND):
        sy, ly, ny = span(dy, ref.shape[0] - 2 * widths[0], widths[0])
        sx, lx, nx = span(dx, ref.shape[1] - 2 * widths[1], widths[1])
        copy = pltpu.make_async_remote_copy(
            src_ref=ref.at[pl.ds(sy, ny), pl.ds(sx, nx)],
            dst_ref=ref.at[pl.ds(ly, ny), pl.ds(lx, nx)],
            send_sem=send_sems.at[i],
            recv_sem=recv_sems.at[i],
            device_id=((ty + dy + 16) % 16, (tx + dx + 8) % 8),
            device_id_type=pl.DeviceIdType.MESH,
        )
        copy.start()
        copies.append(copy)
    return copies


def finish(copies):
    for copy in copies:
        copy.wait()


def inside_tile(x, row, row_limit, first, col_limit):
    column = first + iota(x.shape, 0) // 16
    return jnp.where((column >= 0) & (column < col_limit) & row_inside(row, row_limit), x, 0.0)


def whole_kernel(
    readers, raw, head, w4, fs, mo, ms, co, cs, mm, mf, fm, ff,
    out,
    r_fs, r_mo, r_ms, r_co, r_cs, r_mm, r_mf, r_fm, r_ff,
    w_fo, w_fs, w_mo, w_ms, w_co, w_cs, w_mm, w_mf, w_fm, w_ff, w_head,
    outgoing, arrived, held,
    base_ref, z_ref, a_ref,
    quads, skip, in_ref, b_ref, s_ref,
    coarse, middle, ci_ref, co_ref, s2_ref, u1_ref, mi_ref, mm_ref, u2_ref, fi_ref, fm_ref,
    first_ref, second_ref, turn_ref,
    load_sems, row_send, row_recv, near_send, near_recv,
    quad_send, quad_recv, skip_send, skip_recv, coarse_send, coarse_recv, middle_send, middle_recv,
):
    ty, tx = lax.axis_index("ty"), lax.axis_index("tx")
    mesh_id = pl.DeviceIdType.MESH
    loads = [
        pltpu.make_async_copy(source, target, load_sems.at[i])
        for i, (source, target) in enumerate(
            zip((fs, mo, ms, co, cs, mm, mf, fm, ff), (r_fs, r_mo, r_ms, r_co, r_cs, r_mm, r_mf, r_fm, r_ff))
        )
    ]
    for load in loads:
        load.start()

    barrier = pltpu.get_barrier_semaphore()
    greeted = [(ty, (tx + d) % 8) for d in range(1, 8)]
    greeted += [((ty + dy + 16) % 16, (tx + dx + 8) % 8) for dy in (-1, 1) for dx in (-1, 0, 1)]
    for device in greeted:
        pl.semaphore_signal(barrier, inc=1, device_id=device, device_id_type=mesh_id)
    pl.semaphore_wait(barrier, len(greeted))

    reader = [readers[ty * 8 + c] for c in range(8)]
    for c in range(8):
        rank = 0
        for earlier in range(c):
            rank += (reader[earlier] == reader[c]).astype(jnp.int32)
        outgoing[c] = raw[jnp.minimum(rank, 2)]
    copies = []
    for d in range(1, 8):
        peer = (tx + d) % 8
        copy = pltpu.make_async_remote_copy(
            src_ref=outgoing.at[peer],
            dst_ref=arrived.at[tx],
            send_sem=row_send.at[d],
            recv_sem=row_recv.at[d],
            device_id=(ty, peer),
            device_id_type=mesh_id,
        )
        copy.start()
        copies.append(copy)
    arrived[tx] = outgoing[tx]
    build_open(w4, base_ref, w_fo)
    loads[0].wait()
    build_fine(spread_blocks(r_fs, 32), w_fs)
    finish(copies)
    own = readers[ty * 8 + tx] % 8
    held[1, 1] = arrived[own]
    copies = []
    for i, (dy, dx) in enumerate([(0, 1), (1, 0), (1, 1)]):
        copy = pltpu.make_async_remote_copy(
            src_ref=held.at[1, 1],
            dst_ref=held.at[1 - dy, 1 - dx],
            send_sem=near_send.at[i],
            recv_sem=near_recv.at[i],
            device_id=((ty + dy) % 16, (tx + dx) % 8),
            device_id_type=mesh_id,
        )
        copy.start()
        copies.append(copy)
    loads[1].wait()
    build_middle_open(spread_blocks(r_mo, 64, 1), w_mo)
    build_head(head, w_head)
    finish(copies)

    z_ref[:, 0:8] = jnp.zeros((20, 8, 128), F32)
    z_ref[:, 32:40] = jnp.zeros((20, 8, 128), F32)
    lane = iota((32, 128), 1)
    lines = []
    for br in range(4):
        bricks = []
        for bc in range(4):
            brick = held[br // 2, bc // 2, br % 2 * 2 + bc % 2].astype(F32)
            ok = True
            if br == 0:
                ok = ty > 0
            if br == 3:
                ok = ty < 15
            if bc == 0:
                ok = (tx > 0) & ok
            if bc == 3:
                ok = (tx < 7) & ok
            if ok is not True:
                brick = jnp.where(ok, brick, 0.0)
            bricks.append(brick)
        for r in ((6, 7), range(8), range(8), (0, 1))[br]:
            y = 8 * br + r - 6
            line = jnp.where(lane < 36, pltpu.roll(bricks[3], (34 - 16 * r) % 128, 1), 0.0)
            line = jnp.where(lane < 34, pltpu.roll(bricks[2], (18 - 16 * r) % 128, 1), line)
            line = jnp.where(lane < 18, pltpu.roll(bricks[1], (2 - 16 * r) % 128, 1), line)
            line = jnp.where(lane < 2, pltpu.roll(bricks[0], (-14 - 16 * r) % 128, 1), line)
            z_ref[y, 4:36, :] = line
            parts = [z_ref[y, pl.ds(2 + z, 16, stride=2), :] for z in range(6)]
            for t in range(2):
                tile = parts[3 * t]
                for i in (1, 2):
                    tile = tile + pltpu.roll(parts[3 * t + i], 40 * i, 1)
                parts[t] = tile
            lines.append(jnp.concatenate(parts[:2], axis=1).astype(BF16))
    lhs = jnp.concatenate(
        [jnp.concatenate(lines[dy : dy + 18], axis=0) for dy in range(3)], axis=1
    )
    shape = (288, 128)
    k_row, p_lane = iota(shape, 0) % 16, iota(shape, 1) // 32 % 2
    line_ok = row_inside(ty * 16 - 1 + iota(shape, 0) // 16, 256)
    ends_ok = ~((k_row == 0) & (p_lane == 1)) & ~((k_row == 15) & (p_lane == 0)) & line_ok
    px_lane = iota(shape, 1) // 64
    for xp in range(17):
        acc = jnp.maximum(jnp.dot(lhs, w_fo[xp], preferred_element_type=F32), 0.0)
        for half, ok in enumerate((line_ok, ends_ok)):
            if xp == 0:
                ok = ok & ((px_lane == 1) | (tx > 0))
            if xp == 16:
                ok = ok & ((px_lane == 0) | (tx < 7))
            tile = jnp.where(ok, acc[:, 128 * half : 128 * half + 128], 0.0).astype(BF16)
            a_ref[:, xp, :, 128 * half : 128 * half + 128] = as_blocks(tile)
    quad_lane = lane_block((4, 16, 128), 32)

    def second(yg):
        acc = jnp.maximum(conv(a_ref, w_fs, yg, 16), 0.0)
        skip[2 + 2 * yg, 1:17] = as_blocks(acc[:, :128].astype(BF16))
        skip[3 + 2 * yg, 1:17] = as_blocks(acc[:, 128:].astype(BF16))
        top = jnp.maximum(acc[:, :128], acc[:, 128:])
        top = jnp.maximum(top, pltpu.roll(top, 64, 1))
        top = jnp.maximum(top, pltpu.roll(top, 32, 1)).reshape(4, 4, 16, 128)
        quad = top[:, 0]
        for q in range(1, 4):
            quad = jnp.where(quad_lane == q, top[:, q], quad)
        quads[2 + yg, 1:5] = quad.astype(BF16)

    for yg in range(8):
        second(yg)
    copies = exchange(quads, (2, 1), quad_send, quad_recv, ty, tx)
    skip_copies = exchange(skip, (2, 1), skip_send, skip_recv, ty, tx)
    loads[2].wait()
    build_middle(spread_blocks(r_ms, 64), w_ms)
    loads[3].wait()
    build_middle(spread_blocks(r_co, 64), w_co)
    finish(copies)

    def spread(y):
        c = as_rows(quads[y]).astype(F32)
        c = inside_tile(c, ty * 8 - 2 + y, 128, tx * 4 - 1, 32)
        below, above = from_below(c), from_above(c)
        lanes = lane_block(c.shape, 32)
        for q in range(4):
            tile = jnp.where(lanes == 0, pltpu.roll(c, (-32 * q) % 128, 1), 0.0)
            tile = jnp.where(lanes == 1, pltpu.roll(below, (32 - 32 * q) % 128, 1), tile)
            tile = jnp.where(lanes == 2, pltpu.roll(above, (64 - 32 * q) % 128, 1), tile)
            blocks = as_blocks(tile.astype(BF16))
            lane = 128 * (q % 2)
            for quad in range(6):
                place = 2 * quad - 1 + q // 2
                if 0 <= place < 10:
                    in_ref[y, place, :, lane : lane + 128] = blocks[quad]

    loop(12, spread, 3)
    mask1 = column_mask(144, tx * 16 - 1, 16, 8)

    def middle_open(yg, acc):
        for py in range(2):
            inside = row_inside(ty * 8 - 1 + 2 * yg + py, 128)
            store_middle(b_ref, 2 * yg + py, kept(acc[:, 128 * py : 128 * py + 128], mask1, inside))

    each(conv_all(in_ref, w_mo, 5, 9), middle_open)
    low = lane_block((4, 8, 128), 64) == 0

    def middle_second(yg, acc):
        acc = jnp.maximum(acc, 0.0)
        middle[4 + 2 * yg, 2:10] = as_blocks(acc[:, :128].astype(BF16))
        middle[5 + 2 * yg, 2:10] = as_blocks(acc[:, 128:].astype(BF16))
        top = jnp.maximum(acc[:, :128], acc[:, 128:])
        top = jnp.maximum(top, pltpu.roll(top, 64, 1))
        s_ref[yg] = jnp.maximum(top, from_above(top))
        some = s_ref[yg, pl.ds(0, 64, stride=2), :].reshape(4, 2, 8, 128)
        pair = jnp.where(low, some[:, 0], some[:, 1])
        coarse[4 + yg, 2:6] = jnp.concatenate([pair, jnp.zeros_like(pair)], axis=1).astype(BF16)

    each(conv_all(b_ref, w_ms, 4, 8), middle_second)
    copies = exchange(coarse, (4, 2), coarse_send, coarse_recv, ty, tx)
    middle_copies = exchange(middle, (4, 2), middle_send, middle_recv, ty, tx)
    loads[4].wait()
    build_middle(spread_blocks(r_cs, 64), w_cs)
    loads[5].wait()
    build_middle_merge(r_mm, w_mm)
    finish(copies)

    def coarse_in(y):
        x = as_rows(coarse[y]).astype(F32)
        store_middle(ci_ref, y, inside_tile(x, ty * 4 - 4 + y, 64, tx * 4 - 2, 32))

    loop(12, coarse_in)
    mask2 = column_mask(112, tx * 8 - 3, 8, 8) & (iota((112, 128), 0) % 16 < 8)

    def coarse_open(yg, acc):
        for py in range(2):
            inside = row_inside(ty * 4 - 3 + 2 * yg + py, 64)
            store_middle(co_ref, 2 * yg + py, kept(acc[:, 128 * py : 128 * py + 128], mask2, inside))

    each(conv_all(ci_ref, w_co, 5, 7), coarse_open)
    mask3 = column_mask(96, tx * 8 - 2, 8, 8)

    def coarse_second(yg, acc):
        for py in range(2):
            inside = row_inside(ty * 4 - 2 + 2 * yg + py, 64)
            tile = kept(acc[:, 128 * py : 128 * py + 128], mask3, inside)
            half = tile.reshape(6, 16, 128)[:, :8].reshape(48, 128)
            s2_ref[2 * yg + py, pl.ds(0, 48, stride=2), :] = half
            s2_ref[2 * yg + py, pl.ds(1, 48, stride=2), :] = half
            store_single(u1_ref, 2 * yg + py, s2_ref[2 * yg + py])

    each(conv_all(co_ref, w_cs, 4, 6), coarse_second)
    loads[6].wait()
    build_middle(spread_blocks(r_mf, 64), w_mf)
    finish(middle_copies)

    def middle_in(y):
        x = as_rows(middle[y]).astype(F32)
        store_middle(mi_ref, y, inside_tile(x, ty * 8 - 4 + y, 128, tx * 8 - 2, 64))

    loop(16, middle_in)
    mask4 = column_mask(176, tx * 16 - 3, 16, 8)

    def middle_merge(yg, acc):
        for py in range(2):
            inside = row_inside(ty * 8 - 3 + 2 * yg + py, 128)
            store_middle(mm_ref, 2 * yg + py, kept(acc[:, 128 * py : 128 * py + 128], mask4, inside))

    each(conv_all(mi_ref, w_mm, 7, 11, u1_ref), middle_merge)
    mask5 = column_mask(160, tx * 16 - 2, 16, 8)

    def middle_final(yg, acc):
        for py in range(2):
            inside = row_inside(ty * 8 - 2 + 2 * yg + py, 128)
            store_single(u2_ref, 2 * yg + py, kept(acc[:, 128 * py : 128 * py + 128], mask5, inside))

    each(conv_all(mm_ref, w_mf, 6, 10), middle_final)
    loads[7].wait()
    build_fine_merge(r_fm, w_fm)
    loads[8].wait()
    build_fine(spread_blocks(r_ff, 32), w_ff)
    finish(skip_copies)

    def fine_in(y):
        x = as_rows(skip[y]).astype(F32)
        store_fine(fi_ref, y, inside_tile(x, ty * 16 - 2 + y, 256, tx * 16 - 1, 128))

    loop(20, fine_in, 2)
    mask6 = column_mask(272, tx * 32 - 1, 32, 8)

    def fine_merge(yg):
        acc = conv(fi_ref, w_fm, yg, 17, u2_ref, 1)
        for py in range(2):
            inside = row_inside(ty * 16 - 1 + 2 * yg + py, 256)
            store_fine(fm_ref, 2 * yg + py, kept(acc[:, 128 * py : 128 * py + 128], mask6, inside))

    for yg in range(9):
        fine_merge(yg)

    def fine_final(yg):
        acc = jnp.maximum(conv(fm_ref, w_ff, yg, 16), 0.0).astype(BF16)
        logits = jnp.dot(acc, w_head[...], preferred_element_type=F32)
        low, high = logits[:, :128], logits[:, 128:]
        if yg == 0:
            first_ref[...] = low
            second_ref[...] = high
        else:
            first_ref[...] += pltpu.roll(low, 2 * yg, 1)
            second_ref[...] += pltpu.roll(high, 2 * yg, 1)

    for yg in range(8):
        fine_final(yg)

    def finished(k):
        turn_ref[k, pl.ds(0, 16, stride=2), :] = first_ref[pl.ds(k, 16, stride=16), :]
        turn_ref[k, pl.ds(1, 16, stride=2), :] = second_ref[pl.ds(k, 16, stride=16), :]
        turned = turn_ref[k].T
        for c in range(3):
            for pz in range(2):
                row = 32 * c + 16 * pz
                out[c, 2 * k + pz] = turned[row : row + 16]

    for k in range(16):
        finished(k)


def per_device(
    raw_bricks,
    stretch_reader,
    fine_open,
    fine_second,
    middle_open,
    middle_second,
    coarse_open,
    coarse_second,
    middle_merge,
    middle_final,
    fine_merge,
    fine_final,
    affinity_head,
):
    def flat(w):
        return w.reshape(27, w.shape[3], w.shape[4])

    weights = [
        flat(fine_second),
        flat(middle_open.transpose(0, 1, 2, 4, 3)),
        flat(middle_second),
        flat(coarse_open),
        flat(coarse_second),
        flat(middle_merge),
        flat(middle_final),
        flat(fine_merge),
        flat(fine_final),
    ]
    w4 = jnp.tile(fine_open.reshape(27, 32), (1, 4)).astype(F32)
    vmem = pl.BlockSpec(memory_space=pltpu.VMEM)
    smem = pl.BlockSpec(memory_space=pltpu.SMEM)
    hbm = pl.BlockSpec(memory_space=pl.ANY)
    dma = pltpu.SemaphoreType.DMA

    def half(*shape):
        return pltpu.VMEM(shape, BF16)

    def full(*shape):
        return pltpu.VMEM(shape, F32)

    return pl.pallas_call(
        whole_kernel,
        out_shape=jax.ShapeDtypeStruct((3, DEPTH, TILE_Y, TILE_X), F32),
        in_specs=[smem] + [vmem] * 3 + [hbm] * 9,
        out_specs=vmem,
        scratch_shapes=[half(*w.shape) for w in weights]
        + [half(17, 768, 256)]
        + [half(size, 256) for size in (2048, 2048, 3072, 3072, 3072, 4096, 3072, 3072, 2048, 256)]
        + [
            half(8, 4, 32, 128),
            half(8, 4, 32, 128),
            half(2, 2, 4, 32, 128),
            full(3, 296, 256),
            full(20, 40, 128),
            half(18, 17, 16, 256),
            half(12, 6, 16, 128),
            half(20, 18, 16, 128),
            half(12, 10, 16, 256),
            half(10, 9, 16, 384),
            full(4, 128, 128),
            half(12, 8, 16, 128),
            half(16, 12, 16, 128),
            half(12, 8, 16, 384),
            half(10, 7, 16, 384),
            full(8, 96, 128),
            half(8, 12, 16, 256),
            half(16, 12, 16, 384),
            half(14, 11, 16, 384),
            half(12, 20, 16, 256),
            half(20, 18, 16, 256),
            half(18, 17, 16, 256),
            full(256, 128),
            full(256, 128),
            full(16, 32, 128),
            dma((9,)),
            dma((8,)),
            dma((8,)),
            dma((3,)),
            dma((3,)),
        ]
        + [dma((8,))] * 8,
        name="whole",
        compiler_params=pltpu.CompilerParams(
            vmem_limit_bytes=58 * MIB, collective_id=0, has_side_effects=True
        ),
        cost_estimate=pl.CostEstimate(flops=10**10, bytes_accessed=10**7, transcendentals=0),
    )(stretch_reader, raw_bricks.reshape(3, 4, 32, 128), affinity_head, w4, *weights)


def solution(mesh):
    placed = (P(("ty", "tx"), None, None, None),) + (P(),) * 12
    return jax.shard_map(
        per_device, mesh=mesh, in_specs=placed, out_specs=P(None, None, "ty", "tx"), check_vma=False
    )
```

```python
import jax
import jax.numpy as jnp
from jax import lax
from jax.experimental import pallas as pl
from jax.experimental.pallas import tpu as pltpu
from jax.sharding import PartitionSpec as P

TILE_Y = 16
TILE_X = 32
DEPTH = 32
BF16 = jnp.bfloat16
F32 = jnp.float32
MIB = 1 << 20


def iota(shape, dim):
    return lax.broadcasted_iota(jnp.int32, shape, dim)


def lane_block(shape, width):
    return lax.shift_right_logical(iota(shape, len(shape) - 1), width.bit_length() - 1)


def spread_blocks(w_ref, out_chans, out_dim=0):
    eye = (iota((out_chans, 128), 0) == iota((out_chans, 128), 1) % out_chans).astype(BF16)
    return [
        lax.dot_general(w_ref[t], eye, (((out_dim,), (0,)), ((), ())), preferred_element_type=F32)
        for t in range(27)
    ]


def tap(a, b, e):
    if 0 <= a <= 2 and 0 <= b <= 2 and 0 <= e <= 2:
        return 9 * a + 3 * b + e
    return None


def masked_sum(blocks, taps, width):
    shape = blocks[0].shape
    lanes = lane_block(shape, width)
    tile = jnp.zeros(shape, F32)
    for place, index in enumerate(taps):
        if index is not None:
            tile = jnp.where(lanes == place, blocks[index], tile)
    return tile


def build_fine(blocks, out_ref):
    for y in range(4):
        for j in range(2):
            for half in range(2):
                for px_in in range(2):
                    for slot in range(2):
                        z = (1 + slot) if half == 0 else (3, 0)[slot]
                        row = (y * 2 + j) * 256 + half * 128 + px_in * 64 + slot * 32
                        for py in range(2):
                            taps = [
                                tap(z - pz, y - py, 2 * j + px_in - px)
                                for px in range(2)
                                for pz in range(2)
                            ]
                            out_ref[row : row + 32, py * 128 : (py + 1) * 128] = masked_sum(
                                blocks, taps, 32
                            ).astype(BF16)


def build_middle(blocks, out_ref):
    for y in range(4):
        for j in range(2):
            for slot, dz in enumerate((1, 0, 2)):
                for px_in in range(2):
                    row = (y * 2 + j) * 384 + slot * 128 + px_in * 64
                    for py in range(2):
                        taps = [tap(dz, y - py, 2 * j + px_in - px) for px in range(2)]
                        out_ref[row : row + 64, py * 128 : (py + 1) * 128] = masked_sum(
                            blocks, taps, 64
                        ).astype(BF16)


def build_middle_open(blocks, out_ref):
    for y in range(4):
        for j in range(2):
            for px_in in range(2):
                for slot, dz in enumerate((1, 0, 2, 9)):
                    row = (y * 2 + j) * 256 + px_in * 128 + slot * 32
                    for py in range(2):
                        taps = [tap(dz, y - py, 2 * j + px_in - px) for px in range(2)]
                        out_ref[row : row + 32, py * 128 : (py + 1) * 128] = masked_sum(
                            blocks, taps, 64
                        ).astype(BF16)


def build_up(zcombined, out_ref, row0):
    shape = (64, 128)
    odd = lane_block(shape, 64) == 1
    for slot in range(4):
        for xc in range(2):
            rows = None
            if slot < 3:
                rows = []
                for dy in range(3):
                    t = zcombined[slot][dy]
                    if xc == 0:
                        rows.append(jnp.where(odd, t[0], t[0] + t[1]))
                    else:
                        rows.append(jnp.where(odd, t[1] + t[2], t[2]))
            for yc in range(2):
                row = row0 + (yc * 2 + xc) * 256 + slot * 64
                for py in range(2):
                    if rows is None:
                        tile = jnp.zeros(shape, F32)
                    elif (py, yc) == (0, 0):
                        tile = rows[0] + rows[1]
                    elif (py, yc) == (0, 1):
                        tile = rows[2]
                    elif (py, yc) == (1, 0):
                        tile = rows[0]
                    else:
                        tile = rows[1] + rows[2]
                    out_ref[row : row + 64, py * 128 : (py + 1) * 128] = tile.astype(BF16)


def build_open(w_ref, base_ref, out_ref):
    base_ref[...] = jnp.zeros_like(base_ref)
    eye = (iota((32, 128), 0) == iota((32, 128), 1) % 32).astype(BF16)
    rows = []
    for t in range(9):
        three = jnp.dot(w_ref[t], eye, preferred_element_type=F32)
        rows += [three[dx : dx + 1] for dx in range(3)]
    for dy in range(3):
        for z in range(6):
            for x in range(4):
                row = 40 + z // 3 * 128 + z % 3 * 40 + x
                for half in range(2):
                    taps = []
                    for px in range(2):
                        for p in range(2):
                            z_out = p if half == 0 else (2, -1)[p]
                            taps.append(tap(z - 1 - z_out, dy, x - px))
                    base_ref[dy, row : row + 1, 128 * half : 128 * half + 128] = masked_sum(
                        rows, taps, 32
                    )
    for xp in range(17):
        for dy in range(3):
            out_ref[xp, 256 * dy : 256 * dy + 256] = base_ref[
                dy, 40 - 2 * xp : 296 - 2 * xp
            ].astype(BF16)


def build_middle_merge(w_ref, out_ref):
    both = spread_blocks(w_ref, 64)
    build_middle([block[64:128] for block in both], out_ref)
    up = [block[:64] for block in both]
    grid = [[[up[9 * dz + 3 * dy + dx] for dx in range(3)] for dy in range(3)] for dz in (1, 0, 2)]
    build_up(grid, out_ref, 3072)


def build_fine_merge(w_ref, out_ref):
    both = spread_blocks(w_ref, 32)
    build_fine([block[64:96] for block in both], out_ref)
    up = [block[:64] for block in both]
    odd_z = lane_block((64, 128), 32) % 2 == 1

    def zmix(slot, dy, dx):
        w0, w1, w2 = (up[9 * a + 3 * dy + dx] for a in range(3))
        if slot == 0:
            return jnp.where(odd_z, w0 + w1, w1 + w2)
        if slot == 1:
            return jnp.where(odd_z, 0.0, w0)
        return jnp.where(odd_z, w2, 0.0)

    grid = [[[zmix(slot, dy, dx) for dx in range(3)] for dy in range(3)] for slot in range(3)]
    build_up(grid, out_ref, 2048)


def build_head(head_ref, out_ref):
    column = iota((256, 32), 0) % 128 // 32
    picked = jnp.zeros((256, 32), F32)
    for c in range(3):
        picked = jnp.where(column == c, head_ref[c : c + 1, :].astype(F32), picked)
    eye = (iota((256, 32), 0) % 32 == iota((256, 32), 1)).astype(BF16)
    full = lax.dot_general(
        eye, picked.astype(BF16), (((1,), (1,)), ((), ())), preferred_element_type=F32
    )
    row, col = iota((256, 256), 0), iota((256, 256), 1)
    fits = (row // 64 % 2 == col // 128) & (row // 32 % 2 == col // 16 % 2)
    fits = fits & (row // 128 == col % 16) & (col % 128 < 96)
    out_ref[...] = jnp.where(fits, full, 0.0).astype(BF16)


class Masks:
    def __init__(self):
        row, lane = iota((16, 128), 0), iota((16, 128), 1)

        def factor(where):
            return jnp.where(where, 1.0, 0.0).astype(F32)

        first, last = row > 0, row < 15
        odd = (lane & 32) != 0
        self.below, self.above = factor(first), factor(last)
        self.ends_below, self.ends_above = factor(odd & first), factor(~odd & last)
        self.low, self.high_below = factor(lane < 64), factor((lane >= 64) & first)
        self.px = [factor(lane < 64), factor(lane >= 64)]
        self.coarse_z = factor(row < 8)
        block = lane >> 5
        self.block = [factor(block == 0), factor((block == 1) & first), factor((block == 2) & last)]


def scaled(x, factor):
    return as_rows(as_blocks(x) * factor[None])


def row_below(x):
    return pltpu.roll(x, 1, 0)


def row_above(x):
    return pltpu.roll(x, x.shape[0] - 1, 0)


def as_rows(x):
    return x.reshape(x.shape[0] * 16, x.shape[2])


def as_blocks(x):
    return x.reshape(x.shape[0] // 16, 16, x.shape[1])


def up_window(src, yg, shift, groups):
    y, x = yg + shift, shift
    return [as_rows(src[y + yc, x + xc : x + xc + groups]) for yc in range(2) for xc in range(2)]


def window(src, yg, groups, up=None):
    pieces = [as_rows(src[2 * yg + y, j : j + groups]) for y in range(4) for j in range(2)]
    if up is not None:
        pieces += up_window(up, yg, 0, groups)
    return jnp.concatenate(pieces, axis=1)


def conv(src, w_ref, yg, groups):
    lhs = window(src, yg, groups)
    return jnp.dot(lhs, w_ref[...], preferred_element_type=F32)


def conv_all(src, w_ref, lines, groups, up=None):
    lhs = jnp.concatenate([window(src, yg, groups, up) for yg in range(lines)], axis=0)
    acc = jnp.dot(lhs, w_ref[...], preferred_element_type=F32)
    rows = groups * 16
    return [acc[yg * rows : (yg + 1) * rows] for yg in range(lines)]


def store_fine(ref, y, tile, m):
    ends = scaled(row_below(tile), m.ends_below) + scaled(row_above(tile), m.ends_above)
    ref[y, :, :, 0:128] = as_blocks(tile.astype(BF16))
    ref[y, :, :, 128:256] = as_blocks(ends.astype(BF16))


def store_middle(ref, y, tile, m):
    ref[y, :, :, 0:128] = as_blocks(tile.astype(BF16))
    ref[y, :, :, 128:256] = as_blocks(scaled(row_below(tile), m.below).astype(BF16))
    ref[y, :, :, 256:384] = as_blocks(scaled(row_above(tile), m.above).astype(BF16))


def store_single(ref, y, tile, m):
    below, above = row_below(tile), scaled(row_above(tile), m.above)
    near = [
        scaled(tile, m.low) + scaled(pltpu.roll(below, 64, 1), m.high_below),
        scaled(pltpu.roll(tile, 64, 1), m.low) + scaled(below, m.high_below),
    ]
    far = [above, pltpu.roll(above, 64, 1)]
    for px in range(2):
        a, b = as_blocks(near[px].astype(BF16)), as_blocks(far[px].astype(BF16))
        for xg in range(tile.shape[0] // 16):
            ref[y, 2 * xg + px, :, 0:128] = a[xg]
            ref[y, 2 * xg + px, :, 128:256] = b[xg]


def clear_outside(ref, lines, places, ty, tx, m, split=False):
    count = ref.shape[1]
    parts = ref.shape[3] // 128

    def halve(place, px):
        factor = jnp.concatenate([m.px[px]] * parts, axis=1).astype(BF16)
        ref[:, place] = ref[:, place] * factor[None]

    @pl.when(ty == 0)
    def _():
        ref[0:lines] = jnp.zeros((lines,) + ref.shape[1:], BF16)

    @pl.when(ty == 15)
    def _():
        ref[ref.shape[0] - lines :] = jnp.zeros((lines,) + ref.shape[1:], BF16)

    @pl.when(tx == 0)
    def _():
        if places:
            ref[:, 0:places] = jnp.zeros((ref.shape[0], places) + ref.shape[2:], BF16)
        if split:
            halve(places, 1)

    @pl.when(tx == 7)
    def _():
        if places:
            ref[:, count - places :] = jnp.zeros((ref.shape[0], places) + ref.shape[2:], BF16)
        if split:
            halve(count - 1 - places, 0)


def loop(count, body, unroll=1):
    def step(i, carry):
        body(i)
        return carry

    lax.fori_loop(0, count, step, 0, unroll=unroll)


def each(parts, body):
    for i, part in enumerate(parts):
        body(i, part)


AROUND = [(-1, 0), (1, 0), (-1, -1), (-1, 1), (1, -1), (1, 1), (0, -1), (0, 1)]
ALONG_TY, ALONG_TX = range(6), range(6, 8)


def span(step, core, width):
    if step == 0:
        return width, width, core
    if step > 0:
        return core, 0, width
    return width, core + width, width


def exchange(ref, widths, send_sems, recv_sems, ty, tx, directions=range(8)):
    copies = []
    for i in directions:
        dy, dx = AROUND[i]
        sy, ly, ny = span(dy, ref.shape[0] - 2 * widths[0], widths[0])
        sx, lx, nx = span(dx, ref.shape[1] - 2 * widths[1], widths[1])
        copy = pltpu.make_async_remote_copy(
            src_ref=ref.at[pl.ds(sy, ny), pl.ds(sx, nx)],
            dst_ref=ref.at[pl.ds(ly, ny), pl.ds(lx, nx)],
            send_sem=send_sems.at[i],
            recv_sem=recv_sems.at[i],
            device_id=((ty + dy + 16) % 16, (tx + dx + 8) % 8),
            device_id_type=pl.DeviceIdType.MESH,
        )
        copy.start()
        copies.append(copy)
    return copies


def finish(copies):
    for copy in copies:
        copy.wait()


def whole_kernel(
    readers, raw, head, fo, fs, mo, ms, co, cs, mm, mf, fm, ff,
    out,
    r_fs, r_mo, r_ms, r_co, r_cs, r_mm, r_mf, r_fm, r_ff,
    w_fo, w_fs, w_mo, w_ms, w_co, w_cs, w_mm, w_mf, w_fm, w_ff, w_head,
    outgoing, arrived, held,
    base_ref, z_ref, a_ref,
    quads, skip, in_ref, b_ref, s_ref,
    coarse, middle, ci_ref, co_ref, s2_ref, u1_ref, mi_ref, mm_ref, u2_ref, fi_ref, fm_ref,
    part_ref, last_ref, first_ref, second_ref, turn_ref, bricks_ref,
    load_sems, row_send, row_recv, near_send, near_recv,
    quad_send, quad_recv, skip_send, skip_recv, coarse_send, coarse_recv, middle_send, middle_recv,
):
    ty, tx = lax.axis_index("ty"), lax.axis_index("tx")
    m = Masks()
    mesh_id = pl.DeviceIdType.MESH
    loads = [
        pltpu.make_async_copy(source, target, load_sems.at[i])
        for i, (source, target) in enumerate(
            zip((fs, mo, ms, co, cs, mm, mf, fm, ff), (r_fs, r_mo, r_ms, r_co, r_cs, r_mm, r_mf, r_fm, r_ff))
        )
    ]
    for load in loads:
        load.start()

    barrier = pltpu.get_barrier_semaphore()
    greeted = [(ty, (tx + d) % 8) for d in range(1, 8)]
    greeted += [((ty + dy + 16) % 16, (tx + dx + 8) % 8) for dy in (-1, 1) for dx in (-1, 0, 1)]
    for device in greeted:
        pl.semaphore_signal(barrier, inc=1, device_id=device, device_id_type=mesh_id)
    for slot in range(3):
        for z in range(32):
            bricks_ref[slot, pl.ds(z, 4, stride=32), :] = raw[
                slot, :, 128 * z : 128 * z + 128
            ].astype(F32)

    pl.semaphore_wait(barrier, len(greeted))

    reader = [readers[ty * 8 + c] for c in range(8)]
    for c in range(8):
        rank = 0
        for earlier in range(c):
            rank += (reader[earlier] == reader[c]).astype(jnp.int32)
        outgoing[c] = bricks_ref[jnp.minimum(rank, 2)].astype(BF16).reshape(4, 32, 128)
    copies = []
    for d in range(1, 8):
        peer = (tx + d) % 8
        copy = pltpu.make_async_remote_copy(
            src_ref=outgoing.at[peer],
            dst_ref=arrived.at[tx],
            send_sem=row_send.at[d],
            recv_sem=row_recv.at[d],
            device_id=(ty, peer),
            device_id_type=mesh_id,
        )
        copy.start()
        copies.append(copy)
    arrived[tx] = outgoing[tx]
    build_open(fo, base_ref, w_fo)
    loads[0].wait()
    build_fine(spread_blocks(r_fs, 32), w_fs)
    finish(copies)
    own = readers[ty * 8 + tx] % 8
    held[1, 1] = arrived[own]
    copies = []
    for i, (dy, dx) in enumerate([(0, 1), (1, 0), (1, 1)]):
        copy = pltpu.make_async_remote_copy(
            src_ref=held.at[1, 1],
            dst_ref=held.at[1 - dy, 1 - dx],
            send_sem=near_send.at[i],
            recv_sem=near_recv.at[i],
            device_id=((ty + dy) % 16, (tx + dx) % 8),
            device_id_type=mesh_id,
        )
        copy.start()
        copies.append(copy)
    loads[1].wait()
    build_middle_open(spread_blocks(r_mo, 64, 1), w_mo)
    build_head(head, w_head)
    loads[2].wait()
    build_middle(spread_blocks(r_ms, 64), w_ms)
    loads[3].wait()
    build_middle(spread_blocks(r_co, 64), w_co)
    finish(copies)

    z_ref[:, 0:8] = jnp.zeros((20, 8, 128), F32)
    z_ref[:, 32:40] = jnp.zeros((20, 8, 128), F32)
    lane = iota((32, 128), 1)
    lines = []
    for br in range(4):
        bricks = []
        for bc in range(4):
            brick = held[br // 2, bc // 2, br % 2 * 2 + bc % 2].astype(F32)
            ok = True
            if br == 0:
                ok = ty > 0
            if br == 3:
                ok = ty < 15
            if bc == 0:
                ok = (tx > 0) & ok
            if bc == 3:
                ok = (tx < 7) & ok
            if ok is not True:
                brick = jnp.where(ok, brick, 0.0)
            bricks.append(brick)
        for r in ((6, 7), range(8), range(8), (0, 1))[br]:
            y = 8 * br + r - 6
            line = jnp.where(lane < 36, pltpu.roll(bricks[3], (34 - 16 * r) % 128, 1), 0.0)
            line = jnp.where(lane < 34, pltpu.roll(bricks[2], (18 - 16 * r) % 128, 1), line)
            line = jnp.where(lane < 18, pltpu.roll(bricks[1], (2 - 16 * r) % 128, 1), line)
            line = jnp.where(lane < 2, pltpu.roll(bricks[0], (-14 - 16 * r) % 128, 1), line)
            z_ref[y, 4:36, :] = line
            parts = [z_ref[y, pl.ds(2 + z, 16, stride=2), :] for z in range(6)]
            for t in range(2):
                tile = parts[3 * t]
                for i in (1, 2):
                    tile = tile + pltpu.roll(parts[3 * t + i], 40 * i, 1)
                parts[t] = tile
            lines.append(jnp.concatenate(parts[:2], axis=1).astype(BF16))
    lhs = jnp.concatenate(
        [jnp.concatenate(lines[dy : dy + 18], axis=0) for dy in range(3)], axis=1
    )
    ends = m.ends_below + m.ends_above
    for xp in range(17):
        acc = jnp.maximum(jnp.dot(lhs, w_fo[xp], preferred_element_type=F32), 0.0)
        a_ref[:, xp, :, 0:128] = as_blocks(acc[:, :128].astype(BF16))
        a_ref[:, xp, :, 128:256] = as_blocks(scaled(acc[:, 128:], ends).astype(BF16))
    clear_outside(a_ref, 1, 0, ty, tx, m, split=True)
    quad_lane = lane_block((4, 16, 128), 32)

    def second(yg):
        acc = jnp.maximum(conv(a_ref, w_fs, yg, 16), 0.0)
        skip[2 + 2 * yg, 1:17] = as_blocks(acc[:, :128].astype(BF16))
        skip[3 + 2 * yg, 1:17] = as_blocks(acc[:, 128:].astype(BF16))
        top = jnp.maximum(acc[:, :128], acc[:, 128:])
        top = jnp.maximum(top, pltpu.roll(top, 64, 1))
        top = jnp.maximum(top, pltpu.roll(top, 32, 1)).reshape(4, 4, 16, 128)
        quad = top[:, 0]
        for q in range(1, 4):
            quad = jnp.where(quad_lane == q, top[:, q], quad)
        quads[2 + yg, 1:5] = quad.astype(BF16)

    for yg in (0, 1, 6, 7):
        second(yg)
    copies = exchange(quads, (2, 1), quad_send, quad_recv, ty, tx, ALONG_TY)
    skip_copies = exchange(skip, (2, 1), skip_send, skip_recv, ty, tx, ALONG_TY)
    for yg in range(2, 6):
        second(yg)
    copies += exchange(quads, (2, 1), quad_send, quad_recv, ty, tx, ALONG_TX)
    skip_copies += exchange(skip, (2, 1), skip_send, skip_recv, ty, tx, ALONG_TX)
    loads[4].wait()
    build_middle(spread_blocks(r_cs, 64), w_cs)
    loads[5].wait()
    build_middle_merge(r_mm, w_mm)
    loads[6].wait()
    build_middle(spread_blocks(r_mf, 64), w_mf)
    loads[7].wait()
    build_fine_merge(r_fm, w_fm)
    loads[8].wait()
    build_fine(spread_blocks(r_ff, 32), w_ff)
    finish(copies)

    clear_outside(quads, 2, 1, ty, tx, m)

    def spread(y):
        c = as_rows(quads[y]).astype(F32)
        below, above = row_below(c), row_above(c)
        for q in range(4):
            tile = scaled(pltpu.roll(c, (-32 * q) % 128, 1), m.block[0])
            tile = tile + scaled(pltpu.roll(below, (32 - 32 * q) % 128, 1), m.block[1])
            tile = tile + scaled(pltpu.roll(above, (64 - 32 * q) % 128, 1), m.block[2])
            blocks = as_blocks(tile.astype(BF16))
            lane = 128 * (q % 2)
            for quad in range(6):
                place = 2 * quad - 1 + q // 2
                if 0 <= place < 10:
                    in_ref[y, place, :, lane : lane + 128] = blocks[quad]

    loop(12, spread, 3)

    def middle_open(yg, acc):
        for py in range(2):
            tile = jnp.maximum(acc[:, 128 * py : 128 * py + 128], 0.0)
            store_middle(b_ref, 2 * yg + py, tile, m)

    each(conv_all(in_ref, w_mo, 5, 9), middle_open)
    clear_outside(b_ref, 1, 0, ty, tx, m, split=True)
    low = lane_block((4, 8, 128), 64) == 0

    def middle_second(yg, acc):
        acc = jnp.maximum(acc, 0.0)
        middle[4 + 2 * yg, 2:10] = as_blocks(acc[:, :128].astype(BF16))
        middle[5 + 2 * yg, 2:10] = as_blocks(acc[:, 128:].astype(BF16))
        top = jnp.maximum(acc[:, :128], acc[:, 128:])
        top = jnp.maximum(top, pltpu.roll(top, 64, 1))
        s_ref[yg] = jnp.maximum(top, row_above(top))
        some = s_ref[yg, pl.ds(0, 64, stride=2), :].reshape(4, 2, 8, 128)
        pair = jnp.where(low, some[:, 0], some[:, 1])
        coarse[4 + yg, 1:3] = pair.reshape(2, 16, 128).astype(BF16)

    each(conv_all(b_ref, w_ms, 4, 8), middle_second)
    copies = exchange(coarse, (4, 1), coarse_send, coarse_recv, ty, tx)
    middle_copies = exchange(middle, (4, 2), middle_send, middle_recv, ty, tx)

    finish(skip_copies)
    clear_outside(skip, 2, 1, ty, tx, m)

    def fine_in(y):
        x = as_rows(skip[y]).astype(F32)
        store_fine(fi_ref, y, x, m)

    loop(20, fine_in, 2)
    for yg in range(9):
        part_ref[yg] = jnp.dot(
            window(fi_ref, yg, 17), w_fm[0:2048], preferred_element_type=F32
        )
    finish(copies)

    clear_outside(coarse, 4, 1, ty, tx, m)

    def coarse_in(y):
        x = coarse[y].astype(F32).reshape(8, 8, 128)
        x = as_rows(jnp.concatenate([x, jnp.zeros_like(x)], axis=1))
        store_middle(ci_ref, y, x, m)

    loop(12, coarse_in)

    def coarse_open(yg, acc):
        for py in range(2):
            tile = jnp.maximum(acc[:, 128 * py : 128 * py + 128], 0.0)
            tile = scaled(tile, m.coarse_z)
            store_middle(co_ref, 2 * yg + py, tile, m)

    each(conv_all(ci_ref, w_co, 5, 7), coarse_open)
    clear_outside(co_ref, 3, 1, ty, tx, m, split=True)

    def coarse_second(yg, acc):
        for py in range(2):
            tile = jnp.maximum(acc[:, 128 * py : 128 * py + 128], 0.0)
            half = tile.reshape(6, 16, 128)[:, :8].reshape(48, 128)
            s2_ref[2 * yg + py, pl.ds(0, 48, stride=2), :] = half
            s2_ref[2 * yg + py, pl.ds(1, 48, stride=2), :] = half
            store_single(u1_ref, 2 * yg + py, s2_ref[2 * yg + py], m)

    each(conv_all(co_ref, w_cs, 4, 6), coarse_second)
    clear_outside(u1_ref, 2, 2, ty, tx, m)
    finish(middle_copies)
    clear_outside(middle, 4, 2, ty, tx, m)

    def middle_in(y):
        x = as_rows(middle[y]).astype(F32)
        store_middle(mi_ref, y, x, m)

    loop(16, middle_in)

    def middle_merge(yg, acc):
        for py in range(2):
            tile = jnp.maximum(acc[:, 128 * py : 128 * py + 128], 0.0)
            store_middle(mm_ref, 2 * yg + py, tile, m)

    each(conv_all(mi_ref, w_mm, 7, 11, u1_ref), middle_merge)
    clear_outside(mm_ref, 3, 1, ty, tx, m, split=True)

    def middle_final(yg, acc):
        for py in range(2):
            tile = jnp.maximum(acc[:, 128 * py : 128 * py + 128], 0.0)
            store_single(u2_ref, 2 * yg + py, tile, m)

    each(conv_all(mm_ref, w_mf, 6, 10), middle_final)
    clear_outside(u2_ref, 2, 2, ty, tx, m)


    def fine_merge(yg):
        acc = part_ref[yg] + jnp.dot(
            jnp.concatenate(up_window(u2_ref, yg, 1, 17), axis=1),
            w_fm[2048:3072],
            preferred_element_type=F32,
        )
        for py in range(2):
            tile = jnp.maximum(acc[:, 128 * py : 128 * py + 128], 0.0)
            store_fine(fm_ref, 2 * yg + py, tile, m)

    for yg in range(9):
        fine_merge(yg)
    clear_outside(fm_ref, 1, 0, ty, tx, m, split=True)

    def fine_final(yg):
        last_ref[yg] = jnp.maximum(conv(fm_ref, w_ff, yg, 16), 0.0).astype(BF16)

    for yg in range(8):
        fine_final(yg)
    totals = [None, None]
    for yg in range(8):
        logits = jnp.dot(last_ref[yg], w_head[...], preferred_element_type=F32)
        for px in range(2):
            part = logits[:, 128 * px : 128 * px + 128]
            totals[px] = part if yg == 0 else totals[px] + pltpu.roll(part, 2 * yg, 1)
    first_ref[...] = totals[0]
    second_ref[...] = totals[1]

    def finished(k):
        turn_ref[k, pl.ds(0, 16, stride=2), :] = first_ref[pl.ds(k, 16, stride=16), :]
        turn_ref[k, pl.ds(1, 16, stride=2), :] = second_ref[pl.ds(k, 16, stride=16), :]
        turned = turn_ref[k].T
        for c in range(3):
            for pz in range(2):
                row = 32 * c + 16 * pz
                out[c, 2 * k + pz] = turned[row : row + 16]

    for k in range(16):
        finished(k)


def per_device(
    raw_bricks,
    stretch_reader,
    fine_open,
    fine_second,
    middle_open,
    middle_second,
    coarse_open,
    coarse_second,
    middle_merge,
    middle_final,
    fine_merge,
    fine_final,
    affinity_head,
):
    def flat(w):
        return w.reshape(27, w.shape[3], w.shape[4])

    weights = [
        flat(fine_second),
        flat(middle_open.transpose(0, 1, 2, 4, 3)),
        flat(middle_second),
        flat(coarse_open),
        flat(coarse_second),
        flat(middle_merge),
        flat(middle_final),
        flat(fine_merge),
        flat(fine_final),
    ]
    opening = fine_open.transpose(0, 1, 4, 2, 3).reshape(9, 3, 32)
    vmem = pl.BlockSpec(memory_space=pltpu.VMEM)
    smem = pl.BlockSpec(memory_space=pltpu.SMEM)
    hbm = pl.BlockSpec(memory_space=pl.ANY)
    dma = pltpu.SemaphoreType.DMA

    def half(*shape):
        return pltpu.VMEM(shape, BF16)

    def full(*shape):
        return pltpu.VMEM(shape, F32)

    return pl.pallas_call(
        whole_kernel,
        out_shape=jax.ShapeDtypeStruct((3, DEPTH, TILE_Y, TILE_X), F32),
        in_specs=[smem] + [vmem] * 3 + [hbm] * 9,
        out_specs=vmem,
        scratch_shapes=[half(*w.shape) for w in weights]
        + [half(17, 768, 256)]
        + [half(size, 256) for size in (2048, 2048, 3072, 3072, 3072, 4096, 3072, 3072, 2048, 256)]
        + [
            half(8, 4, 32, 128),
            half(8, 4, 32, 128),
            half(2, 2, 4, 32, 128),
            full(3, 296, 256),
            full(20, 40, 128),
            half(18, 17, 16, 256),
            half(12, 6, 16, 128),
            half(20, 18, 16, 128),
            half(12, 10, 16, 256),
            half(10, 9, 16, 384),
            full(4, 128, 128),
            half(12, 4, 16, 128),
            half(16, 12, 16, 128),
            half(12, 8, 16, 384),
            half(10, 7, 16, 384),
            full(8, 96, 128),
            half(8, 12, 16, 256),
            half(16, 12, 16, 384),
            half(14, 11, 16, 384),
            half(12, 20, 16, 256),
            half(20, 18, 16, 256),
            half(18, 17, 16, 256),
            full(9, 272, 256),
            half(8, 256, 256),
            full(256, 128),
            full(256, 128),
            full(16, 32, 128),
            full(3, 128, 128),
            dma((9,)),
            dma((8,)),
            dma((8,)),
            dma((3,)),
            dma((3,)),
        ]
        + [dma((8,))] * 8,
        name="whole",
        compiler_params=pltpu.CompilerParams(
            vmem_limit_bytes=58 * MIB, collective_id=0, has_side_effects=True
        ),
        cost_estimate=pl.CostEstimate(flops=10**10, bytes_accessed=10**7, transcendentals=0),
    )(stretch_reader, raw_bricks[0], affinity_head, opening, *weights)


def solution(mesh):
    placed = (P(("ty", "tx"), None, None, None),) + (P(),) * 12
    return jax.shard_map(
        per_device, mesh=mesh, in_specs=placed, out_specs=P(None, None, "ty", "tx"), check_vma=False
    )
```

```python
import jax
import jax.numpy as jnp
from jax import lax
from jax.experimental import pallas as pl
from jax.experimental.pallas import tpu as pltpu
from jax.sharding import PartitionSpec as P

TILE_Y = 16
TILE_X = 32
DEPTH = 32
BF16 = jnp.bfloat16
F32 = jnp.float32
MIB = 1 << 20


def iota(shape, dim):
    return lax.broadcasted_iota(jnp.int32, shape, dim)


def lane_block(shape, width):
    return lax.shift_right_logical(iota(shape, len(shape) - 1), width.bit_length() - 1)


def spread_blocks(w_ref, out_chans, out_dim=0):
    eye = (iota((out_chans, 128), 0) == iota((out_chans, 128), 1) % out_chans).astype(BF16)
    return [
        lax.dot_general(w_ref[t], eye, (((out_dim,), (0,)), ((), ())), preferred_element_type=F32)
        for t in range(27)
    ]


def tap(a, b, e):
    if 0 <= a <= 2 and 0 <= b <= 2 and 0 <= e <= 2:
        return 9 * a + 3 * b + e
    return None


def masked_sum(blocks, taps, width):
    shape = blocks[0].shape
    lanes = lane_block(shape, width)
    tile = jnp.zeros(shape, F32)
    for place, index in enumerate(taps):
        if index is not None:
            tile = jnp.where(lanes == place, blocks[index], tile)
    return tile


def build_fine(blocks, out_ref):
    for y in range(4):
        for j in range(2):
            for half in range(2):
                for px_in in range(2):
                    for slot in range(2):
                        z = (1 + slot) if half == 0 else (3, 0)[slot]
                        row = (y * 2 + j) * 256 + half * 128 + px_in * 64 + slot * 32
                        for py in range(2):
                            taps = [
                                tap(z - pz, y - py, 2 * j + px_in - px)
                                for px in range(2)
                                for pz in range(2)
                            ]
                            out_ref[row : row + 32, py * 128 : (py + 1) * 128] = masked_sum(
                                blocks, taps, 32
                            ).astype(BF16)


def build_middle(blocks, out_ref):
    for y in range(4):
        for j in range(2):
            for slot, dz in enumerate((1, 0, 2)):
                for px_in in range(2):
                    row = (y * 2 + j) * 384 + slot * 128 + px_in * 64
                    for py in range(2):
                        taps = [tap(dz, y - py, 2 * j + px_in - px) for px in range(2)]
                        out_ref[row : row + 64, py * 128 : (py + 1) * 128] = masked_sum(
                            blocks, taps, 64
                        ).astype(BF16)


def build_middle_open(blocks, out_ref):
    for y in range(4):
        for j in range(2):
            for px_in in range(2):
                for slot, dz in enumerate((1, 0, 2, 9)):
                    row = (y * 2 + j) * 256 + px_in * 128 + slot * 32
                    for py in range(2):
                        taps = [tap(dz, y - py, 2 * j + px_in - px) for px in range(2)]
                        out_ref[row : row + 32, py * 128 : (py + 1) * 128] = masked_sum(
                            blocks, taps, 64
                        ).astype(BF16)


def build_up(zcombined, out_ref, row0):
    shape = (64, 128)
    odd = lane_block(shape, 64) == 1
    for slot in range(4):
        for xc in range(2):
            rows = None
            if slot < 3:
                rows = []
                for dy in range(3):
                    t = zcombined[slot][dy]
                    if xc == 0:
                        rows.append(jnp.where(odd, t[0], t[0] + t[1]))
                    else:
                        rows.append(jnp.where(odd, t[1] + t[2], t[2]))
            for yc in range(2):
                row = row0 + (yc * 2 + xc) * 256 + slot * 64
                for py in range(2):
                    if rows is None:
                        tile = jnp.zeros(shape, F32)
                    elif (py, yc) == (0, 0):
                        tile = rows[0] + rows[1]
                    elif (py, yc) == (0, 1):
                        tile = rows[2]
                    elif (py, yc) == (1, 0):
                        tile = rows[0]
                    else:
                        tile = rows[1] + rows[2]
                    out_ref[row : row + 64, py * 128 : (py + 1) * 128] = tile.astype(BF16)


def build_open(w_ref, base_ref, out_ref):
    base_ref[...] = jnp.zeros_like(base_ref)
    eye = (iota((32, 128), 0) == iota((32, 128), 1) % 32).astype(BF16)
    rows = []
    for t in range(9):
        three = jnp.dot(w_ref[t], eye, preferred_element_type=F32)
        rows += [three[dx : dx + 1] for dx in range(3)]
    for dy in range(3):
        for z in range(6):
            for x in range(4):
                row = 40 + z // 3 * 128 + z % 3 * 40 + x
                for half in range(2):
                    taps = []
                    for px in range(2):
                        for p in range(2):
                            z_out = p if half == 0 else (2, -1)[p]
                            taps.append(tap(z - 1 - z_out, dy, x - px))
                    base_ref[dy, row : row + 1, 128 * half : 128 * half + 128] = masked_sum(
                        rows, taps, 32
                    )
    for xp in range(17):
        for dy in range(3):
            out_ref[xp, 256 * dy : 256 * dy + 256] = base_ref[
                dy, 40 - 2 * xp : 296 - 2 * xp
            ].astype(BF16)


def build_middle_merge(w_ref, out_ref):
    both = spread_blocks(w_ref, 64)
    build_middle([block[64:128] for block in both], out_ref)
    up = [block[:64] for block in both]
    grid = [[[up[9 * dz + 3 * dy + dx] for dx in range(3)] for dy in range(3)] for dz in (1, 0, 2)]
    build_up(grid, out_ref, 3072)


def build_fine_merge(w_ref, out_ref):
    both = spread_blocks(w_ref, 32)
    build_fine([block[64:96] for block in both], out_ref)
    up = [block[:64] for block in both]
    odd_z = lane_block((64, 128), 32) % 2 == 1

    def zmix(slot, dy, dx):
        w0, w1, w2 = (up[9 * a + 3 * dy + dx] for a in range(3))
        if slot == 0:
            return jnp.where(odd_z, w0 + w1, w1 + w2)
        if slot == 1:
            return jnp.where(odd_z, 0.0, w0)
        return jnp.where(odd_z, w2, 0.0)

    grid = [[[zmix(slot, dy, dx) for dx in range(3)] for dy in range(3)] for slot in range(3)]
    build_up(grid, out_ref, 2048)


def build_head(head_ref, out_ref):
    column = iota((256, 32), 0) % 128 // 32
    picked = jnp.zeros((256, 32), F32)
    for c in range(3):
        picked = jnp.where(column == c, head_ref[c : c + 1, :].astype(F32), picked)
    eye = (iota((256, 32), 0) % 32 == iota((256, 32), 1)).astype(BF16)
    full = lax.dot_general(
        eye, picked.astype(BF16), (((1,), (1,)), ((), ())), preferred_element_type=F32
    )
    row, col = iota((256, 256), 0), iota((256, 256), 1)
    fits = (row // 64 % 2 == col // 128) & (row // 32 % 2 == col // 16 % 2)
    fits = fits & (row // 128 == col % 16) & (col % 128 < 96)
    base = jnp.where(fits, full, 0.0)
    for yg in range(8):
        for px in range(2):
            part = base[:, 128 * px : 128 * px + 128]
            out_ref[256 * yg : 256 * yg + 256, 128 * px : 128 * px + 128] = pltpu.roll(
                part, 2 * yg, 1
            ).astype(BF16)


class Masks:
    def __init__(self):
        row, lane = iota((16, 128), 0), iota((16, 128), 1)

        def factor(where):
            return jnp.where(where, 1.0, 0.0).astype(F32)

        first, last = row > 0, row < 15
        odd = (lane & 32) != 0
        self.below, self.above = factor(first), factor(last)
        self.ends_below, self.ends_above = factor(odd & first), factor(~odd & last)
        self.low, self.high_below = factor(lane < 64), factor((lane >= 64) & first)
        self.px = [factor(lane < 64), factor(lane >= 64)]
        self.coarse_z = factor(row < 8)
        block = lane >> 5
        self.block = [factor(block == 0), factor((block == 1) & first), factor((block == 2) & last)]


def scaled(x, factor):
    return as_rows(as_blocks(x) * factor[None])


def row_below(x):
    return pltpu.roll(x, 1, 0)


def row_above(x):
    return pltpu.roll(x, x.shape[0] - 1, 0)


def as_rows(x):
    return x.reshape(x.shape[0] * 16, x.shape[2])


def as_blocks(x):
    return x.reshape(x.shape[0] // 16, 16, x.shape[1])


def up_window(src, yg, shift, groups):
    y, x = yg + shift, shift
    return [as_rows(src[y + yc, x + xc : x + xc + groups]) for yc in range(2) for xc in range(2)]


def window(src, yg, groups, up=None):
    pieces = [as_rows(src[2 * yg + y, j : j + groups]) for y in range(4) for j in range(2)]
    if up is not None:
        pieces += up_window(up, yg, 0, groups)
    return jnp.concatenate(pieces, axis=1)


def conv(src, w_ref, yg, groups):
    lhs = window(src, yg, groups)
    return jnp.dot(lhs, w_ref[...], preferred_element_type=F32)


def conv_lines(src, w_ref, counts, groups, body, up=None):
    first, rows = 0, groups * 16
    for count in counts:
        lines = range(first, first + count)
        lhs = jnp.concatenate([window(src, yg, groups, up) for yg in lines], axis=0)
        acc = jnp.dot(lhs, w_ref[...], preferred_element_type=F32)
        for i, yg in enumerate(lines):
            body(yg, acc[i * rows : (i + 1) * rows])
        first += count


def store_fine(ref, y, tile, m):
    ends = scaled(row_below(tile), m.ends_below) + scaled(row_above(tile), m.ends_above)
    ref[y, :, :, 0:128] = as_blocks(tile.astype(BF16))
    ref[y, :, :, 128:256] = as_blocks(ends.astype(BF16))


def store_middle(ref, y, tile, m):
    ref[y, :, :, 0:128] = as_blocks(tile.astype(BF16))
    ref[y, :, :, 128:256] = as_blocks(scaled(row_below(tile), m.below).astype(BF16))
    ref[y, :, :, 256:384] = as_blocks(scaled(row_above(tile), m.above).astype(BF16))


def store_single(ref, y, tile, m):
    below, above = row_below(tile), scaled(row_above(tile), m.above)
    near = [
        scaled(tile, m.low) + scaled(pltpu.roll(below, 64, 1), m.high_below),
        scaled(pltpu.roll(tile, 64, 1), m.low) + scaled(below, m.high_below),
    ]
    far = [above, pltpu.roll(above, 64, 1)]
    for px in range(2):
        a, b = as_blocks(near[px].astype(BF16)), as_blocks(far[px].astype(BF16))
        for xg in range(tile.shape[0] // 16):
            ref[y, 2 * xg + px, :, 0:128] = a[xg]
            ref[y, 2 * xg + px, :, 128:256] = b[xg]


def clear_outside(ref, lines, places, ty, tx, m, split=False):
    count = ref.shape[1]
    parts = ref.shape[3] // 128

    def halve(place, px):
        factor = jnp.concatenate([m.px[px]] * parts, axis=1).astype(BF16)
        ref[:, place] = ref[:, place] * factor[None]

    @pl.when(ty == 0)
    def _():
        ref[0:lines] = jnp.zeros((lines,) + ref.shape[1:], BF16)

    @pl.when(ty == 15)
    def _():
        ref[ref.shape[0] - lines :] = jnp.zeros((lines,) + ref.shape[1:], BF16)

    @pl.when(tx == 0)
    def _():
        if places:
            ref[:, 0:places] = jnp.zeros((ref.shape[0], places) + ref.shape[2:], BF16)
        if split:
            halve(places, 1)

    @pl.when(tx == 7)
    def _():
        if places:
            ref[:, count - places :] = jnp.zeros((ref.shape[0], places) + ref.shape[2:], BF16)
        if split:
            halve(count - 1 - places, 0)


def loop(count, body, unroll=1):
    def step(i, carry):
        body(i)
        return carry

    lax.fori_loop(0, count, step, 0, unroll=unroll)


AROUND = [(-1, 0), (1, 0), (-1, -1), (-1, 1), (1, -1), (1, 1), (0, -1), (0, 1)]
ALONG_TY, ALONG_TX = range(6), range(6, 8)


def span(step, core, width):
    if step == 0:
        return width, width, core
    if step > 0:
        return core, 0, width
    return width, core + width, width


def exchange(ref, widths, send_sems, recv_sems, ty, tx, directions=range(8)):
    copies = []
    for i in directions:
        dy, dx = AROUND[i]
        sy, ly, ny = span(dy, ref.shape[0] - 2 * widths[0], widths[0])
        sx, lx, nx = span(dx, ref.shape[1] - 2 * widths[1], widths[1])
        copy = pltpu.make_async_remote_copy(
            src_ref=ref.at[pl.ds(sy, ny), pl.ds(sx, nx)],
            dst_ref=ref.at[pl.ds(ly, ny), pl.ds(lx, nx)],
            send_sem=send_sems.at[i],
            recv_sem=recv_sems.at[i],
            device_id=((ty + dy + 16) % 16, (tx + dx + 8) % 8),
            device_id_type=pl.DeviceIdType.MESH,
        )
        sends, receives = neighbour(dy, dx, ty, tx), neighbour(-dy, -dx, ty, tx)
        pl.when(sends)(copy.start)
        copies.append((copy, sends, receives))
    return copies


def neighbour(dy, dx, ty, tx):
    there = [tx >= 0]
    if dy:
        there.append(ty < 15 if dy > 0 else ty > 0)
    if dx:
        there.append(tx < 7 if dx > 0 else tx > 0)
    return there[-1] if len(there) < 3 else there[1] & there[2]


def finish(copies):
    for copy, sends, receives in copies:
        pl.when(receives)(copy.wait_recv)
    for copy, sends, receives in copies:
        pl.when(sends)(copy.wait_send)


def whole_kernel(
    readers, raw, head, fo, fs, mo, ms, co, cs, mm, mf, fm, ff,
    out,
    r_fs, r_mo, r_ms, r_co, r_cs, r_mm, r_mf, r_fm, r_ff,
    w_fo, w_fs, w_mo, w_ms, w_co, w_cs, w_mm, w_mf, w_fm, w_ff, w_head,
    outgoing, arrived, held,
    base_ref, z_ref, a_ref,
    quads, skip, in_ref, b_ref, s_ref,
    coarse, middle, ci_ref, co_ref, s2_ref, u1_ref, mi_ref, mm_ref, u2_ref, fi_ref, fm_ref,
    part_ref, last_ref, first_ref, second_ref, turn_ref, bricks_ref,
    load_sems, row_send, row_recv, near_send, near_recv,
    quad_send, quad_recv, skip_send, skip_recv, coarse_send, coarse_recv, middle_send, middle_recv,
):
    ty, tx = lax.axis_index("ty"), lax.axis_index("tx")
    m = Masks()
    mesh_id = pl.DeviceIdType.MESH
    loads = [
        pltpu.make_async_copy(source, target, load_sems.at[i])
        for i, (source, target) in enumerate(
            zip((fs, mo, ms, co, cs, mm, mf, fm, ff), (r_fs, r_mo, r_ms, r_co, r_cs, r_mm, r_mf, r_fm, r_ff))
        )
    ]
    for load in loads:
        load.start()

    barrier = pltpu.get_barrier_semaphore()
    greeted = [(ty, (tx + d) % 8) for d in range(1, 8)]
    greeted += [((ty + dy + 16) % 16, (tx + dx + 8) % 8) for dy in (-1, 1) for dx in (-1, 0, 1)]
    for device in greeted:
        pl.semaphore_signal(barrier, inc=1, device_id=device, device_id_type=mesh_id)
    for slot in range(3):
        for z in range(32):
            bricks_ref[slot, pl.ds(z, 4, stride=32), :] = raw[
                slot, :, 128 * z : 128 * z + 128
            ].astype(F32)

    pl.semaphore_wait(barrier, len(greeted))

    reader = [readers[ty * 8 + c] for c in range(8)]
    for c in range(8):
        rank = 0
        for earlier in range(c):
            rank += (reader[earlier] == reader[c]).astype(jnp.int32)
        outgoing[c] = bricks_ref[jnp.minimum(rank, 2)].astype(BF16).reshape(4, 32, 128)
    copies = []
    for d in range(1, 8):
        peer = (tx + d) % 8
        copy = pltpu.make_async_remote_copy(
            src_ref=outgoing.at[peer],
            dst_ref=arrived.at[tx],
            send_sem=row_send.at[d],
            recv_sem=row_recv.at[d],
            device_id=(ty, peer),
            device_id_type=mesh_id,
        )
        copy.start()
        copies.append(copy)
    arrived[tx] = outgoing[tx]
    build_open(fo, base_ref, w_fo)
    loads[0].wait()
    build_fine(spread_blocks(r_fs, 32), w_fs)
    for copy in copies:
        copy.wait()
    own = readers[ty * 8 + tx] % 8
    held[1, 1] = arrived[own]
    copies = []
    for i, (dy, dx) in enumerate([(0, 1), (1, 0), (1, 1)]):
        copy = pltpu.make_async_remote_copy(
            src_ref=held.at[1, 1],
            dst_ref=held.at[1 - dy, 1 - dx],
            send_sem=near_send.at[i],
            recv_sem=near_recv.at[i],
            device_id=((ty + dy) % 16, (tx + dx) % 8),
            device_id_type=mesh_id,
        )
        copy.start()
        copies.append(copy)
    loads[1].wait()
    build_middle_open(spread_blocks(r_mo, 64, 1), w_mo)
    loads[2].wait()
    build_middle(spread_blocks(r_ms, 64), w_ms)
    loads[3].wait()
    build_middle(spread_blocks(r_co, 64), w_co)
    for copy in copies:
        copy.wait()

    z_ref[:, 0:8] = jnp.zeros((20, 8, 128), F32)
    z_ref[:, 32:40] = jnp.zeros((20, 8, 128), F32)
    lane = iota((32, 128), 1)
    lines = []
    for br in range(4):
        bricks = []
        for bc in range(4):
            brick = held[br // 2, bc // 2, br % 2 * 2 + bc % 2].astype(F32)
            ok = True
            if br == 0:
                ok = ty > 0
            if br == 3:
                ok = ty < 15
            if bc == 0:
                ok = (tx > 0) & ok
            if bc == 3:
                ok = (tx < 7) & ok
            if ok is not True:
                brick = jnp.where(ok, brick, 0.0)
            bricks.append(brick)
        for r in ((6, 7), range(8), range(8), (0, 1))[br]:
            y = 8 * br + r - 6
            line = jnp.where(lane < 36, pltpu.roll(bricks[3], (34 - 16 * r) % 128, 1), 0.0)
            line = jnp.where(lane < 34, pltpu.roll(bricks[2], (18 - 16 * r) % 128, 1), line)
            line = jnp.where(lane < 18, pltpu.roll(bricks[1], (2 - 16 * r) % 128, 1), line)
            line = jnp.where(lane < 2, pltpu.roll(bricks[0], (-14 - 16 * r) % 128, 1), line)
            z_ref[y, 4:36, :] = line
            parts = [z_ref[y, pl.ds(2 + z, 16, stride=2), :] for z in range(6)]
            for t in range(2):
                tile = parts[3 * t]
                for i in (1, 2):
                    tile = tile + pltpu.roll(parts[3 * t + i], 40 * i, 1)
                parts[t] = tile
            lines.append(jnp.concatenate(parts[:2], axis=1).astype(BF16))
    lhs = jnp.concatenate(
        [jnp.concatenate(lines[dy : dy + 18], axis=0) for dy in range(3)], axis=1
    )
    ends = m.ends_below + m.ends_above
    for xp in range(17):
        acc = jnp.maximum(jnp.dot(lhs, w_fo[xp], preferred_element_type=F32), 0.0)
        a_ref[:, xp, :, 0:128] = as_blocks(acc[:, :128].astype(BF16))
        a_ref[:, xp, :, 128:256] = as_blocks(scaled(acc[:, 128:], ends).astype(BF16))
    clear_outside(a_ref, 1, 0, ty, tx, m, split=True)
    quad_lane = lane_block((4, 16, 128), 32)

    def second(yg):
        acc = jnp.maximum(conv(a_ref, w_fs, yg, 16), 0.0)
        skip[2 + 2 * yg, 1:17] = as_blocks(acc[:, :128].astype(BF16))
        skip[3 + 2 * yg, 1:17] = as_blocks(acc[:, 128:].astype(BF16))
        top = jnp.maximum(acc[:, :128], acc[:, 128:])
        top = jnp.maximum(top, pltpu.roll(top, 64, 1))
        top = jnp.maximum(top, pltpu.roll(top, 32, 1)).reshape(4, 4, 16, 128)
        quad = top[:, 0]
        for q in range(1, 4):
            quad = jnp.where(quad_lane == q, top[:, q], quad)
        quads[2 + yg, 1:5] = quad.astype(BF16)

    for yg in (0, 1, 6, 7):
        second(yg)
    copies = exchange(quads, (2, 1), quad_send, quad_recv, ty, tx, ALONG_TY)
    for yg in range(2, 6):
        second(yg)
    copies += exchange(quads, (2, 1), quad_send, quad_recv, ty, tx, ALONG_TX)
    skip_copies = exchange(skip, (2, 1), skip_send, skip_recv, ty, tx)
    loads[4].wait()
    build_middle(spread_blocks(r_cs, 64), w_cs)
    loads[5].wait()
    build_middle_merge(r_mm, w_mm)
    loads[6].wait()
    build_middle(spread_blocks(r_mf, 64), w_mf)
    loads[7].wait()
    build_fine_merge(r_fm, w_fm)
    loads[8].wait()
    build_fine(spread_blocks(r_ff, 32), w_ff)
    build_head(head, w_head)
    finish(copies)

    clear_outside(quads, 2, 1, ty, tx, m)

    def spread(y):
        c = as_rows(quads[y]).astype(F32)
        below, above = row_below(c), row_above(c)
        for q in range(4):
            tile = scaled(pltpu.roll(c, (-32 * q) % 128, 1), m.block[0])
            tile = tile + scaled(pltpu.roll(below, (32 - 32 * q) % 128, 1), m.block[1])
            tile = tile + scaled(pltpu.roll(above, (64 - 32 * q) % 128, 1), m.block[2])
            blocks = as_blocks(tile.astype(BF16))
            lane = 128 * (q % 2)
            for quad in range(6):
                place = 2 * quad - 1 + q // 2
                if 0 <= place < 10:
                    in_ref[y, place, :, lane : lane + 128] = blocks[quad]

    loop(12, spread, 3)

    def middle_open(yg, acc):
        for py in range(2):
            tile = jnp.maximum(acc[:, 128 * py : 128 * py + 128], 0.0)
            store_middle(b_ref, 2 * yg + py, tile, m)

    conv_lines(in_ref, w_mo, (2, 3), 9, middle_open)
    clear_outside(b_ref, 1, 0, ty, tx, m, split=True)
    low = lane_block((4, 8, 128), 64) == 0

    def middle_second(yg, acc):
        acc = jnp.maximum(acc, 0.0)
        middle[4 + 2 * yg, 2:10] = as_blocks(acc[:, :128].astype(BF16))
        middle[5 + 2 * yg, 2:10] = as_blocks(acc[:, 128:].astype(BF16))
        top = jnp.maximum(acc[:, :128], acc[:, 128:])
        top = jnp.maximum(top, pltpu.roll(top, 64, 1))
        s_ref[yg] = jnp.maximum(top, row_above(top))
        some = s_ref[yg, pl.ds(0, 64, stride=2), :].reshape(4, 2, 8, 128)
        pair = jnp.where(low, some[:, 0], some[:, 1])
        coarse[4 + yg, 1:3] = pair.reshape(2, 16, 128).astype(BF16)

    conv_lines(b_ref, w_ms, (2, 2), 8, middle_second)
    copies = exchange(coarse, (4, 1), coarse_send, coarse_recv, ty, tx)
    middle_copies = exchange(middle, (4, 2), middle_send, middle_recv, ty, tx)

    finish(skip_copies)
    clear_outside(skip, 2, 1, ty, tx, m)

    def fine_in(y):
        x = as_rows(skip[y]).astype(F32)
        store_fine(fi_ref, y, x, m)

    loop(20, fine_in, 2)
    for yg in range(9):
        part_ref[yg] = jnp.dot(
            window(fi_ref, yg, 17), w_fm[0:2048], preferred_element_type=F32
        )
    finish(copies)

    clear_outside(coarse, 4, 1, ty, tx, m)

    def coarse_in(y):
        x = coarse[y].astype(F32).reshape(8, 8, 128)
        x = as_rows(jnp.concatenate([x, jnp.zeros_like(x)], axis=1))
        store_middle(ci_ref, y, x, m)

    loop(12, coarse_in)

    def coarse_open(yg, acc):
        for py in range(2):
            tile = jnp.maximum(acc[:, 128 * py : 128 * py + 128], 0.0)
            tile = scaled(tile, m.coarse_z)
            store_middle(co_ref, 2 * yg + py, tile, m)

    conv_lines(ci_ref, w_co, (2, 3), 7, coarse_open)
    clear_outside(co_ref, 3, 1, ty, tx, m, split=True)

    def coarse_second(yg, acc):
        for py in range(2):
            tile = jnp.maximum(acc[:, 128 * py : 128 * py + 128], 0.0)
            half = tile.reshape(6, 16, 128)[:, :8].reshape(48, 128)
            s2_ref[2 * yg + py, pl.ds(0, 48, stride=2), :] = half
            s2_ref[2 * yg + py, pl.ds(1, 48, stride=2), :] = half
            store_single(u1_ref, 2 * yg + py, s2_ref[2 * yg + py], m)

    conv_lines(co_ref, w_cs, (2, 2), 6, coarse_second)
    clear_outside(u1_ref, 2, 2, ty, tx, m)
    finish(middle_copies)
    clear_outside(middle, 4, 2, ty, tx, m)

    def middle_in(y):
        x = as_rows(middle[y]).astype(F32)
        store_middle(mi_ref, y, x, m)

    loop(16, middle_in)

    def middle_merge(yg, acc):
        for py in range(2):
            tile = jnp.maximum(acc[:, 128 * py : 128 * py + 128], 0.0)
            store_middle(mm_ref, 2 * yg + py, tile, m)

    conv_lines(mi_ref, w_mm, (2, 2, 3), 11, middle_merge, u1_ref)
    clear_outside(mm_ref, 3, 1, ty, tx, m, split=True)

    def middle_final(yg, acc):
        for py in range(2):
            tile = jnp.maximum(acc[:, 128 * py : 128 * py + 128], 0.0)
            store_single(u2_ref, 2 * yg + py, tile, m)

    conv_lines(mm_ref, w_mf, (2, 2, 2), 10, middle_final)
    clear_outside(u2_ref, 2, 2, ty, tx, m)


    def fine_merge(yg):
        acc = part_ref[yg] + jnp.dot(
            jnp.concatenate(up_window(u2_ref, yg, 1, 17), axis=1),
            w_fm[2048:3072],
            preferred_element_type=F32,
        )
        for py in range(2):
            tile = jnp.maximum(acc[:, 128 * py : 128 * py + 128], 0.0)
            store_fine(fm_ref, 2 * yg + py, tile, m)

    for yg in range(9):
        fine_merge(yg)
    clear_outside(fm_ref, 1, 0, ty, tx, m, split=True)

    def fine_final(yg):
        last_ref[yg] = jnp.maximum(conv(fm_ref, w_ff, yg, 16), 0.0).astype(BF16)

    for yg in range(8):
        fine_final(yg)
    logits = jnp.dot(
        jnp.concatenate([last_ref[yg] for yg in range(8)], axis=1),
        w_head[...],
        preferred_element_type=F32,
    )
    first_ref[...] = logits[:, :128]
    second_ref[...] = logits[:, 128:]

    def finished(k):
        turn_ref[k, pl.ds(0, 16, stride=2), :] = first_ref[pl.ds(k, 16, stride=16), :]
        turn_ref[k, pl.ds(1, 16, stride=2), :] = second_ref[pl.ds(k, 16, stride=16), :]
        turned = turn_ref[k].T
        for c in range(3):
            for pz in range(2):
                row = 32 * c + 16 * pz
                out[c, 2 * k + pz] = turned[row : row + 16]

    for k in range(16):
        finished(k)


def per_device(
    raw_bricks,
    stretch_reader,
    fine_open,
    fine_second,
    middle_open,
    middle_second,
    coarse_open,
    coarse_second,
    middle_merge,
    middle_final,
    fine_merge,
    fine_final,
    affinity_head,
):
    def flat(w):
        return w.reshape(27, w.shape[3], w.shape[4])

    weights = [
        flat(fine_second),
        flat(middle_open.transpose(0, 1, 2, 4, 3)),
        flat(middle_second),
        flat(coarse_open),
        flat(coarse_second),
        flat(middle_merge),
        flat(middle_final),
        flat(fine_merge),
        flat(fine_final),
    ]
    opening = fine_open.transpose(0, 1, 4, 2, 3).reshape(9, 3, 32)
    vmem = pl.BlockSpec(memory_space=pltpu.VMEM)
    smem = pl.BlockSpec(memory_space=pltpu.SMEM)
    hbm = pl.BlockSpec(memory_space=pl.ANY)
    dma = pltpu.SemaphoreType.DMA

    def half(*shape):
        return pltpu.VMEM(shape, BF16)

    def full(*shape):
        return pltpu.VMEM(shape, F32)

    return pl.pallas_call(
        whole_kernel,
        out_shape=jax.ShapeDtypeStruct((3, DEPTH, TILE_Y, TILE_X), F32),
        in_specs=[smem] + [vmem] * 3 + [hbm] * 9,
        out_specs=vmem,
        scratch_shapes=[half(*w.shape) for w in weights]
        + [half(17, 768, 256)]
        + [half(size, 256) for size in (2048, 2048, 3072, 3072, 3072, 4096, 3072, 3072, 2048, 2048)]
        + [
            half(8, 4, 32, 128),
            half(8, 4, 32, 128),
            half(2, 2, 4, 32, 128),
            full(3, 296, 256),
            full(20, 40, 128),
            half(18, 17, 16, 256),
            half(12, 6, 16, 128),
            half(20, 18, 16, 128),
            half(12, 10, 16, 256),
            half(10, 9, 16, 384),
            full(4, 128, 128),
            half(12, 4, 16, 128),
            half(16, 12, 16, 128),
            half(12, 8, 16, 384),
            half(10, 7, 16, 384),
            full(8, 96, 128),
            half(8, 12, 16, 256),
            half(16, 12, 16, 384),
            half(14, 11, 16, 384),
            half(12, 20, 16, 256),
            half(20, 18, 16, 256),
            half(18, 17, 16, 256),
            full(9, 272, 256),
            half(8, 256, 256),
            full(256, 128),
            full(256, 128),
            full(16, 32, 128),
            full(3, 128, 128),
            dma((9,)),
            dma((8,)),
            dma((8,)),
            dma((3,)),
            dma((3,)),
        ]
        + [dma((8,))] * 8,
        name="whole",
        compiler_params=pltpu.CompilerParams(
            vmem_limit_bytes=58 * MIB, collective_id=0, has_side_effects=True
        ),
        cost_estimate=pl.CostEstimate(flops=10**10, bytes_accessed=10**7, transcendentals=0),
    )(stretch_reader, raw_bricks[0], affinity_head, opening, *weights)


def solution(mesh):
    placed = (P(("ty", "tx"), None, None, None),) + (P(),) * 12
    return jax.shard_map(
        per_device, mesh=mesh, in_specs=placed, out_specs=P(None, None, "ty", "tx"), check_vma=False
    )
```

```python
import jax
import jax.numpy as jnp
from jax import lax
from jax.experimental import pallas as pl
from jax.experimental.pallas import tpu as pltpu
from jax.sharding import PartitionSpec as P

TILE_Y = 16
TILE_X = 32
DEPTH = 32
BF16 = jnp.bfloat16
F32 = jnp.float32
MIB = 1 << 20


def iota(shape, dim):
    return lax.broadcasted_iota(jnp.int32, shape, dim)


def lane_block(shape, width):
    return lax.shift_right_logical(iota(shape, len(shape) - 1), width.bit_length() - 1)


def spread_blocks(w_ref, out_chans, out_dim=0):
    eye = (iota((out_chans, 128), 0) == iota((out_chans, 128), 1) % out_chans).astype(BF16)
    return [
        lax.dot_general(w_ref[t], eye, (((out_dim,), (0,)), ((), ())), preferred_element_type=F32)
        for t in range(27)
    ]


def tap(a, b, e):
    if 0 <= a <= 2 and 0 <= b <= 2 and 0 <= e <= 2:
        return 9 * a + 3 * b + e
    return None


def masked_sum(blocks, taps, width):
    shape = blocks[0].shape
    lanes = lane_block(shape, width)
    tile = jnp.zeros(shape, F32)
    for place, index in enumerate(taps):
        if index is not None:
            tile = jnp.where(lanes == place, blocks[index], tile)
    return tile


def build_fine(blocks, out_ref):
    for y in range(4):
        for j in range(2):
            for half in range(2):
                for px_in in range(2):
                    for slot in range(2):
                        z = (1 + slot) if half == 0 else (3, 0)[slot]
                        row = (y * 2 + j) * 256 + half * 128 + px_in * 64 + slot * 32
                        for py in range(2):
                            taps = [
                                tap(z - pz, y - py, 2 * j + px_in - px)
                                for px in range(2)
                                for pz in range(2)
                            ]
                            out_ref[row : row + 32, py * 128 : (py + 1) * 128] = masked_sum(
                                blocks, taps, 32
                            ).astype(BF16)


def build_middle(blocks, out_ref):
    for y in range(4):
        for j in range(2):
            for slot, dz in enumerate((1, 0, 2)):
                for px_in in range(2):
                    row = (y * 2 + j) * 384 + slot * 128 + px_in * 64
                    for py in range(2):
                        taps = [tap(dz, y - py, 2 * j + px_in - px) for px in range(2)]
                        out_ref[row : row + 64, py * 128 : (py + 1) * 128] = masked_sum(
                            blocks, taps, 64
                        ).astype(BF16)


def build_middle_open(blocks, out_ref):
    for y in range(4):
        for j in range(2):
            for px_in in range(2):
                for slot, dz in enumerate((1, 0, 2, 9)):
                    row = (y * 2 + j) * 256 + px_in * 128 + slot * 32
                    for py in range(2):
                        taps = [tap(dz, y - py, 2 * j + px_in - px) for px in range(2)]
                        out_ref[row : row + 32, py * 128 : (py + 1) * 128] = masked_sum(
                            blocks, taps, 64
                        ).astype(BF16)


def build_up(zcombined, out_ref, row0):
    shape = (64, 128)
    odd = lane_block(shape, 64) == 1
    for slot in range(4):
        for xc in range(2):
            rows = None
            if slot < 3:
                rows = []
                for dy in range(3):
                    t = zcombined[slot][dy]
                    if xc == 0:
                        rows.append(jnp.where(odd, t[0], t[0] + t[1]))
                    else:
                        rows.append(jnp.where(odd, t[1] + t[2], t[2]))
            for yc in range(2):
                row = row0 + (yc * 2 + xc) * 256 + slot * 64
                for py in range(2):
                    if rows is None:
                        tile = jnp.zeros(shape, F32)
                    elif (py, yc) == (0, 0):
                        tile = rows[0] + rows[1]
                    elif (py, yc) == (0, 1):
                        tile = rows[2]
                    elif (py, yc) == (1, 0):
                        tile = rows[0]
                    else:
                        tile = rows[1] + rows[2]
                    out_ref[row : row + 64, py * 128 : (py + 1) * 128] = tile.astype(BF16)


def build_open(w_ref, base_ref, out_ref):
    base_ref[...] = jnp.zeros_like(base_ref)
    eye = (iota((32, 128), 0) == iota((32, 128), 1) % 32).astype(BF16)
    rows = []
    for t in range(9):
        three = jnp.dot(w_ref[t], eye, preferred_element_type=F32)
        rows += [three[dx : dx + 1] for dx in range(3)]
    for dy in range(3):
        for z in range(6):
            for x in range(4):
                row = 40 + z // 3 * 128 + z % 3 * 40 + x
                for half in range(2):
                    taps = []
                    for px in range(2):
                        for p in range(2):
                            z_out = p if half == 0 else (2, -1)[p]
                            taps.append(tap(z - 1 - z_out, dy, x - px))
                    base_ref[dy, row : row + 1, 128 * half : 128 * half + 128] = masked_sum(
                        rows, taps, 32
                    )
    for xp in range(17):
        for dy in range(3):
            out_ref[xp, 256 * dy : 256 * dy + 256] = base_ref[
                dy, 40 - 2 * xp : 296 - 2 * xp
            ].astype(BF16)


def build_middle_merge(w_ref, out_ref):
    both = spread_blocks(w_ref, 64)
    build_middle([block[64:128] for block in both], out_ref)
    up = [block[:64] for block in both]
    grid = [[[up[9 * dz + 3 * dy + dx] for dx in range(3)] for dy in range(3)] for dz in (1, 0, 2)]
    build_up(grid, out_ref, 3072)


def build_fine_merge(w_ref, out_ref):
    both = spread_blocks(w_ref, 32)
    build_fine([block[64:96] for block in both], out_ref)
    up = [block[:64] for block in both]
    odd_z = lane_block((64, 128), 32) % 2 == 1

    def zmix(slot, dy, dx):
        w0, w1, w2 = (up[9 * a + 3 * dy + dx] for a in range(3))
        if slot == 0:
            return jnp.where(odd_z, w0 + w1, w1 + w2)
        if slot == 1:
            return jnp.where(odd_z, 0.0, w0)
        return jnp.where(odd_z, w2, 0.0)

    grid = [[[zmix(slot, dy, dx) for dx in range(3)] for dy in range(3)] for slot in range(3)]
    build_up(grid, out_ref, 2048)


def build_head(head_ref, out_ref):
    column = iota((256, 32), 0) % 128 // 32
    picked = jnp.zeros((256, 32), F32)
    for c in range(3):
        picked = jnp.where(column == c, head_ref[c : c + 1, :].astype(F32), picked)
    eye = (iota((256, 32), 0) % 32 == iota((256, 32), 1)).astype(BF16)
    full = lax.dot_general(
        eye, picked.astype(BF16), (((1,), (1,)), ((), ())), preferred_element_type=F32
    )
    row, col = iota((256, 256), 0), iota((256, 256), 1)
    fits = (row // 64 % 2 == col // 128) & (row // 32 % 2 == col // 16 % 2)
    fits = fits & (row // 128 == col % 16) & (col % 128 < 96)
    base = jnp.where(fits, full, 0.0)
    for yg in range(8):
        for px in range(2):
            part = base[:, 128 * px : 128 * px + 128]
            out_ref[256 * yg : 256 * yg + 256, 128 * px : 128 * px + 128] = pltpu.roll(
                part, 2 * yg, 1
            ).astype(BF16)


class Masks:
    def __init__(self):
        row, lane = iota((16, 128), 0), iota((16, 128), 1)

        def factor(where):
            return jnp.where(where, 1.0, 0.0).astype(F32)

        first, last = row > 0, row < 15
        odd = (lane & 32) != 0
        self.below, self.above = factor(first), factor(last)
        self.ends_below, self.ends_above = factor(odd & first), factor(~odd & last)
        self.low, self.high_below = factor(lane < 64), factor((lane >= 64) & first)
        self.px = [factor(lane < 64), factor(lane >= 64)]
        self.coarse_z = factor(row < 8)
        block = lane >> 5
        self.block = [factor(block == 0), factor((block == 1) & first), factor((block == 2) & last)]


def scaled(x, factor):
    return as_rows(as_blocks(x) * factor[None])


def row_below(x):
    return pltpu.roll(x, 1, 0)


def row_above(x):
    return pltpu.roll(x, x.shape[0] - 1, 0)


def as_rows(x):
    return x.reshape(x.shape[0] * 16, x.shape[2])


def as_blocks(x):
    return x.reshape(x.shape[0] // 16, 16, x.shape[1])


def up_window(src, yg, shift, groups):
    y, x = yg + shift, shift
    return [as_rows(src[y + yc, x + xc : x + xc + groups]) for yc in range(2) for xc in range(2)]


def window(src, yg, groups, up=None):
    pieces = [as_rows(src[2 * yg + y, j : j + groups]) for y in range(4) for j in range(2)]
    if up is not None:
        pieces += up_window(up, yg, 0, groups)
    return jnp.concatenate(pieces, axis=1)


def conv(src, w_ref, yg, groups):
    lhs = window(src, yg, groups)
    return jnp.dot(lhs, w_ref[...], preferred_element_type=F32)


def conv_lines(src, w_ref, counts, groups, body, up=None, beside=None):
    first, rows = 0, groups * 16
    for number, count in enumerate(counts):
        if beside is not None:
            beside(number)
        lines = range(first, first + count)
        lhs = jnp.concatenate([window(src, yg, groups, up) for yg in lines], axis=0)
        acc = jnp.dot(lhs, w_ref[...], preferred_element_type=F32)
        for i, yg in enumerate(lines):
            body(yg, acc[i * rows : (i + 1) * rows])
        first += count


def store_fine(ref, y, tile, m):
    ends = scaled(row_below(tile), m.ends_below) + scaled(row_above(tile), m.ends_above)
    ref[y, :, :, 0:128] = as_blocks(tile.astype(BF16))
    ref[y, :, :, 128:256] = as_blocks(ends.astype(BF16))


def store_middle(ref, y, tile, m):
    ref[y, :, :, 0:128] = as_blocks(tile.astype(BF16))
    ref[y, :, :, 128:256] = as_blocks(scaled(row_below(tile), m.below).astype(BF16))
    ref[y, :, :, 256:384] = as_blocks(scaled(row_above(tile), m.above).astype(BF16))


def store_single(ref, y, tile, m):
    below, above = row_below(tile), scaled(row_above(tile), m.above)
    near = [
        scaled(tile, m.low) + scaled(pltpu.roll(below, 64, 1), m.high_below),
        scaled(pltpu.roll(tile, 64, 1), m.low) + scaled(below, m.high_below),
    ]
    far = [above, pltpu.roll(above, 64, 1)]
    for px in range(2):
        a, b = as_blocks(near[px].astype(BF16)), as_blocks(far[px].astype(BF16))
        for xg in range(tile.shape[0] // 16):
            ref[y, 2 * xg + px, :, 0:128] = a[xg]
            ref[y, 2 * xg + px, :, 128:256] = b[xg]


def clear_outside(ref, lines, places, ty, tx, m, split=False):
    count = ref.shape[1]
    parts = ref.shape[3] // 128

    def halve(place, px):
        factor = jnp.concatenate([m.px[px]] * parts, axis=1).astype(BF16)
        ref[:, place] = ref[:, place] * factor[None]

    @pl.when(ty == 0)
    def _():
        ref[0:lines] = jnp.zeros((lines,) + ref.shape[1:], BF16)

    @pl.when(ty == 15)
    def _():
        ref[ref.shape[0] - lines :] = jnp.zeros((lines,) + ref.shape[1:], BF16)

    @pl.when(tx == 0)
    def _():
        if places:
            ref[:, 0:places] = jnp.zeros((ref.shape[0], places) + ref.shape[2:], BF16)
        if split:
            halve(places, 1)

    @pl.when(tx == 7)
    def _():
        if places:
            ref[:, count - places :] = jnp.zeros((ref.shape[0], places) + ref.shape[2:], BF16)
        if split:
            halve(count - 1 - places, 0)


def loop(count, body, unroll=1):
    def step(i, carry):
        body(i)
        return carry

    lax.fori_loop(0, count, step, 0, unroll=unroll)


AROUND = [(-1, 0), (1, 0), (-1, -1), (-1, 1), (1, -1), (1, 1), (0, -1), (0, 1)]
ALONG_TY, ALONG_TX = range(6), range(6, 8)


def span(step, core, width):
    if step == 0:
        return width, width, core
    if step > 0:
        return core, 0, width
    return width, core + width, width


def exchange(ref, widths, send_sems, recv_sems, ty, tx, directions=range(8)):
    copies = []
    for i in directions:
        dy, dx = AROUND[i]
        sy, ly, ny = span(dy, ref.shape[0] - 2 * widths[0], widths[0])
        sx, lx, nx = span(dx, ref.shape[1] - 2 * widths[1], widths[1])
        copy = pltpu.make_async_remote_copy(
            src_ref=ref.at[pl.ds(sy, ny), pl.ds(sx, nx)],
            dst_ref=ref.at[pl.ds(ly, ny), pl.ds(lx, nx)],
            send_sem=send_sems.at[i],
            recv_sem=recv_sems.at[i],
            device_id=((ty + dy + 16) % 16, (tx + dx + 8) % 8),
            device_id_type=pl.DeviceIdType.MESH,
        )
        sends, receives = neighbour(dy, dx, ty, tx), neighbour(-dy, -dx, ty, tx)
        pl.when(sends)(copy.start)
        copies.append((copy, sends, receives))
    return copies


def neighbour(dy, dx, ty, tx):
    there = [tx >= 0]
    if dy:
        there.append(ty < 15 if dy > 0 else ty > 0)
    if dx:
        there.append(tx < 7 if dx > 0 else tx > 0)
    return there[-1] if len(there) < 3 else there[1] & there[2]


def finish(copies):
    for copy, sends, receives in copies:
        pl.when(receives)(copy.wait_recv)
    for copy, sends, receives in copies:
        pl.when(sends)(copy.wait_send)


def whole_kernel(
    readers, raw, head, fo, fs, mo, ms, co, cs, mm, mf, fm, ff,
    out,
    r_fs, r_mo, r_ms, r_co, r_cs, r_mm, r_mf, r_fm, r_ff,
    w_fo, w_fs, w_mo, w_ms, w_co, w_cs, w_mm, w_mf, w_fm, w_ff, w_head,
    outgoing, arrived, held,
    base_ref, z_ref, a_ref,
    quads, skip, in_ref, b_ref, s_ref,
    coarse, middle, ci_ref, co_ref, s2_ref, u1_ref, mi_ref, mm_ref, u2_ref, fi_ref, fm_ref,
    part_ref, last_ref, bricks_ref,
    load_sems, row_send, row_recv, near_send, near_recv,
    quad_send, quad_recv, skip_send, skip_recv, coarse_send, coarse_recv, middle_send, middle_recv,
):
    ty, tx = lax.axis_index("ty"), lax.axis_index("tx")
    m = Masks()
    mesh_id = pl.DeviceIdType.MESH
    loads = [
        pltpu.make_async_copy(source, target, load_sems.at[i])
        for i, (source, target) in enumerate(
            zip((fs, mo, ms, co, cs, mm, mf, fm, ff), (r_fs, r_mo, r_ms, r_co, r_cs, r_mm, r_mf, r_fm, r_ff))
        )
    ]
    for load in loads:
        load.start()

    barrier = pltpu.get_barrier_semaphore()
    greeted = [(ty, (tx + d) % 8) for d in range(1, 8)]
    greeted += [((ty + dy + 16) % 16, (tx + dx + 8) % 8) for dy in (-1, 1) for dx in (-1, 0, 1)]
    for device in greeted:
        pl.semaphore_signal(barrier, inc=1, device_id=device, device_id_type=mesh_id)
    for slot in range(3):
        for z in range(32):
            bricks_ref[slot, pl.ds(z, 4, stride=32), :] = raw[
                slot, :, 128 * z : 128 * z + 128
            ].astype(F32)

    pl.semaphore_wait(barrier, len(greeted))

    reader = [readers[ty * 8 + c] for c in range(8)]
    for c in range(8):
        rank = 0
        for earlier in range(c):
            rank += (reader[earlier] == reader[c]).astype(jnp.int32)
        outgoing[c] = bricks_ref[jnp.minimum(rank, 2)].astype(BF16).reshape(4, 32, 128)
    copies = []
    for d in range(1, 8):
        peer = (tx + d) % 8
        copy = pltpu.make_async_remote_copy(
            src_ref=outgoing.at[peer],
            dst_ref=arrived.at[tx],
            send_sem=row_send.at[d],
            recv_sem=row_recv.at[d],
            device_id=(ty, peer),
            device_id_type=mesh_id,
        )
        copy.start()
        copies.append(copy)
    arrived[tx] = outgoing[tx]
    build_open(fo, base_ref, w_fo)
    loads[0].wait()
    build_fine(spread_blocks(r_fs, 32), w_fs)
    for copy in copies:
        copy.wait()
    own = readers[ty * 8 + tx] % 8
    held[1, 1] = arrived[own]
    copies = []
    for i, (dy, dx) in enumerate([(0, 1), (1, 0), (1, 1)]):
        copy = pltpu.make_async_remote_copy(
            src_ref=held.at[1, 1],
            dst_ref=held.at[1 - dy, 1 - dx],
            send_sem=near_send.at[i],
            recv_sem=near_recv.at[i],
            device_id=((ty + dy) % 16, (tx + dx) % 8),
            device_id_type=mesh_id,
        )
        copy.start()
        copies.append(copy)
    loads[1].wait()
    build_middle_open(spread_blocks(r_mo, 64, 1), w_mo)
    loads[2].wait()
    build_middle(spread_blocks(r_ms, 64), w_ms)
    loads[3].wait()
    build_middle(spread_blocks(r_co, 64), w_co)
    for copy in copies:
        copy.wait()

    z_ref[:, 0:8] = jnp.zeros((20, 8, 128), F32)
    z_ref[:, 32:40] = jnp.zeros((20, 8, 128), F32)
    lane = iota((32, 128), 1)
    lines = []
    for br in range(4):
        bricks = []
        for bc in range(4):
            brick = held[br // 2, bc // 2, br % 2 * 2 + bc % 2].astype(F32)
            ok = True
            if br == 0:
                ok = ty > 0
            if br == 3:
                ok = ty < 15
            if bc == 0:
                ok = (tx > 0) & ok
            if bc == 3:
                ok = (tx < 7) & ok
            if ok is not True:
                brick = jnp.where(ok, brick, 0.0)
            bricks.append(brick)
        for r in ((6, 7), range(8), range(8), (0, 1))[br]:
            y = 8 * br + r - 6
            line = jnp.where(lane < 36, pltpu.roll(bricks[3], (34 - 16 * r) % 128, 1), 0.0)
            line = jnp.where(lane < 34, pltpu.roll(bricks[2], (18 - 16 * r) % 128, 1), line)
            line = jnp.where(lane < 18, pltpu.roll(bricks[1], (2 - 16 * r) % 128, 1), line)
            line = jnp.where(lane < 2, pltpu.roll(bricks[0], (-14 - 16 * r) % 128, 1), line)
            z_ref[y, 4:36, :] = line
            parts = [z_ref[y, pl.ds(2 + z, 16, stride=2), :] for z in range(6)]
            for t in range(2):
                tile = parts[3 * t]
                for i in (1, 2):
                    tile = tile + pltpu.roll(parts[3 * t + i], 40 * i, 1)
                parts[t] = tile
            lines.append(jnp.concatenate(parts[:2], axis=1).astype(BF16))
    lhs = jnp.concatenate(
        [jnp.concatenate(lines[dy : dy + 18], axis=0) for dy in range(3)], axis=1
    )
    ends = m.ends_below + m.ends_above
    for xp in range(17):
        acc = jnp.maximum(jnp.dot(lhs, w_fo[xp], preferred_element_type=F32), 0.0)
        a_ref[:, xp, :, 0:128] = as_blocks(acc[:, :128].astype(BF16))
        a_ref[:, xp, :, 128:256] = as_blocks(scaled(acc[:, 128:], ends).astype(BF16))
    clear_outside(a_ref, 1, 0, ty, tx, m, split=True)
    quad_lane = lane_block((4, 16, 128), 32)

    def second(yg):
        acc = jnp.maximum(conv(a_ref, w_fs, yg, 16), 0.0)
        skip[2 + 2 * yg, 1:17] = as_blocks(acc[:, :128].astype(BF16))
        skip[3 + 2 * yg, 1:17] = as_blocks(acc[:, 128:].astype(BF16))
        top = jnp.maximum(acc[:, :128], acc[:, 128:])
        top = jnp.maximum(top, pltpu.roll(top, 64, 1))
        top = jnp.maximum(top, pltpu.roll(top, 32, 1)).reshape(4, 4, 16, 128)
        quad = top[:, 0]
        for q in range(1, 4):
            quad = jnp.where(quad_lane == q, top[:, q], quad)
        quads[2 + yg, 1:5] = quad.astype(BF16)

    for yg in (0, 1, 6, 7):
        second(yg)
    copies = exchange(quads, (2, 1), quad_send, quad_recv, ty, tx, ALONG_TY)
    for yg in range(2, 6):
        second(yg)
    copies += exchange(quads, (2, 1), quad_send, quad_recv, ty, tx, ALONG_TX)
    skip_copies = exchange(skip, (2, 1), skip_send, skip_recv, ty, tx)
    loads[4].wait()
    build_middle(spread_blocks(r_cs, 64), w_cs)
    loads[5].wait()
    build_middle_merge(r_mm, w_mm)
    loads[6].wait()
    build_middle(spread_blocks(r_mf, 64), w_mf)
    loads[7].wait()
    build_fine_merge(r_fm, w_fm)
    loads[8].wait()
    build_fine(spread_blocks(r_ff, 32), w_ff)
    build_head(head, w_head)
    finish(copies)

    clear_outside(quads, 2, 1, ty, tx, m)

    def spread(y):
        c = as_rows(quads[y]).astype(F32)
        below, above = row_below(c), row_above(c)
        for q in range(4):
            tile = scaled(pltpu.roll(c, (-32 * q) % 128, 1), m.block[0])
            tile = tile + scaled(pltpu.roll(below, (32 - 32 * q) % 128, 1), m.block[1])
            tile = tile + scaled(pltpu.roll(above, (64 - 32 * q) % 128, 1), m.block[2])
            blocks = as_blocks(tile.astype(BF16))
            lane = 128 * (q % 2)
            for quad in range(6):
                place = 2 * quad - 1 + q // 2
                if 0 <= place < 10:
                    in_ref[y, place, :, lane : lane + 128] = blocks[quad]

    def spread_lines(number):
        for y in (range(6), range(6, 12))[number]:
            spread(y)


    def middle_open(yg, acc):
        for py in range(2):
            tile = jnp.maximum(acc[:, 128 * py : 128 * py + 128], 0.0)
            store_middle(b_ref, 2 * yg + py, tile, m)

    conv_lines(in_ref, w_mo, (2, 3), 9, middle_open, beside=spread_lines)
    clear_outside(b_ref, 1, 0, ty, tx, m, split=True)
    low = lane_block((4, 8, 128), 64) == 0

    def middle_second(yg, acc):
        acc = jnp.maximum(acc, 0.0)
        middle[4 + 2 * yg, 2:10] = as_blocks(acc[:, :128].astype(BF16))
        middle[5 + 2 * yg, 2:10] = as_blocks(acc[:, 128:].astype(BF16))
        top = jnp.maximum(acc[:, :128], acc[:, 128:])
        top = jnp.maximum(top, pltpu.roll(top, 64, 1))
        s_ref[yg] = jnp.maximum(top, row_above(top))
        some = s_ref[yg, pl.ds(0, 64, stride=2), :].reshape(4, 2, 8, 128)
        pair = jnp.where(low, some[:, 0], some[:, 1])
        coarse[4 + yg, 1:3] = pair.reshape(2, 16, 128).astype(BF16)

    conv_lines(b_ref, w_ms, (2, 2), 8, middle_second)
    copies = exchange(coarse, (4, 1), coarse_send, coarse_recv, ty, tx)
    middle_copies = exchange(middle, (4, 2), middle_send, middle_recv, ty, tx)

    finish(skip_copies)
    clear_outside(skip, 2, 1, ty, tx, m)

    def fine_in(y):
        x = as_rows(skip[y]).astype(F32)
        store_fine(fi_ref, y, x, m)

    def fine_part(yg):
        for y in range(4) if yg == 0 else (2 * yg + 2, 2 * yg + 3):
            fine_in(y)
        part_ref[yg] = jnp.dot(
            window(fi_ref, yg, 17), w_fm[0:2048], preferred_element_type=F32
        )

    for yg in range(4):
        fine_part(yg)
    finish(copies)
    finish(middle_copies)
    clear_outside(middle, 4, 2, ty, tx, m)
    clear_outside(coarse, 4, 1, ty, tx, m)

    def coarse_in(y):
        x = coarse[y].astype(F32).reshape(8, 8, 128)
        x = as_rows(jnp.concatenate([x, jnp.zeros_like(x)], axis=1))
        store_middle(ci_ref, y, x, m)

    def middle_in(y):
        x = as_rows(middle[y]).astype(F32)
        store_middle(mi_ref, y, x, m)

    def beside_open(number):
        for y in (range(6), range(6, 12))[number]:
            coarse_in(y)
        fine_part(4 + number)

    def beside_second(number):
        for y in (range(8), range(8, 16))[number]:
            middle_in(y)
        fine_part(6 + number)


    def coarse_open(yg, acc):
        for py in range(2):
            tile = jnp.maximum(acc[:, 128 * py : 128 * py + 128], 0.0)
            tile = scaled(tile, m.coarse_z)
            store_middle(co_ref, 2 * yg + py, tile, m)

    conv_lines(ci_ref, w_co, (2, 3), 7, coarse_open, beside=beside_open)
    clear_outside(co_ref, 3, 1, ty, tx, m, split=True)

    def coarse_second(yg, acc):
        for py in range(2):
            tile = jnp.maximum(acc[:, 128 * py : 128 * py + 128], 0.0)
            half = tile.reshape(6, 16, 128)[:, :8].reshape(48, 128)
            s2_ref[2 * yg + py, pl.ds(0, 48, stride=2), :] = half
            s2_ref[2 * yg + py, pl.ds(1, 48, stride=2), :] = half
            store_single(u1_ref, 2 * yg + py, s2_ref[2 * yg + py], m)

    conv_lines(co_ref, w_cs, (2, 2), 6, coarse_second, beside=beside_second)
    fine_part(8)
    clear_outside(u1_ref, 2, 2, ty, tx, m)

    def middle_merge(yg, acc):
        for py in range(2):
            tile = jnp.maximum(acc[:, 128 * py : 128 * py + 128], 0.0)
            store_middle(mm_ref, 2 * yg + py, tile, m)

    conv_lines(mi_ref, w_mm, (2, 2, 3), 11, middle_merge, u1_ref)
    clear_outside(mm_ref, 3, 1, ty, tx, m, split=True)

    def middle_final(yg, acc):
        for py in range(2):
            tile = jnp.maximum(acc[:, 128 * py : 128 * py + 128], 0.0)
            store_single(u2_ref, 2 * yg + py, tile, m)

    conv_lines(mm_ref, w_mf, (2, 2, 2), 10, middle_final)
    clear_outside(u2_ref, 2, 2, ty, tx, m)


    def fine_merge(yg):
        acc = part_ref[yg] + jnp.dot(
            jnp.concatenate(up_window(u2_ref, yg, 1, 17), axis=1),
            w_fm[2048:3072],
            preferred_element_type=F32,
        )
        for py in range(2):
            tile = jnp.maximum(acc[:, 128 * py : 128 * py + 128], 0.0)
            store_fine(fm_ref, 2 * yg + py, tile, m)

    for yg in range(9):
        fine_merge(yg)
    clear_outside(fm_ref, 1, 0, ty, tx, m, split=True)

    def fine_final(yg):
        last_ref[yg] = jnp.maximum(conv(fm_ref, w_ff, yg, 16), 0.0).astype(BF16)

    for yg in range(8):
        fine_final(yg)
    logits = jnp.dot(
        jnp.concatenate([last_ref[yg] for yg in range(8)], axis=1),
        w_head[...],
        preferred_element_type=F32,
    )
    out[0] = logits[:, :128]
    out[1] = logits[:, 128:]


def finish_kernel(logits, out, turn_ref):
    for k in range(16):
        turn_ref[k, pl.ds(0, 16, stride=2), :] = logits[0, pl.ds(k, 16, stride=16), :]
        turn_ref[k, pl.ds(1, 16, stride=2), :] = logits[1, pl.ds(k, 16, stride=16), :]
        turned = turn_ref[k].T
        for c in range(3):
            for pz in range(2):
                row = 32 * c + 16 * pz
                out[c, 2 * k + pz] = turned[row : row + 16]


def per_device(
    raw_bricks,
    stretch_reader,
    fine_open,
    fine_second,
    middle_open,
    middle_second,
    coarse_open,
    coarse_second,
    middle_merge,
    middle_final,
    fine_merge,
    fine_final,
    affinity_head,
):
    def flat(w):
        return w.reshape(27, w.shape[3], w.shape[4])

    weights = [
        flat(fine_second),
        flat(middle_open.transpose(0, 1, 2, 4, 3)),
        flat(middle_second),
        flat(coarse_open),
        flat(coarse_second),
        flat(middle_merge),
        flat(middle_final),
        flat(fine_merge),
        flat(fine_final),
    ]
    opening = fine_open.transpose(0, 1, 4, 2, 3).reshape(9, 3, 32)
    vmem = pl.BlockSpec(memory_space=pltpu.VMEM)
    smem = pl.BlockSpec(memory_space=pltpu.SMEM)
    hbm = pl.BlockSpec(memory_space=pl.ANY)
    dma = pltpu.SemaphoreType.DMA

    def half(*shape):
        return pltpu.VMEM(shape, BF16)

    def full(*shape):
        return pltpu.VMEM(shape, F32)

    logits = pl.pallas_call(
        whole_kernel,
        out_shape=jax.ShapeDtypeStruct((2, 256, 128), F32),
        in_specs=[smem] + [vmem] * 3 + [hbm] * 9,
        out_specs=vmem,
        scratch_shapes=[half(*w.shape) for w in weights]
        + [half(17, 768, 256)]
        + [half(size, 256) for size in (2048, 2048, 3072, 3072, 3072, 4096, 3072, 3072, 2048, 2048)]
        + [
            half(8, 4, 32, 128),
            half(8, 4, 32, 128),
            half(2, 2, 4, 32, 128),
            full(3, 296, 256),
            full(20, 40, 128),
            half(18, 17, 16, 256),
            half(12, 6, 16, 128),
            half(20, 18, 16, 128),
            half(12, 10, 16, 256),
            half(10, 9, 16, 384),
            full(4, 128, 128),
            half(12, 4, 16, 128),
            half(16, 12, 16, 128),
            half(12, 8, 16, 384),
            half(10, 7, 16, 384),
            full(8, 96, 128),
            half(8, 12, 16, 256),
            half(16, 12, 16, 384),
            half(14, 11, 16, 384),
            half(12, 20, 16, 256),
            half(20, 18, 16, 256),
            half(18, 17, 16, 256),
            full(9, 272, 256),
            half(8, 256, 256),
            full(3, 128, 128),
            dma((9,)),
            dma((8,)),
            dma((8,)),
            dma((3,)),
            dma((3,)),
        ]
        + [dma((8,))] * 8,
        name="whole",
        compiler_params=pltpu.CompilerParams(
            vmem_limit_bytes=58 * MIB, collective_id=0, has_side_effects=True
        ),
        cost_estimate=pl.CostEstimate(flops=10**10, bytes_accessed=10**7, transcendentals=0),
    )(stretch_reader, raw_bricks[0], affinity_head, opening, *weights)
    return pl.pallas_call(
        finish_kernel,
        out_shape=jax.ShapeDtypeStruct((3, DEPTH, TILE_Y, TILE_X), F32),
        in_specs=[vmem],
        out_specs=vmem,
        scratch_shapes=[full(16, 32, 128)],
        name="finish",
        compiler_params=pltpu.CompilerParams(vmem_limit_bytes=4 * MIB),
    )(logits)


def solution(mesh):
    placed = (P(("ty", "tx"), None, None, None),) + (P(),) * 12
    return jax.shard_map(
        per_device, mesh=mesh, in_specs=placed, out_specs=P(None, None, "ty", "tx"), check_vma=False
    )
```

```python
import jax
import jax.numpy as jnp
from jax import lax
from jax.experimental import pallas as pl
from jax.experimental.pallas import tpu as pltpu
from jax.sharding import PartitionSpec as P

TILE_Y = 16
TILE_X = 32
DEPTH = 32
BF16 = jnp.bfloat16
F32 = jnp.float32
MIB = 1 << 20


def iota(shape, dim):
    return lax.broadcasted_iota(jnp.int32, shape, dim)


def lane_block(shape, width):
    return lax.shift_right_logical(iota(shape, len(shape) - 1), width.bit_length() - 1)


def spread_blocks(w_ref, out_chans, out_dim=0):
    eye = (iota((out_chans, 128), 0) == iota((out_chans, 128), 1) % out_chans).astype(BF16)
    return [
        lax.dot_general(w_ref[t], eye, (((out_dim,), (0,)), ((), ())), preferred_element_type=F32)
        for t in range(27)
    ]


def tap(a, b, e):
    if 0 <= a <= 2 and 0 <= b <= 2 and 0 <= e <= 2:
        return 9 * a + 3 * b + e
    return None


def masked_sum(blocks, taps, width):
    shape = blocks[0].shape
    lanes = lane_block(shape, width)
    tile = jnp.zeros(shape, F32)
    for place, index in enumerate(taps):
        if index is not None:
            tile = jnp.where(lanes == place, blocks[index], tile)
    return tile


def build_fine(blocks, out_ref):
    for y in range(4):
        for j in range(2):
            for half in range(2):
                for px_in in range(2):
                    for slot in range(2):
                        z = (1 + slot) if half == 0 else (3, 0)[slot]
                        row = (y * 2 + j) * 256 + half * 128 + px_in * 64 + slot * 32
                        for py in range(2):
                            taps = [
                                tap(z - pz, y - py, 2 * j + px_in - px)
                                for px in range(2)
                                for pz in range(2)
                            ]
                            out_ref[row : row + 32, py * 128 : (py + 1) * 128] = masked_sum(
                                blocks, taps, 32
                            ).astype(BF16)


def build_middle(blocks, out_ref):
    for y in range(4):
        for j in range(2):
            for slot, dz in enumerate((1, 0, 2)):
                for px_in in range(2):
                    row = (y * 2 + j) * 384 + slot * 128 + px_in * 64
                    for py in range(2):
                        taps = [tap(dz, y - py, 2 * j + px_in - px) for px in range(2)]
                        out_ref[row : row + 64, py * 128 : (py + 1) * 128] = masked_sum(
                            blocks, taps, 64
                        ).astype(BF16)


def build_middle_open(blocks, out_ref):
    for y in range(4):
        for j in range(2):
            for px_in in range(2):
                for slot, dz in enumerate((1, 0, 2, 9)):
                    row = (y * 2 + j) * 256 + px_in * 128 + slot * 32
                    for py in range(2):
                        taps = [tap(dz, y - py, 2 * j + px_in - px) for px in range(2)]
                        out_ref[row : row + 32, py * 128 : (py + 1) * 128] = masked_sum(
                            blocks, taps, 64
                        ).astype(BF16)


def build_up(zcombined, out_ref, row0):
    shape = (64, 128)
    odd = lane_block(shape, 64) == 1
    for slot in range(4):
        for xc in range(2):
            rows = None
            if slot < 3:
                rows = []
                for dy in range(3):
                    t = zcombined[slot][dy]
                    if xc == 0:
                        rows.append(jnp.where(odd, t[0], t[0] + t[1]))
                    else:
                        rows.append(jnp.where(odd, t[1] + t[2], t[2]))
            for yc in range(2):
                row = row0 + (yc * 2 + xc) * 256 + slot * 64
                for py in range(2):
                    if rows is None:
                        tile = jnp.zeros(shape, F32)
                    elif (py, yc) == (0, 0):
                        tile = rows[0] + rows[1]
                    elif (py, yc) == (0, 1):
                        tile = rows[2]
                    elif (py, yc) == (1, 0):
                        tile = rows[0]
                    else:
                        tile = rows[1] + rows[2]
                    out_ref[row : row + 64, py * 128 : (py + 1) * 128] = tile.astype(BF16)


def build_open(w_ref, base_ref, out_ref):
    base_ref[...] = jnp.zeros_like(base_ref)
    eye = (iota((32, 128), 0) == iota((32, 128), 1) % 32).astype(BF16)
    rows = []
    for t in range(9):
        three = jnp.dot(w_ref[t], eye, preferred_element_type=F32)
        rows += [three[dx : dx + 1] for dx in range(3)]
    for dy in range(3):
        for z in range(6):
            for x in range(4):
                row = 40 + z // 3 * 128 + z % 3 * 40 + x
                for half in range(2):
                    taps = []
                    for px in range(2):
                        for p in range(2):
                            z_out = p if half == 0 else (2, -1)[p]
                            taps.append(tap(z - 1 - z_out, dy, x - px))
                    base_ref[dy, row : row + 1, 128 * half : 128 * half + 128] = masked_sum(
                        rows, taps, 32
                    )
    for xp in range(17):
        for dy in range(3):
            out_ref[xp, 256 * dy : 256 * dy + 256] = base_ref[
                dy, 40 - 2 * xp : 296 - 2 * xp
            ].astype(BF16)


def build_middle_merge(w_ref, out_ref):
    both = spread_blocks(w_ref, 64)
    build_middle([block[64:128] for block in both], out_ref)
    up = [block[:64] for block in both]
    grid = [[[up[9 * dz + 3 * dy + dx] for dx in range(3)] for dy in range(3)] for dz in (1, 0, 2)]
    build_up(grid, out_ref, 3072)


def build_fine_merge(w_ref, out_ref):
    both = spread_blocks(w_ref, 32)
    build_fine([block[64:96] for block in both], out_ref)
    up = [block[:64] for block in both]
    odd_z = lane_block((64, 128), 32) % 2 == 1

    def zmix(slot, dy, dx):
        w0, w1, w2 = (up[9 * a + 3 * dy + dx] for a in range(3))
        if slot == 0:
            return jnp.where(odd_z, w0 + w1, w1 + w2)
        if slot == 1:
            return jnp.where(odd_z, 0.0, w0)
        return jnp.where(odd_z, w2, 0.0)

    grid = [[[zmix(slot, dy, dx) for dx in range(3)] for dy in range(3)] for slot in range(3)]
    build_up(grid, out_ref, 2048)


def build_head(head_ref, out_ref):
    column = iota((256, 32), 0) % 128 // 32
    picked = jnp.zeros((256, 32), F32)
    for c in range(3):
        picked = jnp.where(column == c, head_ref[c : c + 1, :].astype(F32), picked)
    eye = (iota((256, 32), 0) % 32 == iota((256, 32), 1)).astype(BF16)
    full = lax.dot_general(
        eye, picked.astype(BF16), (((1,), (1,)), ((), ())), preferred_element_type=F32
    )
    row, col = iota((256, 256), 0), iota((256, 256), 1)
    fits = (row // 64 % 2 == col // 128) & (row // 32 % 2 == col // 16 % 2)
    fits = fits & (row // 128 == col % 16) & (col % 128 < 96)
    base = jnp.where(fits, full, 0.0)
    for yg in range(8):
        for px in range(2):
            part = base[:, 128 * px : 128 * px + 128]
            out_ref[256 * yg : 256 * yg + 256, 128 * px : 128 * px + 128] = pltpu.roll(
                part, 2 * yg, 1
            ).astype(BF16)


class Masks:
    def __init__(self):
        row, lane = iota((16, 128), 0), iota((16, 128), 1)

        def factor(where):
            return jnp.where(where, 1.0, 0.0).astype(F32)

        first, last = row > 0, row < 15
        odd = (lane & 32) != 0
        self.below, self.above = factor(first), factor(last)
        self.ends_below, self.ends_above = factor(odd & first), factor(~odd & last)
        self.low, self.high_below = factor(lane < 64), factor((lane >= 64) & first)
        self.px = [factor(lane < 64), factor(lane >= 64)]
        self.coarse_z = factor(row < 8)
        block = lane >> 5
        self.block = [factor(block == 0), factor((block == 1) & first), factor((block == 2) & last)]


def scaled(x, factor):
    return as_rows(as_blocks(x) * factor[None])


def row_below(x):
    return pltpu.roll(x, 1, 0)


def row_above(x):
    return pltpu.roll(x, x.shape[0] - 1, 0)


def as_rows(x):
    return x.reshape(x.shape[0] * 16, x.shape[2])


def as_blocks(x):
    return x.reshape(x.shape[0] // 16, 16, x.shape[1])


def up_window(src, yg, shift, groups):
    y, x = yg + shift, shift
    return [as_rows(src[y + yc, x + xc : x + xc + groups]) for yc in range(2) for xc in range(2)]


def window(src, yg, groups, up=None):
    pieces = [as_rows(src[2 * yg + y, j : j + groups]) for y in range(4) for j in range(2)]
    if up is not None:
        pieces += up_window(up, yg, 0, groups)
    return jnp.concatenate(pieces, axis=1)


def conv(src, w_ref, yg, groups):
    lhs = window(src, yg, groups)
    return jnp.dot(lhs, w_ref[...], preferred_element_type=F32)


def conv_lines(src, w_ref, counts, groups, body, up=None):
    first, rows = 0, groups * 16
    for count in counts:
        lines = range(first, first + count)
        lhs = jnp.concatenate([window(src, yg, groups, up) for yg in lines], axis=0)
        acc = jnp.dot(lhs, w_ref[...], preferred_element_type=F32)
        for i, yg in enumerate(lines):
            body(yg, acc[i * rows : (i + 1) * rows])
        first += count


def store_fine(ref, y, tile, m):
    ends = scaled(row_below(tile), m.ends_below) + scaled(row_above(tile), m.ends_above)
    ref[y, :, :, 0:128] = as_blocks(tile.astype(BF16))
    ref[y, :, :, 128:256] = as_blocks(ends.astype(BF16))


def store_middle(ref, y, tile, m):
    ref[y, :, :, 0:128] = as_blocks(tile.astype(BF16))
    ref[y, :, :, 128:256] = as_blocks(scaled(row_below(tile), m.below).astype(BF16))
    ref[y, :, :, 256:384] = as_blocks(scaled(row_above(tile), m.above).astype(BF16))


def store_single(ref, y, tile, m):
    below, above = row_below(tile), scaled(row_above(tile), m.above)
    near = [
        scaled(tile, m.low) + scaled(pltpu.roll(below, 64, 1), m.high_below),
        scaled(pltpu.roll(tile, 64, 1), m.low) + scaled(below, m.high_below),
    ]
    far = [above, pltpu.roll(above, 64, 1)]
    for px in range(2):
        a, b = as_blocks(near[px].astype(BF16)), as_blocks(far[px].astype(BF16))
        for xg in range(tile.shape[0] // 16):
            ref[y, 2 * xg + px, :, 0:128] = a[xg]
            ref[y, 2 * xg + px, :, 128:256] = b[xg]


def clear_outside(ref, lines, places, ty, tx, m, split=False):
    count = ref.shape[1]
    parts = ref.shape[3] // 128

    def halve(place, px):
        factor = jnp.concatenate([m.px[px]] * parts, axis=1).astype(BF16)
        ref[:, place] = ref[:, place] * factor[None]

    @pl.when(ty == 0)
    def _():
        ref[0:lines] = jnp.zeros((lines,) + ref.shape[1:], BF16)

    @pl.when(ty == 15)
    def _():
        ref[ref.shape[0] - lines :] = jnp.zeros((lines,) + ref.shape[1:], BF16)

    @pl.when(tx == 0)
    def _():
        if places:
            ref[:, 0:places] = jnp.zeros((ref.shape[0], places) + ref.shape[2:], BF16)
        if split:
            halve(places, 1)

    @pl.when(tx == 7)
    def _():
        if places:
            ref[:, count - places :] = jnp.zeros((ref.shape[0], places) + ref.shape[2:], BF16)
        if split:
            halve(count - 1 - places, 0)


def loop(count, body, unroll=1):
    def step(i, carry):
        body(i)
        return carry

    lax.fori_loop(0, count, step, 0, unroll=unroll)


AROUND = [(-1, 0), (1, 0), (-1, -1), (-1, 1), (1, -1), (1, 1), (0, -1), (0, 1)]
ALONG_TY, ALONG_TX = range(6), range(6, 8)


def span(step, core, width):
    if step == 0:
        return width, width, core
    if step > 0:
        return core, 0, width
    return width, core + width, width


def exchange(ref, widths, send_sems, recv_sems, ty, tx, directions=range(8)):
    copies = []
    for i in directions:
        dy, dx = AROUND[i]
        sy, ly, ny = span(dy, ref.shape[0] - 2 * widths[0], widths[0])
        sx, lx, nx = span(dx, ref.shape[1] - 2 * widths[1], widths[1])
        copy = pltpu.make_async_remote_copy(
            src_ref=ref.at[pl.ds(sy, ny), pl.ds(sx, nx)],
            dst_ref=ref.at[pl.ds(ly, ny), pl.ds(lx, nx)],
            send_sem=send_sems.at[i],
            recv_sem=recv_sems.at[i],
            device_id=((ty + dy + 16) % 16, (tx + dx + 8) % 8),
            device_id_type=pl.DeviceIdType.MESH,
        )
        sends, receives = neighbour(dy, dx, ty, tx), neighbour(-dy, -dx, ty, tx)
        pl.when(sends)(copy.start)
        copies.append((copy, sends, receives))
    return copies


def neighbour(dy, dx, ty, tx):
    there = [tx >= 0]
    if dy:
        there.append(ty < 15 if dy > 0 else ty > 0)
    if dx:
        there.append(tx < 7 if dx > 0 else tx > 0)
    return there[-1] if len(there) < 3 else there[1] & there[2]


def finish(copies):
    for copy, sends, receives in copies:
        pl.when(receives)(copy.wait_recv)
    for copy, sends, receives in copies:
        pl.when(sends)(copy.wait_send)


def whole_kernel(
    readers, raw, head, fo, fs, mo, ms, co, cs, mm, mf, fm, ff,
    out,
    r_fs, r_mo, r_ms, r_co, r_cs, r_mm, r_mf, r_fm, r_ff,
    w_fo, w_fs, w_mo, w_ms, w_co, w_cs, w_mm, w_mf, w_fm, w_ff, w_head,
    outgoing, arrived, held,
    base_ref, z_ref, a_ref,
    quads, skip, in_ref, b_ref, s_ref,
    coarse, middle, ci_ref, co_ref, s2_ref, u1_ref, mi_ref, mm_ref, u2_ref, fi_ref, fm_ref,
    part_ref, last_ref, bricks_ref,
    load_sems, row_send, row_recv, near_send, near_recv,
    quad_send, quad_recv, skip_send, skip_recv, coarse_send, coarse_recv, middle_send, middle_recv,
):
    ty, tx = lax.axis_index("ty"), lax.axis_index("tx")
    m = Masks()
    mesh_id = pl.DeviceIdType.MESH
    loads = [
        pltpu.make_async_copy(source, target, load_sems.at[i])
        for i, (source, target) in enumerate(
            zip((fs, mo, ms, co, cs, mm, mf, fm, ff), (r_fs, r_mo, r_ms, r_co, r_cs, r_mm, r_mf, r_fm, r_ff))
        )
    ]
    for load in loads:
        load.start()

    barrier = pltpu.get_barrier_semaphore()
    greeted = [(ty, (tx + d) % 8) for d in range(1, 8)]
    greeted += [((ty + dy + 16) % 16, (tx + dx + 8) % 8) for dy in (-1, 1) for dx in (-1, 0, 1)]
    for device in greeted:
        pl.semaphore_signal(barrier, inc=1, device_id=device, device_id_type=mesh_id)
    for slot in range(3):
        for z in range(32):
            bricks_ref[slot, pl.ds(z, 4, stride=32), :] = raw[
                slot, :, 128 * z : 128 * z + 128
            ].astype(F32)

    pl.semaphore_wait(barrier, len(greeted))

    reader = [readers[ty * 8 + c] for c in range(8)]
    for c in range(8):
        rank = 0
        for earlier in range(c):
            rank += (reader[earlier] == reader[c]).astype(jnp.int32)
        outgoing[c] = bricks_ref[jnp.minimum(rank, 2)].astype(BF16).reshape(4, 32, 128)
    copies = []
    for d in range(1, 8):
        peer = (tx + d) % 8
        copy = pltpu.make_async_remote_copy(
            src_ref=outgoing.at[peer],
            dst_ref=arrived.at[tx],
            send_sem=row_send.at[d],
            recv_sem=row_recv.at[d],
            device_id=(ty, peer),
            device_id_type=mesh_id,
        )
        copy.start()
        copies.append(copy)
    arrived[tx] = outgoing[tx]
    build_open(fo, base_ref, w_fo)
    loads[0].wait()
    build_fine(spread_blocks(r_fs, 32), w_fs)
    for copy in copies:
        copy.wait()
    own = readers[ty * 8 + tx] % 8
    held[1, 1] = arrived[own]
    copies = []
    for i, (dy, dx) in enumerate([(0, 1), (1, 0), (1, 1)]):
        copy = pltpu.make_async_remote_copy(
            src_ref=held.at[1, 1],
            dst_ref=held.at[1 - dy, 1 - dx],
            send_sem=near_send.at[i],
            recv_sem=near_recv.at[i],
            device_id=((ty + dy) % 16, (tx + dx) % 8),
            device_id_type=mesh_id,
        )
        copy.start()
        copies.append(copy)
    loads[1].wait()
    build_middle_open(spread_blocks(r_mo, 64, 1), w_mo)
    loads[2].wait()
    build_middle(spread_blocks(r_ms, 64), w_ms)
    loads[3].wait()
    build_middle(spread_blocks(r_co, 64), w_co)
    for copy in copies:
        copy.wait()

    z_ref[:, 0:8] = jnp.zeros((20, 8, 128), F32)
    z_ref[:, 32:40] = jnp.zeros((20, 8, 128), F32)
    lane = iota((32, 128), 1)
    lines = []
    for br in range(4):
        bricks = []
        for bc in range(4):
            brick = held[br // 2, bc // 2, br % 2 * 2 + bc % 2].astype(F32)
            ok = True
            if br == 0:
                ok = ty > 0
            if br == 3:
                ok = ty < 15
            if bc == 0:
                ok = (tx > 0) & ok
            if bc == 3:
                ok = (tx < 7) & ok
            if ok is not True:
                brick = jnp.where(ok, brick, 0.0)
            bricks.append(brick)
        for r in ((6, 7), range(8), range(8), (0, 1))[br]:
            y = 8 * br + r - 6
            line = jnp.where(lane < 36, pltpu.roll(bricks[3], (34 - 16 * r) % 128, 1), 0.0)
            line = jnp.where(lane < 34, pltpu.roll(bricks[2], (18 - 16 * r) % 128, 1), line)
            line = jnp.where(lane < 18, pltpu.roll(bricks[1], (2 - 16 * r) % 128, 1), line)
            line = jnp.where(lane < 2, pltpu.roll(bricks[0], (-14 - 16 * r) % 128, 1), line)
            z_ref[y, 4:36, :] = line
            parts = [z_ref[y, pl.ds(2 + z, 16, stride=2), :] for z in range(6)]
            for t in range(2):
                tile = parts[3 * t]
                for i in (1, 2):
                    tile = tile + pltpu.roll(parts[3 * t + i], 40 * i, 1)
                parts[t] = tile
            lines.append(jnp.concatenate(parts[:2], axis=1).astype(BF16))
    lhs = jnp.concatenate(
        [jnp.concatenate(lines[dy : dy + 18], axis=0) for dy in range(3)], axis=1
    )
    ends = m.ends_below + m.ends_above
    for xp in range(17):
        acc = jnp.maximum(jnp.dot(lhs, w_fo[xp], preferred_element_type=F32), 0.0)
        a_ref[:, xp, :, 0:128] = as_blocks(acc[:, :128].astype(BF16))
        a_ref[:, xp, :, 128:256] = as_blocks(scaled(acc[:, 128:], ends).astype(BF16))
    clear_outside(a_ref, 1, 0, ty, tx, m, split=True)
    quad_lane = lane_block((4, 16, 128), 32)

    def second(yg):
        acc = jnp.maximum(conv(a_ref, w_fs, yg, 16), 0.0)
        skip[2 + 2 * yg, 1:17] = as_blocks(acc[:, :128].astype(BF16))
        skip[3 + 2 * yg, 1:17] = as_blocks(acc[:, 128:].astype(BF16))
        top = jnp.maximum(acc[:, :128], acc[:, 128:])
        top = jnp.maximum(top, pltpu.roll(top, 64, 1))
        top = jnp.maximum(top, pltpu.roll(top, 32, 1)).reshape(4, 4, 16, 128)
        quad = top[:, 0]
        for q in range(1, 4):
            quad = jnp.where(quad_lane == q, top[:, q], quad)
        quads[2 + yg, 1:5] = quad.astype(BF16)

    for yg in (0, 1, 6, 7):
        second(yg)
    copies = exchange(quads, (2, 1), quad_send, quad_recv, ty, tx, ALONG_TY)
    for yg in range(2, 6):
        second(yg)
    copies += exchange(quads, (2, 1), quad_send, quad_recv, ty, tx, ALONG_TX)
    skip_copies = exchange(skip, (2, 1), skip_send, skip_recv, ty, tx)
    loads[4].wait()
    build_middle(spread_blocks(r_cs, 64), w_cs)
    loads[5].wait()
    build_middle_merge(r_mm, w_mm)
    loads[6].wait()
    build_middle(spread_blocks(r_mf, 64), w_mf)
    loads[7].wait()
    build_fine_merge(r_fm, w_fm)
    loads[8].wait()
    build_fine(spread_blocks(r_ff, 32), w_ff)
    build_head(head, w_head)
    finish(copies)

    clear_outside(quads, 2, 1, ty, tx, m)

    def spread(y):
        c = as_rows(quads[y]).astype(F32)
        below, above = row_below(c), row_above(c)
        for q in range(4):
            tile = scaled(pltpu.roll(c, (-32 * q) % 128, 1), m.block[0])
            tile = tile + scaled(pltpu.roll(below, (32 - 32 * q) % 128, 1), m.block[1])
            tile = tile + scaled(pltpu.roll(above, (64 - 32 * q) % 128, 1), m.block[2])
            blocks = as_blocks(tile.astype(BF16))
            lane = 128 * (q % 2)
            for quad in range(6):
                place = 2 * quad - 1 + q // 2
                if 0 <= place < 10:
                    in_ref[y, place, :, lane : lane + 128] = blocks[quad]

    loop(12, spread, 3)

    def middle_open(yg, acc):
        for py in range(2):
            tile = jnp.maximum(acc[:, 128 * py : 128 * py + 128], 0.0)
            store_middle(b_ref, 2 * yg + py, tile, m)

    conv_lines(in_ref, w_mo, (2, 3), 9, middle_open)
    clear_outside(b_ref, 1, 0, ty, tx, m, split=True)
    low = lane_block((4, 8, 128), 64) == 0

    def middle_second(yg, acc):
        acc = jnp.maximum(acc, 0.0)
        middle[4 + 2 * yg, 2:10] = as_blocks(acc[:, :128].astype(BF16))
        middle[5 + 2 * yg, 2:10] = as_blocks(acc[:, 128:].astype(BF16))
        top = jnp.maximum(acc[:, :128], acc[:, 128:])
        top = jnp.maximum(top, pltpu.roll(top, 64, 1))
        s_ref[yg] = jnp.maximum(top, row_above(top))
        some = s_ref[yg, pl.ds(0, 64, stride=2), :].reshape(4, 2, 8, 128)
        pair = jnp.where(low, some[:, 0], some[:, 1])
        coarse[4 + yg, 1:3] = pair.reshape(2, 16, 128).astype(BF16)

    conv_lines(b_ref, w_ms, (2, 2), 8, middle_second)
    copies = exchange(coarse, (4, 1), coarse_send, coarse_recv, ty, tx)
    middle_copies = exchange(middle, (4, 2), middle_send, middle_recv, ty, tx)

    finish(skip_copies)
    clear_outside(skip, 2, 1, ty, tx, m)

    def fine_in(y):
        x = as_rows(skip[y]).astype(F32)
        store_fine(fi_ref, y, x, m)

    loop(20, fine_in, 2)
    for yg in range(9):
        part_ref[yg] = jnp.dot(
            window(fi_ref, yg, 17), w_fm[0:2048], preferred_element_type=F32
        )
    finish(copies)

    clear_outside(coarse, 4, 1, ty, tx, m)

    def coarse_in(y):
        x = coarse[y].astype(F32).reshape(8, 8, 128)
        x = as_rows(jnp.concatenate([x, jnp.zeros_like(x)], axis=1))
        store_middle(ci_ref, y, x, m)

    loop(12, coarse_in)

    def coarse_open(yg, acc):
        for py in range(2):
            tile = jnp.maximum(acc[:, 128 * py : 128 * py + 128], 0.0)
            tile = scaled(tile, m.coarse_z)
            store_middle(co_ref, 2 * yg + py, tile, m)

    conv_lines(ci_ref, w_co, (2, 3), 7, coarse_open)
    clear_outside(co_ref, 3, 1, ty, tx, m, split=True)

    def coarse_second(yg, acc):
        for py in range(2):
            tile = jnp.maximum(acc[:, 128 * py : 128 * py + 128], 0.0)
            half = tile.reshape(6, 16, 128)[:, :8].reshape(48, 128)
            s2_ref[2 * yg + py, pl.ds(0, 48, stride=2), :] = half
            s2_ref[2 * yg + py, pl.ds(1, 48, stride=2), :] = half
            store_single(u1_ref, 2 * yg + py, s2_ref[2 * yg + py], m)

    conv_lines(co_ref, w_cs, (2, 2), 6, coarse_second)
    clear_outside(u1_ref, 2, 2, ty, tx, m)
    finish(middle_copies)
    clear_outside(middle, 4, 2, ty, tx, m)

    def middle_in(y):
        x = as_rows(middle[y]).astype(F32)
        store_middle(mi_ref, y, x, m)

    loop(16, middle_in)

    def middle_merge(yg, acc):
        for py in range(2):
            tile = jnp.maximum(acc[:, 128 * py : 128 * py + 128], 0.0)
            store_middle(mm_ref, 2 * yg + py, tile, m)

    conv_lines(mi_ref, w_mm, (1,) * 7, 11, middle_merge, u1_ref)
    clear_outside(mm_ref, 3, 1, ty, tx, m, split=True)

    def middle_final(yg, acc):
        for py in range(2):
            tile = jnp.maximum(acc[:, 128 * py : 128 * py + 128], 0.0)
            store_single(u2_ref, 2 * yg + py, tile, m)

    conv_lines(mm_ref, w_mf, (1,) * 6, 10, middle_final)
    clear_outside(u2_ref, 2, 2, ty, tx, m)


    def fine_merge(yg):
        acc = part_ref[yg] + jnp.dot(
            jnp.concatenate(up_window(u2_ref, yg, 1, 17), axis=1),
            w_fm[2048:3072],
            preferred_element_type=F32,
        )
        for py in range(2):
            tile = jnp.maximum(acc[:, 128 * py : 128 * py + 128], 0.0)
            store_fine(fm_ref, 2 * yg + py, tile, m)

    for yg in range(9):
        fine_merge(yg)
    clear_outside(fm_ref, 1, 0, ty, tx, m, split=True)

    def fine_final(yg):
        last_ref[yg] = jnp.maximum(conv(fm_ref, w_ff, yg, 16), 0.0).astype(BF16)

    for yg in range(8):
        fine_final(yg)
    logits = jnp.dot(
        jnp.concatenate([last_ref[yg] for yg in range(8)], axis=1),
        w_head[...],
        preferred_element_type=F32,
    )
    out[0] = logits[:, :128]
    out[1] = logits[:, 128:]


def finish_kernel(logits, out, turn_ref):
    for k in range(16):
        turn_ref[k, pl.ds(0, 16, stride=2), :] = logits[0, pl.ds(k, 16, stride=16), :]
        turn_ref[k, pl.ds(1, 16, stride=2), :] = logits[1, pl.ds(k, 16, stride=16), :]
        turned = turn_ref[k].T
        for c in range(3):
            for pz in range(2):
                row = 32 * c + 16 * pz
                out[c, 2 * k + pz] = turned[row : row + 16]


def per_device(
    raw_bricks,
    stretch_reader,
    fine_open,
    fine_second,
    middle_open,
    middle_second,
    coarse_open,
    coarse_second,
    middle_merge,
    middle_final,
    fine_merge,
    fine_final,
    affinity_head,
):
    def flat(w):
        return w.reshape(27, w.shape[3], w.shape[4])

    weights = [
        flat(fine_second),
        flat(middle_open.transpose(0, 1, 2, 4, 3)),
        flat(middle_second),
        flat(coarse_open),
        flat(coarse_second),
        flat(middle_merge),
        flat(middle_final),
        flat(fine_merge),
        flat(fine_final),
    ]
    opening = fine_open.transpose(0, 1, 4, 2, 3).reshape(9, 3, 32)
    vmem = pl.BlockSpec(memory_space=pltpu.VMEM)
    smem = pl.BlockSpec(memory_space=pltpu.SMEM)
    hbm = pl.BlockSpec(memory_space=pl.ANY)
    dma = pltpu.SemaphoreType.DMA

    def half(*shape):
        return pltpu.VMEM(shape, BF16)

    def full(*shape):
        return pltpu.VMEM(shape, F32)

    logits = pl.pallas_call(
        whole_kernel,
        out_shape=jax.ShapeDtypeStruct((2, 256, 128), F32),
        in_specs=[smem] + [vmem] * 3 + [hbm] * 9,
        out_specs=vmem,
        scratch_shapes=[half(*w.shape) for w in weights]
        + [half(17, 768, 256)]
        + [half(size, 256) for size in (2048, 2048, 3072, 3072, 3072, 4096, 3072, 3072, 2048, 2048)]
        + [
            half(8, 4, 32, 128),
            half(8, 4, 32, 128),
            half(2, 2, 4, 32, 128),
            full(3, 296, 256),
            full(20, 40, 128),
            half(18, 17, 16, 256),
            half(12, 6, 16, 128),
            half(20, 18, 16, 128),
            half(12, 10, 16, 256),
            half(10, 9, 16, 384),
            full(4, 128, 128),
            half(12, 4, 16, 128),
            half(16, 12, 16, 128),
            half(12, 8, 16, 384),
            half(10, 7, 16, 384),
            full(8, 96, 128),
            half(8, 12, 16, 256),
            half(16, 12, 16, 384),
            half(14, 11, 16, 384),
            half(12, 20, 16, 256),
            half(20, 18, 16, 256),
            half(18, 17, 16, 256),
            full(9, 272, 256),
            half(8, 256, 256),
            full(3, 128, 128),
            dma((9,)),
            dma((8,)),
            dma((8,)),
            dma((3,)),
            dma((3,)),
        ]
        + [dma((8,))] * 8,
        name="whole",
        compiler_params=pltpu.CompilerParams(
            vmem_limit_bytes=58 * MIB, collective_id=0, has_side_effects=True
        ),
        cost_estimate=pl.CostEstimate(flops=10**10, bytes_accessed=10**7, transcendentals=0),
    )(stretch_reader, raw_bricks[0], affinity_head, opening, *weights)
    return pl.pallas_call(
        finish_kernel,
        out_shape=jax.ShapeDtypeStruct((3, DEPTH, TILE_Y, TILE_X), F32),
        in_specs=[vmem],
        out_specs=vmem,
        scratch_shapes=[full(16, 32, 128)],
        name="finish",
        compiler_params=pltpu.CompilerParams(vmem_limit_bytes=4 * MIB),
    )(logits)


def solution(mesh):
    placed = (P(("ty", "tx"), None, None, None),) + (P(),) * 12
    return jax.shard_map(
        per_device, mesh=mesh, in_specs=placed, out_specs=P(None, None, "ty", "tx"), check_vma=False
    )
```

```python
import jax
import jax.numpy as jnp
from jax import lax
from jax.experimental import pallas as pl
from jax.experimental.pallas import tpu as pltpu
from jax.sharding import PartitionSpec as P

TILE_Y = 16
TILE_X = 32
DEPTH = 32
BF16 = jnp.bfloat16
F32 = jnp.float32
MIB = 1 << 20


def iota(shape, dim):
    return lax.broadcasted_iota(jnp.int32, shape, dim)


def lane_block(shape, width):
    return lax.shift_right_logical(iota(shape, len(shape) - 1), width.bit_length() - 1)


def spread_blocks(w_ref, out_chans, out_dim=0):
    eye = (iota((out_chans, 128), 0) == iota((out_chans, 128), 1) % out_chans).astype(BF16)
    return [
        lax.dot_general(w_ref[t], eye, (((out_dim,), (0,)), ((), ())), preferred_element_type=F32)
        for t in range(27)
    ]


def tap(a, b, e):
    if 0 <= a <= 2 and 0 <= b <= 2 and 0 <= e <= 2:
        return 9 * a + 3 * b + e
    return None


def masked_sum(blocks, taps, width):
    shape = blocks[0].shape
    lanes = lane_block(shape, width)
    tile = jnp.zeros(shape, F32)
    for place, index in enumerate(taps):
        if index is not None:
            tile = jnp.where(lanes == place, blocks[index], tile)
    return tile


def build_fine(blocks, out_ref):
    for y in range(4):
        for j in range(2):
            for half in range(2):
                for px_in in range(2):
                    for slot in range(2):
                        z = (1 + slot) if half == 0 else (3, 0)[slot]
                        row = (y * 2 + j) * 256 + half * 128 + px_in * 64 + slot * 32
                        for py in range(2):
                            taps = [
                                tap(z - pz, y - py, 2 * j + px_in - px)
                                for px in range(2)
                                for pz in range(2)
                            ]
                            out_ref[row : row + 32, py * 128 : (py + 1) * 128] = masked_sum(
                                blocks, taps, 32
                            ).astype(BF16)


def build_middle(blocks, out_ref):
    for y in range(4):
        for j in range(2):
            for slot, dz in enumerate((1, 0, 2)):
                for px_in in range(2):
                    row = (y * 2 + j) * 384 + slot * 128 + px_in * 64
                    for py in range(2):
                        taps = [tap(dz, y - py, 2 * j + px_in - px) for px in range(2)]
                        out_ref[row : row + 64, py * 128 : (py + 1) * 128] = masked_sum(
                            blocks, taps, 64
                        ).astype(BF16)


def build_middle_open(blocks, out_ref):
    for y in range(4):
        for j in range(2):
            for px_in in range(2):
                for slot, dz in enumerate((1, 0, 2, 9)):
                    row = (y * 2 + j) * 256 + px_in * 128 + slot * 32
                    for py in range(2):
                        taps = [tap(dz, y - py, 2 * j + px_in - px) for px in range(2)]
                        out_ref[row : row + 32, py * 128 : (py + 1) * 128] = masked_sum(
                            blocks, taps, 64
                        ).astype(BF16)


def build_up(zcombined, out_ref, row0):
    shape = (64, 128)
    odd = lane_block(shape, 64) == 1
    for slot in range(4):
        for xc in range(2):
            rows = None
            if slot < 3:
                rows = []
                for dy in range(3):
                    t = zcombined[slot][dy]
                    if xc == 0:
                        rows.append(jnp.where(odd, t[0], t[0] + t[1]))
                    else:
                        rows.append(jnp.where(odd, t[1] + t[2], t[2]))
            for yc in range(2):
                row = row0 + (yc * 2 + xc) * 256 + slot * 64
                for py in range(2):
                    if rows is None:
                        tile = jnp.zeros(shape, F32)
                    elif (py, yc) == (0, 0):
                        tile = rows[0] + rows[1]
                    elif (py, yc) == (0, 1):
                        tile = rows[2]
                    elif (py, yc) == (1, 0):
                        tile = rows[0]
                    else:
                        tile = rows[1] + rows[2]
                    out_ref[row : row + 64, py * 128 : (py + 1) * 128] = tile.astype(BF16)


def build_open(w_ref, base_ref, out_ref):
    base_ref[...] = jnp.zeros_like(base_ref)
    eye = (iota((32, 128), 0) == iota((32, 128), 1) % 32).astype(BF16)
    rows = []
    for t in range(9):
        three = jnp.dot(w_ref[t], eye, preferred_element_type=F32)
        rows += [three[dx : dx + 1] for dx in range(3)]
    for dy in range(3):
        for z in range(6):
            for x in range(4):
                row = 40 + z // 3 * 128 + z % 3 * 40 + x
                for half in range(2):
                    taps = []
                    for px in range(2):
                        for p in range(2):
                            z_out = p if half == 0 else (2, -1)[p]
                            taps.append(tap(z - 1 - z_out, dy, x - px))
                    base_ref[dy, row : row + 1, 128 * half : 128 * half + 128] = masked_sum(
                        rows, taps, 32
                    )
    for xp in range(17):
        for dy in range(3):
            out_ref[xp, 256 * dy : 256 * dy + 256] = base_ref[
                dy, 40 - 2 * xp : 296 - 2 * xp
            ].astype(BF16)


def build_middle_merge(w_ref, out_ref):
    both = spread_blocks(w_ref, 64)
    build_middle([block[64:128] for block in both], out_ref)
    up = [block[:64] for block in both]
    grid = [[[up[9 * dz + 3 * dy + dx] for dx in range(3)] for dy in range(3)] for dz in (1, 0, 2)]
    build_up(grid, out_ref, 3072)


def build_fine_merge(w_ref, out_ref):
    both = spread_blocks(w_ref, 32)
    build_fine([block[64:96] for block in both], out_ref)
    up = [block[:64] for block in both]
    odd_z = lane_block((64, 128), 32) % 2 == 1

    def zmix(slot, dy, dx):
        w0, w1, w2 = (up[9 * a + 3 * dy + dx] for a in range(3))
        if slot == 0:
            return jnp.where(odd_z, w0 + w1, w1 + w2)
        if slot == 1:
            return jnp.where(odd_z, 0.0, w0)
        return jnp.where(odd_z, w2, 0.0)

    grid = [[[zmix(slot, dy, dx) for dx in range(3)] for dy in range(3)] for slot in range(3)]
    build_up(grid, out_ref, 2048)


def build_head(head_ref, out_ref):
    column = iota((256, 32), 0) % 128 // 32
    picked = jnp.zeros((256, 32), F32)
    for c in range(3):
        picked = jnp.where(column == c, head_ref[c : c + 1, :].astype(F32), picked)
    eye = (iota((256, 32), 0) % 32 == iota((256, 32), 1)).astype(BF16)
    full = lax.dot_general(
        eye, picked.astype(BF16), (((1,), (1,)), ((), ())), preferred_element_type=F32
    )
    row, col = iota((256, 256), 0), iota((256, 256), 1)
    fits = (row // 64 % 2 == col // 128) & (row // 32 % 2 == col // 16 % 2)
    fits = fits & (row // 128 == col % 16) & (col % 128 < 96)
    base = jnp.where(fits, full, 0.0)
    for yg in range(8):
        for px in range(2):
            part = base[:, 128 * px : 128 * px + 128]
            out_ref[256 * yg : 256 * yg + 256, 128 * px : 128 * px + 128] = pltpu.roll(
                part, 2 * yg, 1
            ).astype(BF16)


class Masks:
    def __init__(self):
        row, lane = iota((16, 128), 0), iota((16, 128), 1)

        def factor(where):
            return jnp.where(where, 1.0, 0.0).astype(F32)

        first, last = row > 0, row < 15
        odd = (lane & 32) != 0
        self.below, self.above = factor(first), factor(last)
        self.ends_below, self.ends_above = factor(odd & first), factor(~odd & last)
        self.low, self.high_below = factor(lane < 64), factor((lane >= 64) & first)
        self.px = [factor(lane < 64), factor(lane >= 64)]
        self.coarse_z = factor(row < 8)
        block = lane >> 5
        self.block = [factor(block == 0), factor((block == 1) & first), factor((block == 2) & last)]


def scaled(x, factor):
    return as_rows(as_blocks(x) * factor[None])


def row_below(x):
    return pltpu.roll(x, 1, 0)


def row_above(x):
    return pltpu.roll(x, x.shape[0] - 1, 0)


def as_rows(x):
    return x.reshape(x.shape[0] * 16, x.shape[2])


def as_blocks(x):
    return x.reshape(x.shape[0] // 16, 16, x.shape[1])


def up_window(src, yg, shift, groups):
    y, x = yg + shift, shift
    return [as_rows(src[y + yc, x + xc : x + xc + groups]) for yc in range(2) for xc in range(2)]


def window(src, yg, groups, up=None):
    pieces = [as_rows(src[2 * yg + y, j : j + groups]) for y in range(4) for j in range(2)]
    if up is not None:
        pieces += up_window(up, yg, 0, groups)
    return jnp.concatenate(pieces, axis=1)


def conv(src, w_ref, yg, groups):
    lhs = window(src, yg, groups)
    return jnp.dot(lhs, w_ref[...], preferred_element_type=F32)


def conv_lines(src, w_ref, counts, groups, body, up=None):
    first, rows = 0, groups * 16
    for count in counts:
        lines = range(first, first + count)
        lhs = jnp.concatenate([window(src, yg, groups, up) for yg in lines], axis=0)
        acc = jnp.dot(lhs, w_ref[...], preferred_element_type=F32)
        for i, yg in enumerate(lines):
            body(yg, acc[i * rows : (i + 1) * rows])
        first += count


def store_fine(ref, y, tile, m):
    ends = scaled(row_below(tile), m.ends_below) + scaled(row_above(tile), m.ends_above)
    ref[y, :, :, 0:128] = as_blocks(tile.astype(BF16))
    ref[y, :, :, 128:256] = as_blocks(ends.astype(BF16))


def store_middle(ref, y, tile, m):
    ref[y, :, :, 0:128] = as_blocks(tile.astype(BF16))
    ref[y, :, :, 128:256] = as_blocks(scaled(row_below(tile), m.below).astype(BF16))
    ref[y, :, :, 256:384] = as_blocks(scaled(row_above(tile), m.above).astype(BF16))


def store_single(ref, y, tile, m):
    below, above = row_below(tile), scaled(row_above(tile), m.above)
    near = [
        scaled(tile, m.low) + scaled(pltpu.roll(below, 64, 1), m.high_below),
        scaled(pltpu.roll(tile, 64, 1), m.low) + scaled(below, m.high_below),
    ]
    far = [above, pltpu.roll(above, 64, 1)]
    for px in range(2):
        a, b = as_blocks(near[px].astype(BF16)), as_blocks(far[px].astype(BF16))
        for xg in range(tile.shape[0] // 16):
            ref[y, 2 * xg + px, :, 0:128] = a[xg]
            ref[y, 2 * xg + px, :, 128:256] = b[xg]


def clear_outside(ref, lines, places, ty, tx, m, split=False):
    count = ref.shape[1]
    parts = ref.shape[3] // 128

    def halve(place, px):
        factor = jnp.concatenate([m.px[px]] * parts, axis=1).astype(BF16)
        ref[:, place] = ref[:, place] * factor[None]

    @pl.when(ty == 0)
    def _():
        ref[0:lines] = jnp.zeros((lines,) + ref.shape[1:], BF16)

    @pl.when(ty == 15)
    def _():
        ref[ref.shape[0] - lines :] = jnp.zeros((lines,) + ref.shape[1:], BF16)

    @pl.when(tx == 0)
    def _():
        if places:
            ref[:, 0:places] = jnp.zeros((ref.shape[0], places) + ref.shape[2:], BF16)
        if split:
            halve(places, 1)

    @pl.when(tx == 7)
    def _():
        if places:
            ref[:, count - places :] = jnp.zeros((ref.shape[0], places) + ref.shape[2:], BF16)
        if split:
            halve(count - 1 - places, 0)


def loop(count, body, unroll=1):
    def step(i, carry):
        body(i)
        return carry

    lax.fori_loop(0, count, step, 0, unroll=unroll)


AROUND = [(-1, 0), (1, 0), (-1, -1), (-1, 1), (1, -1), (1, 1), (0, -1), (0, 1)]
ALONG_TY, ALONG_TX = range(6), range(6, 8)


def span(step, core, width):
    if step == 0:
        return width, width, core
    if step > 0:
        return core, 0, width
    return width, core + width, width


def exchange(ref, widths, send_sems, recv_sems, ty, tx, directions=range(8)):
    copies = []
    for i in directions:
        dy, dx = AROUND[i]
        sy, ly, ny = span(dy, ref.shape[0] - 2 * widths[0], widths[0])
        sx, lx, nx = span(dx, ref.shape[1] - 2 * widths[1], widths[1])
        copy = pltpu.make_async_remote_copy(
            src_ref=ref.at[pl.ds(sy, ny), pl.ds(sx, nx)],
            dst_ref=ref.at[pl.ds(ly, ny), pl.ds(lx, nx)],
            send_sem=send_sems.at[i],
            recv_sem=recv_sems.at[i],
            device_id=((ty + dy + 16) % 16, (tx + dx + 8) % 8),
            device_id_type=pl.DeviceIdType.MESH,
        )
        sends, receives = neighbour(dy, dx, ty, tx), neighbour(-dy, -dx, ty, tx)
        pl.when(sends)(copy.start)
        copies.append((copy, sends, receives))
    return copies


def neighbour(dy, dx, ty, tx):
    there = [tx >= 0]
    if dy:
        there.append(ty < 15 if dy > 0 else ty > 0)
    if dx:
        there.append(tx < 7 if dx > 0 else tx > 0)
    return there[-1] if len(there) < 3 else there[1] & there[2]


def finish(copies):
    for copy, sends, receives in copies:
        pl.when(receives)(copy.wait_recv)
    for copy, sends, receives in copies:
        pl.when(sends)(copy.wait_send)


def whole_kernel(
    readers, raw, head, fo, fs, mo, ms, co, cs, mm, mf, fm, ff,
    out,
    r_fs, r_mo, r_ms, r_co, r_cs, r_mm, r_mf, r_fm, r_ff,
    w_fo, w_fs, w_mo, w_ms, w_co, w_cs, w_mm, w_mf, w_fm, w_ff, w_head,
    outgoing, arrived, held,
    base_ref, z_ref, a_ref,
    quads, skip, in_ref, b_ref, s_ref,
    coarse, middle, ci_ref, co_ref, s2_ref, u1_ref, mi_ref, mm_ref, u2_ref, fi_ref, fm_ref,
    part_ref, last_ref, bricks_ref,
    load_sems, row_send, row_recv, near_send, near_recv,
    quad_send, quad_recv, skip_send, skip_recv, coarse_send, coarse_recv, middle_send, middle_recv,
):
    ty, tx = lax.axis_index("ty"), lax.axis_index("tx")
    m = Masks()
    mesh_id = pl.DeviceIdType.MESH
    loads = [
        pltpu.make_async_copy(source, target, load_sems.at[i])
        for i, (source, target) in enumerate(
            zip((fs, mo, ms, co, cs, mm, mf, fm, ff), (r_fs, r_mo, r_ms, r_co, r_cs, r_mm, r_mf, r_fm, r_ff))
        )
    ]
    for load in loads:
        load.start()

    barrier = pltpu.get_barrier_semaphore()
    greeted = [(ty, (tx + d) % 8) for d in range(1, 8)]
    greeted += [((ty + dy + 16) % 16, (tx + dx + 8) % 8) for dy in (-1, 1) for dx in (-1, 0, 1)]
    for device in greeted:
        pl.semaphore_signal(barrier, inc=1, device_id=device, device_id_type=mesh_id)
    for slot in range(3):
        for z in range(32):
            bricks_ref[slot, pl.ds(z, 4, stride=32), :] = raw[
                slot, :, 128 * z : 128 * z + 128
            ].astype(F32)

    pl.semaphore_wait(barrier, len(greeted))

    reader = [readers[ty * 8 + c] for c in range(8)]
    for c in range(8):
        rank = 0
        for earlier in range(c):
            rank += (reader[earlier] == reader[c]).astype(jnp.int32)
        outgoing[c] = bricks_ref[jnp.minimum(rank, 2)].astype(BF16).reshape(4, 32, 128)
    copies = []
    for d in range(1, 8):
        peer = (tx + d) % 8
        copy = pltpu.make_async_remote_copy(
            src_ref=outgoing.at[peer],
            dst_ref=arrived.at[tx],
            send_sem=row_send.at[d],
            recv_sem=row_recv.at[d],
            device_id=(ty, peer),
            device_id_type=mesh_id,
        )
        copy.start()
        copies.append(copy)
    arrived[tx] = outgoing[tx]
    build_open(fo, base_ref, w_fo)
    loads[0].wait()
    build_fine(spread_blocks(r_fs, 32), w_fs)
    for copy in copies:
        copy.wait()
    own = readers[ty * 8 + tx] % 8
    held[1, 1] = arrived[own]
    copies = []
    for i, (dy, dx) in enumerate([(0, 1), (1, 0), (1, 1)]):
        copy = pltpu.make_async_remote_copy(
            src_ref=held.at[1, 1],
            dst_ref=held.at[1 - dy, 1 - dx],
            send_sem=near_send.at[i],
            recv_sem=near_recv.at[i],
            device_id=((ty + dy) % 16, (tx + dx) % 8),
            device_id_type=mesh_id,
        )
        copy.start()
        copies.append(copy)
    loads[1].wait()
    build_middle_open(spread_blocks(r_mo, 64, 1), w_mo)
    loads[2].wait()
    build_middle(spread_blocks(r_ms, 64), w_ms)
    loads[3].wait()
    build_middle(spread_blocks(r_co, 64), w_co)
    for copy in copies:
        copy.wait()

    z_ref[:, 0:8] = jnp.zeros((20, 8, 128), F32)
    z_ref[:, 32:40] = jnp.zeros((20, 8, 128), F32)
    lane = iota((32, 128), 1)
    lines = []
    for br in range(4):
        bricks = []
        for bc in range(4):
            brick = held[br // 2, bc // 2, br % 2 * 2 + bc % 2].astype(F32)
            ok = True
            if br == 0:
                ok = ty > 0
            if br == 3:
                ok = ty < 15
            if bc == 0:
                ok = (tx > 0) & ok
            if bc == 3:
                ok = (tx < 7) & ok
            if ok is not True:
                brick = jnp.where(ok, brick, 0.0)
            bricks.append(brick)
        for r in ((6, 7), range(8), range(8), (0, 1))[br]:
            y = 8 * br + r - 6
            line = jnp.where(lane < 36, pltpu.roll(bricks[3], (34 - 16 * r) % 128, 1), 0.0)
            line = jnp.where(lane < 34, pltpu.roll(bricks[2], (18 - 16 * r) % 128, 1), line)
            line = jnp.where(lane < 18, pltpu.roll(bricks[1], (2 - 16 * r) % 128, 1), line)
            line = jnp.where(lane < 2, pltpu.roll(bricks[0], (-14 - 16 * r) % 128, 1), line)
            z_ref[y, 4:36, :] = line
            parts = [z_ref[y, pl.ds(2 + z, 16, stride=2), :] for z in range(6)]
            for t in range(2):
                tile = parts[3 * t]
                for i in (1, 2):
                    tile = tile + pltpu.roll(parts[3 * t + i], 40 * i, 1)
                parts[t] = tile
            lines.append(jnp.concatenate(parts[:2], axis=1).astype(BF16))
    lhs = jnp.concatenate(
        [jnp.concatenate(lines[dy : dy + 18], axis=0) for dy in range(3)], axis=1
    )
    ends = m.ends_below + m.ends_above
    for xp in range(17):
        acc = jnp.maximum(jnp.dot(lhs, w_fo[xp], preferred_element_type=F32), 0.0)
        a_ref[:, xp, :, 0:128] = as_blocks(acc[:, :128].astype(BF16))
        a_ref[:, xp, :, 128:256] = as_blocks(scaled(acc[:, 128:], ends).astype(BF16))
    clear_outside(a_ref, 1, 0, ty, tx, m, split=True)
    quad_lane = lane_block((4, 16, 128), 32)

    def second(yg):
        acc = jnp.maximum(conv(a_ref, w_fs, yg, 16), 0.0)
        skip[2 + 2 * yg, 1:17] = as_blocks(acc[:, :128].astype(BF16))
        skip[3 + 2 * yg, 1:17] = as_blocks(acc[:, 128:].astype(BF16))
        top = jnp.maximum(acc[:, :128], acc[:, 128:])
        top = jnp.maximum(top, pltpu.roll(top, 64, 1))
        top = jnp.maximum(top, pltpu.roll(top, 32, 1)).reshape(4, 4, 16, 128)
        quad = top[:, 0]
        for q in range(1, 4):
            quad = jnp.where(quad_lane == q, top[:, q], quad)
        quads[2 + yg, 1:5] = quad.astype(BF16)

    for yg in (0, 1, 6, 7):
        second(yg)
    copies = exchange(quads, (2, 1), quad_send, quad_recv, ty, tx, ALONG_TY)
    for yg in range(2, 6):
        second(yg)
    copies += exchange(quads, (2, 1), quad_send, quad_recv, ty, tx, ALONG_TX)
    skip_copies = exchange(skip, (2, 1), skip_send, skip_recv, ty, tx)
    loads[4].wait()
    build_middle(spread_blocks(r_cs, 64), w_cs)
    loads[5].wait()
    build_middle_merge(r_mm, w_mm)
    loads[6].wait()
    build_middle(spread_blocks(r_mf, 64), w_mf)
    loads[7].wait()
    build_fine_merge(r_fm, w_fm)
    loads[8].wait()
    build_fine(spread_blocks(r_ff, 32), w_ff)
    build_head(head, w_head)
    finish(copies)

    clear_outside(quads, 2, 1, ty, tx, m)

    def spread(y):
        c = as_rows(quads[y]).astype(F32)
        below, above = row_below(c), row_above(c)
        for q in range(4):
            tile = scaled(pltpu.roll(c, (-32 * q) % 128, 1), m.block[0])
            tile = tile + scaled(pltpu.roll(below, (32 - 32 * q) % 128, 1), m.block[1])
            tile = tile + scaled(pltpu.roll(above, (64 - 32 * q) % 128, 1), m.block[2])
            blocks = as_blocks(tile.astype(BF16))
            lane = 128 * (q % 2)
            for quad in range(6):
                place = 2 * quad - 1 + q // 2
                if 0 <= place < 10:
                    in_ref[y, place, :, lane : lane + 128] = blocks[quad]

    loop(12, spread, 3)

    def middle_open(yg, acc):
        for py in range(2):
            tile = jnp.maximum(acc[:, 128 * py : 128 * py + 128], 0.0)
            store_middle(b_ref, 2 * yg + py, tile, m)

    conv_lines(in_ref, w_mo, (2, 3), 9, middle_open)
    clear_outside(b_ref, 1, 0, ty, tx, m, split=True)
    low = lane_block((4, 8, 128), 64) == 0

    def middle_second(yg, acc):
        acc = jnp.maximum(acc, 0.0)
        middle[4 + 2 * yg, 2:10] = as_blocks(acc[:, :128].astype(BF16))
        middle[5 + 2 * yg, 2:10] = as_blocks(acc[:, 128:].astype(BF16))
        top = jnp.maximum(acc[:, :128], acc[:, 128:])
        top = jnp.maximum(top, pltpu.roll(top, 64, 1))
        s_ref[yg] = jnp.maximum(top, row_above(top))
        some = s_ref[yg, pl.ds(0, 64, stride=2), :].reshape(4, 2, 8, 128)
        pair = jnp.where(low, some[:, 0], some[:, 1])
        coarse[4 + yg, 1:3] = pair.reshape(2, 16, 128).astype(BF16)

    conv_lines(b_ref, w_ms, (2, 2), 8, middle_second)
    copies = exchange(coarse, (4, 1), coarse_send, coarse_recv, ty, tx)
    middle_copies = exchange(middle, (4, 2), middle_send, middle_recv, ty, tx)

    finish(skip_copies)
    clear_outside(skip, 2, 1, ty, tx, m)

    def fine_in(y):
        x = as_rows(skip[y]).astype(F32)
        store_fine(fi_ref, y, x, m)

    loop(20, fine_in, 4)
    for yg in range(9):
        part_ref[yg] = jnp.dot(
            window(fi_ref, yg, 17), w_fm[0:2048], preferred_element_type=F32
        )
    finish(copies)

    clear_outside(coarse, 4, 1, ty, tx, m)

    def coarse_in(y):
        x = coarse[y].astype(F32).reshape(8, 8, 128)
        x = as_rows(jnp.concatenate([x, jnp.zeros_like(x)], axis=1))
        store_middle(ci_ref, y, x, m)

    loop(12, coarse_in, 4)

    def coarse_open(yg, acc):
        for py in range(2):
            tile = jnp.maximum(acc[:, 128 * py : 128 * py + 128], 0.0)
            tile = scaled(tile, m.coarse_z)
            store_middle(co_ref, 2 * yg + py, tile, m)

    conv_lines(ci_ref, w_co, (2, 3), 7, coarse_open)
    clear_outside(co_ref, 3, 1, ty, tx, m, split=True)

    def coarse_second(yg, acc):
        for py in range(2):
            tile = jnp.maximum(acc[:, 128 * py : 128 * py + 128], 0.0)
            half = tile.reshape(6, 16, 128)[:, :8].reshape(48, 128)
            s2_ref[2 * yg + py, pl.ds(0, 48, stride=2), :] = half
            s2_ref[2 * yg + py, pl.ds(1, 48, stride=2), :] = half
            store_single(u1_ref, 2 * yg + py, s2_ref[2 * yg + py], m)

    conv_lines(co_ref, w_cs, (2, 2), 6, coarse_second)
    clear_outside(u1_ref, 2, 2, ty, tx, m)
    finish(middle_copies)
    clear_outside(middle, 4, 2, ty, tx, m)

    def middle_in(y):
        x = as_rows(middle[y]).astype(F32)
        store_middle(mi_ref, y, x, m)

    loop(16, middle_in, 4)

    def middle_merge(yg, acc):
        for py in range(2):
            tile = jnp.maximum(acc[:, 128 * py : 128 * py + 128], 0.0)
            store_middle(mm_ref, 2 * yg + py, tile, m)

    conv_lines(mi_ref, w_mm, (1,) * 7, 11, middle_merge, u1_ref)
    clear_outside(mm_ref, 3, 1, ty, tx, m, split=True)

    def middle_final(yg, acc):
        for py in range(2):
            tile = jnp.maximum(acc[:, 128 * py : 128 * py + 128], 0.0)
            store_single(u2_ref, 2 * yg + py, tile, m)

    conv_lines(mm_ref, w_mf, (1,) * 6, 10, middle_final)
    clear_outside(u2_ref, 2, 2, ty, tx, m)


    def fine_merge(yg):
        acc = part_ref[yg] + jnp.dot(
            jnp.concatenate(up_window(u2_ref, yg, 1, 17), axis=1),
            w_fm[2048:3072],
            preferred_element_type=F32,
        )
        for py in range(2):
            tile = jnp.maximum(acc[:, 128 * py : 128 * py + 128], 0.0)
            store_fine(fm_ref, 2 * yg + py, tile, m)

    for yg in range(9):
        fine_merge(yg)
    clear_outside(fm_ref, 1, 0, ty, tx, m, split=True)

    def fine_final(yg):
        last_ref[yg] = jnp.maximum(conv(fm_ref, w_ff, yg, 16), 0.0).astype(BF16)

    for yg in range(8):
        fine_final(yg)
    logits = jnp.dot(
        jnp.concatenate([last_ref[yg] for yg in range(8)], axis=1),
        w_head[...],
        preferred_element_type=F32,
    )
    out[0] = logits[:, :128]
    out[1] = logits[:, 128:]


def finish_kernel(logits, out, turn_ref):
    for k in range(16):
        turn_ref[k, pl.ds(0, 16, stride=2), :] = logits[0, pl.ds(k, 16, stride=16), :]
        turn_ref[k, pl.ds(1, 16, stride=2), :] = logits[1, pl.ds(k, 16, stride=16), :]
        turned = turn_ref[k].T
        for c in range(3):
            for pz in range(2):
                row = 32 * c + 16 * pz
                out[c, 2 * k + pz] = turned[row : row + 16]


def per_device(
    raw_bricks,
    stretch_reader,
    fine_open,
    fine_second,
    middle_open,
    middle_second,
    coarse_open,
    coarse_second,
    middle_merge,
    middle_final,
    fine_merge,
    fine_final,
    affinity_head,
):
    def flat(w):
        return w.reshape(27, w.shape[3], w.shape[4])

    weights = [
        flat(fine_second),
        flat(middle_open.transpose(0, 1, 2, 4, 3)),
        flat(middle_second),
        flat(coarse_open),
        flat(coarse_second),
        flat(middle_merge),
        flat(middle_final),
        flat(fine_merge),
        flat(fine_final),
    ]
    opening = fine_open.transpose(0, 1, 4, 2, 3).reshape(9, 3, 32)
    vmem = pl.BlockSpec(memory_space=pltpu.VMEM)
    smem = pl.BlockSpec(memory_space=pltpu.SMEM)
    hbm = pl.BlockSpec(memory_space=pl.ANY)
    dma = pltpu.SemaphoreType.DMA

    def half(*shape):
        return pltpu.VMEM(shape, BF16)

    def full(*shape):
        return pltpu.VMEM(shape, F32)

    logits = pl.pallas_call(
        whole_kernel,
        out_shape=jax.ShapeDtypeStruct((2, 256, 128), F32),
        in_specs=[smem] + [vmem] * 3 + [hbm] * 9,
        out_specs=vmem,
        scratch_shapes=[half(*w.shape) for w in weights]
        + [half(17, 768, 256)]
        + [half(size, 256) for size in (2048, 2048, 3072, 3072, 3072, 4096, 3072, 3072, 2048, 2048)]
        + [
            half(8, 4, 32, 128),
            half(8, 4, 32, 128),
            half(2, 2, 4, 32, 128),
            full(3, 296, 256),
            full(20, 40, 128),
            half(18, 17, 16, 256),
            half(12, 6, 16, 128),
            half(20, 18, 16, 128),
            half(12, 10, 16, 256),
            half(10, 9, 16, 384),
            full(4, 128, 128),
            half(12, 4, 16, 128),
            half(16, 12, 16, 128),
            half(12, 8, 16, 384),
            half(10, 7, 16, 384),
            full(8, 96, 128),
            half(8, 12, 16, 256),
            half(16, 12, 16, 384),
            half(14, 11, 16, 384),
            half(12, 20, 16, 256),
            half(20, 18, 16, 256),
            half(18, 17, 16, 256),
            full(9, 272, 256),
            half(8, 256, 256),
            full(3, 128, 128),
            dma((9,)),
            dma((8,)),
            dma((8,)),
            dma((3,)),
            dma((3,)),
        ]
        + [dma((8,))] * 8,
        name="whole",
        compiler_params=pltpu.CompilerParams(
            vmem_limit_bytes=58 * MIB, collective_id=0, has_side_effects=True
        ),
        cost_estimate=pl.CostEstimate(flops=10**10, bytes_accessed=10**7, transcendentals=0),
    )(stretch_reader, raw_bricks[0], affinity_head, opening, *weights)
    return pl.pallas_call(
        finish_kernel,
        out_shape=jax.ShapeDtypeStruct((3, DEPTH, TILE_Y, TILE_X), F32),
        in_specs=[vmem],
        out_specs=vmem,
        scratch_shapes=[full(16, 32, 128)],
        name="finish",
        compiler_params=pltpu.CompilerParams(vmem_limit_bytes=4 * MIB),
    )(logits)


def solution(mesh):
    placed = (P(("ty", "tx"), None, None, None),) + (P(),) * 12
    return jax.shard_map(
        per_device, mesh=mesh, in_specs=placed, out_specs=P(None, None, "ty", "tx"), check_vma=False
    )
```
